32 devices in a mesh: section: 2 (over z_hi), tensor: 2 (over z_lo), ctx: 8 (over y, x, core).
Axes of the slice: x: 2, y: 2, z: 4 (z_hi: 2, z_lo: 2; z = z_hi * 2 + z_lo), core: 2. Of those that a mesh axis runs over, the one named last changes fastest.
Arguments:
- inputs: bfloat16 [2, 1024, 2048], P(None, ('tensor', 'ctx')), may hold values from -6 to 6
- cotangent: bfloat16 [2, 1024, 2048], P(None, ('tensor', 'ctx')), may hold values from -6 to 6
- slot_order: int32 [2, 8], replicated, may hold values from 0 to 7, each once within a row
- query_weight: bfloat16 [2, 2048, 1280], P('section', 'ctx', 'tensor'), may hold values from -0.125 to 0.125
- key_value_matrix: bfloat16 [2, 2048, 640], P('section', ('tensor', 'ctx')), may hold values from -0.125 to 0.125
- out_weight: bfloat16 [2, 1280, 2048], P('section', 'tensor', 'ctx'), may hold values from -0.625 to 0.625
- gateup_weight: bfloat16 [2, 2048, 2, 5120], P('section', 'ctx', None, 'tensor'), may hold values from -0.125 to 0.125
- down_weight: bfloat16 [2, 5120, 2048], P('section', 'tensor', 'ctx'), may hold values from -0.078125 to 0.078125
- norm_gains: bfloat16 [2, 4224], P('section', ('tensor', 'ctx')), may hold values from 0.5 to 1.5
Outputs:
- section_out: bfloat16 [2, 2, 1024, 2048], P('section', None, ('tensor', 'ctx'))
- input_grads: bfloat16 [2, 2, 1024, 2048], P('section', None, ('tensor', 'ctx'))
- grad_query: float32 [2, 2048, 1280], P('section', 'ctx', 'tensor')
- grad_keyval: float32 [2, 2048, 640], P('section', ('tensor', 'ctx'))
- grad_out: float32 [2, 1280, 2048], P('section', 'tensor', 'ctx')
- grad_gateup: float32 [2, 2048, 2, 5120], P('section', 'ctx', None, 'tensor')
- grad_down: float32 [2, 5120, 2048], P('section', 'tensor', 'ctx')
- grad_gains: float32 [2, 4224], P('section', ('tensor', 'ctx'))
The draws below stay inside these ranges and needn't reach their ends.
Inputs may be any that keep to these rules, and one draw needn't show every extreme that they name: Each row is a permutation: index c of ctx holds tokens slot_order[b, c] * 128 to slot_order[b, c] * 128 + 127 of sequence b.
All inputs are finite; a program needn't handle non-finite values.
Results may differ from the reference program's by a relative error of at most 0.033.
Values may be sent and summed in bfloat16 or wider, within the bound.
A program may use at most 320 MiB of HBM per device.

```python
import jax
import jax.numpy as jnp
from jax import lax

MODEL_WIDTH = 2048
QUERY_HEADS = 20
KEY_VALUE_HEADS = 5
HEAD_SIZE = 64
FF = 5120
SPAN = 128
MICRO = 2
SEQ = 1024
HALF = 64
GAINS = 4224
N_SECTION = 2
N_TENSOR = 2
N_CTX = 8


def steps_of(key, dims, shards, low, largest):
    gain = 1.0
    for dim, parts in shards:
        draws = jax.random.uniform(jax.random.fold_in(jax.random.fold_in(key, 6), dim), (parts,), jnp.float32, low / len(shards), largest / len(shards))
        gain = gain * jnp.repeat(jnp.exp(draws), dims[dim] // parts).reshape((-1,) + (1,) * (len(dims) - 1 - dim))
    return gain


def normal_values(own_key, extent, spread, bound, cuts=(), kind=jnp.bfloat16):
    result = spread * jax.random.normal(own_key, extent, jnp.float32)
    if cuts:
        result = result * steps_of(own_key, extent, cuts, -0.22, 0.18)
    return jnp.clip(result, -bound, bound).astype(kind)


def setup_inputs(seed: int = 0) -> dict:
    keys = jax.random.split(jax.random.key(seed), 10)
    return {
        "inputs": normal_values(keys[0], (MICRO, SEQ, MODEL_WIDTH), 1.0, 6.0, ((1, 16),)),
        "cotangent": normal_values(keys[1], (MICRO, SEQ, MODEL_WIDTH), 1.0, 6.0, ((1, 16),)),
        "slot_order": jax.vmap(lambda own: jax.random.permutation(own, N_CTX))(jax.random.split(keys[2], MICRO)).reshape((MICRO, N_CTX)).astype(jnp.int32),
        "query_weight": normal_values(keys[3], (N_SECTION, MODEL_WIDTH, QUERY_HEADS * HEAD_SIZE), MODEL_WIDTH ** -0.5, 0.125, ((0, 2), (1, 8), (2, 2))),
        "key_value_matrix": normal_values(keys[4], (N_SECTION, MODEL_WIDTH, 2 * KEY_VALUE_HEADS * HEAD_SIZE), MODEL_WIDTH ** -0.5, 0.125, ((0, 2), (1, 16))),
        "out_weight": normal_values(keys[5], (N_SECTION, QUERY_HEADS * HEAD_SIZE, MODEL_WIDTH), (max(1, QUERY_HEADS * HEAD_SIZE * 64 // SEQ)) ** -0.5, 0.625, ((0, 2), (1, 2), (2, 8))),
        "gateup_weight": normal_values(keys[6], (N_SECTION, MODEL_WIDTH, 2, FF), MODEL_WIDTH ** -0.5, 0.125, ((0, 2), (1, 8), (3, 2))),
        "down_weight": normal_values(keys[7], (N_SECTION, FF, MODEL_WIDTH), FF ** -0.5, 0.078125, ((0, 2), (1, 2), (2, 8))),
        "norm_gains": jnp.clip(1.0 + 0.1 * jax.random.normal(keys[8], (N_SECTION, GAINS), jnp.float32), 0.5, 1.5).astype(jnp.bfloat16),
    }


EPSILON = 1e-06
ROPE_BASE = 10000.0
HIGHEST = lax.Precision.HIGHEST

@jax.custom_vjp
def low(v):
    return lax.optimization_barrier(v.astype(jnp.bfloat16)).astype(jnp.float32)

@jax.custom_vjp
def low_back(v):
    return v

def low_keep(v):
    return (low(v), None)

def low_pass(kept, grad):
    return (grad,)

def back_keep(v):
    return (v, None)

def back_low(kept, grad):
    return (low(grad),)
low.defvjp(low_keep, low_pass)
low_back.defvjp(back_keep, back_low)

def rope_tables(positions, head_width):
    half_width = head_width // 2
    frequency = ROPE_BASE ** (-(jnp.arange(half_width, dtype=jnp.float32) * 2.0) / head_width)
    angles = positions.astype(jnp.float32)[:, None] * frequency[None, :]
    return (jnp.cos(angles), jnp.sin(angles))

def rope_apply(values, cosine_rows, sine_rows):
    half_width = values.shape[-1] // 2
    first_half = values[..., :half_width]
    second_half = values[..., half_width:]
    cos_part = cosine_rows[:, None, :]
    sin_part = sine_rows[:, None, :]
    return jnp.concatenate([first_half * cos_part - second_half * sin_part, second_half * cos_part + first_half * sin_part], axis=-1)

def norm_rows(values, scaling):
    return values * lax.rsqrt(lax.optimization_barrier(jnp.mean(values * values, axis=-1, keepdims=True)) + EPSILON) * scaling

def attend(queries, key_rows, value_rows, positions):
    query_group_width = QUERY_HEADS // KEY_VALUE_HEADS
    key_heads = jnp.repeat(key_rows, query_group_width, axis=1)
    value_heads = jnp.repeat(value_rows, query_group_width, axis=1)
    sequence_length = queries.shape[0]
    rows_per_block = min(512, sequence_length)
    blocks_count = sequence_length // rows_per_block
    query_blocks = queries.reshape(blocks_count, rows_per_block, QUERY_HEADS, HEAD_SIZE)
    pos_blocks = positions.reshape(blocks_count, rows_per_block)

    def one_block(packed):
        query_block, pos_block = packed
        scores = jnp.einsum('qhd,khd->hqk', query_block, key_heads, precision=HIGHEST)
        scores = low_back(scores)
        allowed = positions[None, None, :] <= pos_block[None, :, None]
        scores = jnp.where(allowed, scores, -1e+30)
        highest = lax.optimization_barrier(jnp.max(scores, axis=-1, keepdims=True))
        exponent = jnp.exp(scores - highest)
        probability = low(exponent / lax.optimization_barrier(jnp.sum(exponent, axis=-1, keepdims=True)))
        return jnp.einsum('hqk,khd->qhd', probability, value_heads, precision=HIGHEST)
    mixture = lax.map(jax.checkpoint(one_block), (query_blocks, pos_blocks))
    return mixture.reshape(sequence_length, QUERY_HEADS, HEAD_SIZE)

def layer_apply(params, residual, positions):
    query_weight, key_value_matrix, out_weight, gateup_weight, down_weight, gain_all = params
    attn_gain = gain_all[:MODEL_WIDTH]
    ffn_gain = gain_all[MODEL_WIDTH:2 * MODEL_WIDTH]
    query_gain = gain_all[2 * MODEL_WIDTH:2 * MODEL_WIDTH + HEAD_SIZE]
    key_gain = gain_all[2 * MODEL_WIDTH + HEAD_SIZE:]
    sequence_length = residual.shape[0]
    normed = low(norm_rows(residual, attn_gain))
    query_raw = low_back(jnp.dot(normed, query_weight, precision=HIGHEST)).reshape(sequence_length, QUERY_HEADS, HEAD_SIZE)
    key_value_projected = low_back(jnp.dot(normed, key_value_matrix, precision=HIGHEST))
    unrotated_key = key_value_projected[:, :KEY_VALUE_HEADS * HEAD_SIZE].reshape(sequence_length, KEY_VALUE_HEADS, HEAD_SIZE)
    projected_value = key_value_projected[:, KEY_VALUE_HEADS * HEAD_SIZE:].reshape(sequence_length, KEY_VALUE_HEADS, HEAD_SIZE)
    cosine_rows, sine_rows = rope_tables(positions, HEAD_SIZE)
    queries = low(rope_apply(norm_rows(query_raw, query_gain), cosine_rows, sine_rows) * HEAD_SIZE ** (-0.5))
    key_rows = low(rope_apply(norm_rows(unrotated_key, key_gain), cosine_rows, sine_rows))
    value_rows = low(projected_value)
    mixture = attend(queries, key_rows, value_rows, positions)
    mixture = low(low_back(mixture)).reshape(sequence_length, QUERY_HEADS * HEAD_SIZE)
    residual = residual + low_back(jnp.dot(mixture, out_weight, precision=HIGHEST))
    normed = low(norm_rows(residual, ffn_gain))
    gateup = low_back(jnp.dot(normed, gateup_weight.reshape(MODEL_WIDTH, 2 * FF), precision=HIGHEST))
    hidden = low(jax.nn.silu(gateup[:, :FF]) * gateup[:, FF:])
    return residual + low_back(jnp.dot(hidden, down_weight, precision=HIGHEST))

def reference(inputs, cotangent, slot_order, query_weight, key_value_matrix, out_weight, gateup_weight, down_weight, norm_gains):
    params = tuple((weight_part.astype(jnp.float32) for weight_part in (query_weight, key_value_matrix, out_weight, gateup_weight, down_weight, norm_gains)))
    within = (jnp.arange(N_TENSOR)[:, None, None] * HALF + jnp.arange(HALF)[None, None, :]).astype(jnp.int32)
    positions = (slot_order[:, None, :, None] * SPAN + within[None]).reshape(MICRO, SEQ).astype(jnp.int32)
    probes = jnp.zeros((N_SECTION, MICRO, SEQ, MODEL_WIDTH), jnp.float32)

    def forward(params, probes):
        results = [[None] * MICRO for section_no in range(N_SECTION)]
        for batch_no in range(MICRO):
            residual = inputs[batch_no].astype(jnp.float32)
            for section_no in range(N_SECTION):
                if section_no > 0:
                    residual = low(residual)
                residual = low_back(residual + probes[section_no, batch_no])
                residual = layer_apply(tuple((weight_part[section_no] for weight_part in params)), residual, positions[batch_no])
                results[section_no][batch_no] = residual
        stacked = jnp.stack([jnp.stack(row_list) for row_list in results])
        return (stacked[N_SECTION - 1], stacked)
    last_out, pullback, stacked = jax.vjp(forward, params, probes, has_aux=True)
    weight_grads, probe_grads = pullback(cotangent.astype(jnp.float32))
    return (stacked.astype(jnp.bfloat16), probe_grads.astype(jnp.bfloat16), weight_grads[0], weight_grads[1], weight_grads[2], weight_grads[3], weight_grads[4], weight_grads[5])
```

```python
import jax
import jax.numpy as jnp
from jax import lax
from jax.experimental import pallas as pl
from jax.experimental.pallas import tpu as pltpu
from jax.sharding import PartitionSpec as P

MODEL_WIDTH = 2048
QUERY_HEADS = 20
KEY_VALUE_HEADS = 5
HEAD_SIZE = 64


EPSILON = 1e-06
ROPE_BASE = 10000.0
START_PEAK = -1e30


def from_behind(x, axis, by):
    devices = lax.axis_size(axis)
    pairs = [(i, i + by) for i in range(devices) if 0 <= i + by < devices]
    return lax.ppermute(x, axis, pairs)


def rope_tables(positions, head_width):
    half_width = head_width // 2
    frequency = ROPE_BASE ** (-(jnp.arange(half_width, dtype=jnp.float32) * 2.0) / head_width)
    angles = positions.astype(jnp.float32)[:, None] * frequency[None, :]
    return (jnp.cos(angles), jnp.sin(angles))


def rope_apply(values, cosine_rows, sine_rows):
    half_width = values.shape[-1] // 2
    first_half = values[..., :half_width]
    second_half = values[..., half_width:]
    cos_part = cosine_rows[:, None, :]
    sin_part = sine_rows[:, None, :]
    return jnp.concatenate(
        [
            first_half * cos_part - second_half * sin_part,
            second_half * cos_part + first_half * sin_part,
        ],
        axis=-1,
    )


def rope_back(incoming, cosine_rows, sine_rows):
    half_width = incoming.shape[-1] // 2
    first_half = incoming[..., :half_width]
    second_half = incoming[..., half_width:]
    cos_part = cosine_rows[:, None, :]
    sin_part = sine_rows[:, None, :]
    return jnp.concatenate(
        [
            first_half * cos_part + second_half * sin_part,
            second_half * cos_part - first_half * sin_part,
        ],
        axis=-1,
    )


def norm_parts(values, scaling):
    inverse = lax.rsqrt(jnp.mean(values * values, axis=-1, keepdims=True) + EPSILON)
    unit_rows = values * inverse
    return (unit_rows * scaling, unit_rows, inverse)


def norm_back(incoming, unit_rows, inverse, scaling):
    scaled = incoming * scaling
    inner = jnp.mean(scaled * unit_rows, axis=-1, keepdims=True)
    gain_grad = jnp.sum((incoming * unit_rows).reshape(-1, unit_rows.shape[-1]), axis=0)
    return (inverse * (scaled - unit_rows * inner), gain_grad)


def row_product(pieces_list, left_index, right_index):
    left_rows = jnp.concatenate([piece[left_index] for piece in pieces_list], axis=0)
    right_rows = jnp.concatenate([piece[right_index] for piece in pieces_list], axis=0)
    return lax.dot_general(
        left_rows, right_rows, (((0,), (0,)), ((), ())), preferred_element_type=jnp.float32
    )


def grads_from(pieces_list):
    grad_down = row_product(pieces_list, 0, 1)
    grad_gateup = row_product(pieces_list, 2, 3)
    grad_outw = row_product(pieces_list, 4, 5)
    grad_query = row_product(pieces_list, 6, 7)
    grad_keyval = row_product(pieces_list, 8, 9)
    grad_gain = pieces_list[0][10]
    for piece in pieces_list[1:]:
        grad_gain = grad_gain + piece[10]
    return (grad_query, grad_outw, grad_gateup, grad_down, grad_keyval, grad_gain)


def per_device(
    inputs,
    cotangent,
    slot_order,
    query_weight,
    key_value_matrix,
    out_weight,
    gateup_weight,
    down_weight,
    norm_gains,
):
    sections = lax.axis_size("section")
    tensors = lax.axis_size("tensor")
    contexts = lax.axis_size("ctx")
    section_id = lax.axis_index("section")
    tensor_id = lax.axis_index("tensor")
    context_id = lax.axis_index("ctx")
    batches = inputs.shape[0]
    rows_halved = inputs.shape[1]
    local_rows = rows_halved * tensors
    seq_rows = local_rows * contexts
    heads_here = query_weight.shape[2] // HEAD_SIZE
    units_here = down_weight.shape[1]
    key_columns = KEY_VALUE_HEADS * HEAD_SIZE
    rows_per_block = min(512, seq_rows)
    number_of_blocks = seq_rows // rows_per_block
    scale_query = HEAD_SIZE ** (-0.5)
    query_group_width = QUERY_HEADS // KEY_VALUE_HEADS
    head_numbers = tensor_id * heads_here + jnp.arange(heads_here)
    head_picker = head_numbers[:, None] // query_group_width == jnp.arange(KEY_VALUE_HEADS)[None, :]
    select_low = head_picker.astype(jnp.bfloat16)
    select_wide = head_picker.astype(jnp.float32)
    row_half = jnp.arange(rows_halved)
    row_local = jnp.arange(local_rows)
    within_seq = jnp.arange(tensors)[:, None, None] * rows_halved + row_half[None, None, :]

    def gather_rows(values):
        return lax.all_gather(values, "tensor", axis=0, tiled=True)

    def scatter_rows(values):
        return lax.psum_scatter(
            values.astype(jnp.bfloat16), "tensor", scatter_dimension=0, tiled=True
        ).astype(jnp.float32)

    def expand(block_part):
        return jnp.einsum(
            "khd,gh->kgd", block_part, select_low, preferred_element_type=jnp.float32
        ).astype(jnp.bfloat16)

    def block_scores(query_low, block_kv, pos_block, query_pos):
        keys_here = expand(block_kv[:, 0])
        scores = jnp.einsum(
            "qgd,kgd->gqk", query_low, keys_here, preferred_element_type=jnp.float32
        )
        allowed = pos_block[None, :] <= query_pos[:, None]
        return (jnp.where(allowed[None], scores, -jnp.inf), keys_here)

    def split_blocks(key_value_gathered, key_pos):
        return (
            key_value_gathered.reshape(
                number_of_blocks, rows_per_block, 2, KEY_VALUE_HEADS, HEAD_SIZE
            ),
            key_pos.reshape(number_of_blocks, rows_per_block),
        )

    def layer_backward(upstream, kept_state, weights):
        (
            attn_unit,
            attn_inv,
            normed_own,
            normed_all,
            query_unit,
            query_inv,
            query_low,
            key_unit,
            key_inv,
            key_value_gathered,
            log_mass,
            mixture,
            mixture_low,
            ffn_unit,
            ffn_inv,
            second_all,
            gateup,
            hidden_low,
            query_cos,
            query_sin,
            own_cos,
            own_sin,
            query_pos,
            key_pos,
        ) = kept_state
        query_full, out_full, gateup_full, down_full, keyval_full, gains_full = weights
        attn_gain = gains_full[:MODEL_WIDTH]
        ffn_gain = gains_full[MODEL_WIDTH : 2 * MODEL_WIDTH]
        query_gain = gains_full[2 * MODEL_WIDTH : 2 * MODEL_WIDTH + HEAD_SIZE]
        key_gain = gains_full[2 * MODEL_WIDTH + HEAD_SIZE :]
        down_all = gather_rows(upstream.astype(jnp.bfloat16))
        hidden_grad = jnp.dot(down_all, down_full.T, preferred_element_type=jnp.float32)
        gate_values = gateup[:, :units_here]
        up_values = gateup[:, units_here:]
        sigmoid_gate = jax.nn.sigmoid(gate_values)
        gate_grad = (
            hidden_grad * up_values * (sigmoid_gate * (1.0 + gate_values * (1.0 - sigmoid_gate)))
        )
        up_grad = hidden_grad * jax.nn.silu(gate_values)
        gateup_low = jnp.concatenate([gate_grad, up_grad], axis=1).astype(jnp.bfloat16)
        normed_grad = scatter_rows(
            jnp.dot(gateup_low, gateup_full.T, preferred_element_type=jnp.float32)
        )
        residual_part, ffn_gain_grad = norm_back(normed_grad, ffn_unit, ffn_inv, ffn_gain)
        middle = upstream + residual_part
        middle_all = gather_rows(middle.astype(jnp.bfloat16))
        mixture_grad = jnp.dot(middle_all, out_full.T, preferred_element_type=jnp.float32)
        mixture_grad_low = mixture_grad.astype(jnp.bfloat16).reshape(
            local_rows, heads_here, HEAD_SIZE
        )
        offsets = jnp.sum(mixture_grad_low.astype(jnp.float32) * mixture, axis=-1).T
        blocks, pos_blocks = split_blocks(key_value_gathered, key_pos)

        def grad_step(query_grad, packed):
            scores, keys_here = block_scores(query_low, packed[0], packed[1], query_pos)
            weights_full = jnp.exp(scores - log_mass[..., None])
            weights_low = weights_full.astype(jnp.bfloat16)
            values_here = expand(packed[0][:, 1])
            weight_grad = jnp.einsum(
                "qgd,kgd->gqk", mixture_grad_low, values_here, preferred_element_type=jnp.float32
            )
            score_low = (weights_full * (weight_grad - offsets[..., None])).astype(jnp.bfloat16)
            query_grad = query_grad + jnp.einsum(
                "gqk,kgd->qgd", score_low, keys_here, preferred_element_type=jnp.float32
            )
            key_grad = jnp.einsum(
                "gqk,qgd->kgd", score_low, query_low, preferred_element_type=jnp.float32
            )
            value_grad = jnp.einsum(
                "gqk,qgd->kgd", weights_low, mixture_grad_low, preferred_element_type=jnp.float32
            )
            pair_rows = jnp.stack(
                [
                    jnp.einsum("kgd,gh->khd", key_grad, select_wide),
                    jnp.einsum("kgd,gh->khd", value_grad, select_wide),
                ],
                axis=1,
            )
            return (query_grad, pair_rows.reshape(rows_per_block, 2 * key_columns))

        query_grad, pair_blocks = lax.scan(
            grad_step,
            jnp.zeros((local_rows, heads_here, HEAD_SIZE), jnp.float32),
            (blocks, pos_blocks),
        )
        key_value_gradient = lax.psum_scatter(
            pair_blocks.reshape(seq_rows, 2 * key_columns),
            ("tensor", "ctx"),
            scatter_dimension=0,
            tiled=True,
        )
        rotated_key_gradient = key_value_gradient[:, :key_columns].reshape(
            rows_halved, KEY_VALUE_HEADS, HEAD_SIZE
        )
        key_raw_grad, key_gain_grad = norm_back(
            rope_back(rotated_key_gradient, own_cos, own_sin), key_unit, key_inv, key_gain
        )
        keyval_low = jnp.concatenate(
            [key_raw_grad.reshape(rows_halved, key_columns), key_value_gradient[:, key_columns:]],
            axis=1,
        ).astype(jnp.bfloat16)
        own_grad = jnp.dot(keyval_low, keyval_full.T, preferred_element_type=jnp.float32)
        query_raw_grad, query_gain_grad = norm_back(
            rope_back(query_grad * scale_query, query_cos, query_sin),
            query_unit,
            query_inv,
            query_gain,
        )
        query_grad_low = query_raw_grad.reshape(local_rows, heads_here * HEAD_SIZE).astype(
            jnp.bfloat16
        )
        normed_grad = (
            scatter_rows(jnp.dot(query_grad_low, query_full.T, preferred_element_type=jnp.float32))
            + own_grad
        )
        residual_part, attn_gain_grad = norm_back(normed_grad, attn_unit, attn_inv, attn_gain)
        gain_grad = jnp.concatenate([attn_gain_grad, ffn_gain_grad, query_gain_grad, key_gain_grad])
        pieces = (
            hidden_low,
            down_all,
            second_all,
            gateup_low,
            mixture_low,
            middle_all,
            normed_all,
            query_grad_low,
            normed_own,
            keyval_low,
            gain_grad,
        )
        return (middle + residual_part, pieces)

    step_count = batches + sections - 1
    query_full = lax.all_gather(query_weight[0], "ctx", axis=0, tiled=True)
    out_full = lax.all_gather(out_weight[0], "ctx", axis=1, tiled=True)
    gateup_full = lax.all_gather(gateup_weight[0], "ctx", axis=0, tiled=True)
    down_full = lax.all_gather(down_weight[0], "ctx", axis=1, tiled=True)
    keyval_full = lax.all_gather(key_value_matrix[0], ("tensor", "ctx"), axis=0, tiled=True)
    gains_full = lax.all_gather(norm_gains[0], ("tensor", "ctx"), axis=0, tiled=True)
    weights_now = (
        query_full,
        out_full,
        gateup_full.reshape(MODEL_WIDTH, 2 * units_here),
        down_full,
        keyval_full,
        gains_full.astype(jnp.float32),
    )
    received = jnp.zeros_like(inputs[0])
    produced = []
    kept_all = []
    for step_index in range(step_count):
        batch_index = jnp.clip(step_index - section_id, 0, batches - 1)
        first_in = inputs[min(step_index, batches - 1)]
        residual = jnp.where(section_id == 0, first_in, received).astype(jnp.float32)
        layer_residual = residual
        (
            layer_query_full,
            layer_out_full,
            layer_gateup_full,
            layer_down_full,
            layer_keyval_full,
            layer_gains_full,
        ) = weights_now
        layer_attn_gain = layer_gains_full[:MODEL_WIDTH]
        layer_ffn_gain = layer_gains_full[MODEL_WIDTH : 2 * MODEL_WIDTH]
        layer_query_gain = layer_gains_full[2 * MODEL_WIDTH : 2 * MODEL_WIDTH + HEAD_SIZE]
        layer_key_gain = layer_gains_full[2 * MODEL_WIDTH + HEAD_SIZE :]
        slot_row = jnp.sum(
            jnp.where(jnp.arange(batches)[:, None] == batch_index, slot_order, 0), axis=0
        )
        own_slot = jnp.sum(jnp.where(jnp.arange(contexts) == context_id, slot_row, 0))
        positions_query_pos = own_slot * local_rows + row_local
        positions_key_pos = (slot_row[None, :, None] * local_rows + within_seq).reshape(seq_rows)
        own_pos = own_slot * local_rows + tensor_id * rows_halved + row_half
        layer_query_cos, layer_query_sin = rope_tables(positions_query_pos, HEAD_SIZE)
        layer_own_cos, layer_own_sin = rope_tables(own_pos, HEAD_SIZE)
        normed, layer_attn_unit, layer_attn_inv = norm_parts(layer_residual, layer_attn_gain)
        layer_normed_own = normed.astype(jnp.bfloat16)
        layer_normed_all = gather_rows(layer_normed_own)
        query_raw = jnp.dot(
            layer_normed_all, layer_query_full, preferred_element_type=jnp.float32
        ).reshape(local_rows, heads_here, HEAD_SIZE)
        query_hat, layer_query_unit, layer_query_inv = norm_parts(query_raw, layer_query_gain)
        layer_query_low = (
            rope_apply(query_hat, layer_query_cos, layer_query_sin) * scale_query
        ).astype(jnp.bfloat16)
        key_value_projected = jnp.dot(
            layer_normed_own, layer_keyval_full, preferred_element_type=jnp.float32
        )
        key_hat, layer_key_unit, layer_key_inv = norm_parts(
            key_value_projected[:, :key_columns].reshape(rows_halved, KEY_VALUE_HEADS, HEAD_SIZE),
            layer_key_gain,
        )
        key_low = (
            rope_apply(key_hat, layer_own_cos, layer_own_sin)
            .astype(jnp.bfloat16)
            .reshape(rows_halved, key_columns)
        )
        keyval_own = jnp.concatenate(
            [key_low, key_value_projected[:, key_columns:].astype(jnp.bfloat16)], axis=1
        )
        layer_key_value_gathered = lax.all_gather(keyval_own, ("tensor", "ctx"), axis=0, tiled=True)
        attend_query_low = layer_query_low
        attend_query_pos = positions_query_pos
        attend_blocks, attend_pos_blocks = split_blocks(layer_key_value_gathered, positions_key_pos)

        def peak_step(carry, packed):
            old_peak, mass_sum = carry
            scores, unused = block_scores(attend_query_low, packed[0], packed[1], attend_query_pos)
            new_peak = jnp.maximum(old_peak, jnp.max(scores, axis=-1))
            mass_sum = mass_sum * jnp.exp(old_peak - new_peak) + jnp.sum(
                jnp.exp(scores - new_peak[..., None]), axis=-1
            )
            return ((new_peak, mass_sum), None)

        initial = (
            jnp.full((heads_here, local_rows), START_PEAK, jnp.float32),
            jnp.zeros((heads_here, local_rows), jnp.float32),
        )
        (peak_value, mass_sum), unused = lax.scan(
            peak_step, initial, (attend_blocks, attend_pos_blocks)
        )
        attend_log_mass = peak_value + jnp.log(mass_sum)

        def value_step(running, packed):
            scores, unused = block_scores(attend_query_low, packed[0], packed[1], attend_query_pos)
            weights_low = jnp.exp(scores - attend_log_mass[..., None]).astype(jnp.bfloat16)
            values_here = expand(packed[0][:, 1])
            return (
                running
                + jnp.einsum(
                    "gqk,kgd->qgd", weights_low, values_here, preferred_element_type=jnp.float32
                ),
                None,
            )

        attend_mixture, unused = lax.scan(
            value_step,
            jnp.zeros((local_rows, heads_here, HEAD_SIZE), jnp.float32),
            (attend_blocks, attend_pos_blocks),
        )
        layer_mixture_low = attend_mixture.reshape(local_rows, heads_here * HEAD_SIZE).astype(
            jnp.bfloat16
        )
        layer_residual = layer_residual + scatter_rows(
            jnp.dot(layer_mixture_low, layer_out_full, preferred_element_type=jnp.float32)
        )
        normed, layer_ffn_unit, layer_ffn_inv = norm_parts(layer_residual, layer_ffn_gain)
        layer_second_all = gather_rows(normed.astype(jnp.bfloat16))
        layer_gateup = jnp.dot(
            layer_second_all, layer_gateup_full, preferred_element_type=jnp.float32
        )
        layer_hidden_low = (
            jax.nn.silu(layer_gateup[:, :units_here]) * layer_gateup[:, units_here:]
        ).astype(jnp.bfloat16)
        result = layer_residual + scatter_rows(
            jnp.dot(layer_hidden_low, layer_down_full, preferred_element_type=jnp.float32)
        )
        layer_kept_state = (
            layer_attn_unit,
            layer_attn_inv,
            layer_normed_own,
            layer_normed_all,
            layer_query_unit,
            layer_query_inv,
            layer_query_low,
            layer_key_unit,
            layer_key_inv,
            layer_key_value_gathered,
            attend_log_mass,
            attend_mixture,
            layer_mixture_low,
            layer_ffn_unit,
            layer_ffn_inv,
            layer_second_all,
            layer_gateup,
            layer_hidden_low,
            layer_query_cos,
            layer_query_sin,
            layer_own_cos,
            layer_own_sin,
            positions_query_pos,
            positions_key_pos,
        )
        result, kept_state = (result, layer_kept_state)
        result_low = result.astype(jnp.bfloat16)
        produced.append(result_low)
        kept_all.append(kept_state)
        if step_index + 1 < step_count:
            received = from_behind(result_low, "section", 1)
    kept_stack = jax.tree.map(lambda *parts: jnp.stack(parts), *kept_all)
    produced_stack = jnp.stack(produced)
    returned = jnp.zeros_like(inputs[0])
    consumed = []
    pieces_all = []
    for step_index in range(step_count):
        source = jnp.clip(step_index - (sections - 1) + 2 * section_id, 0, step_count - 1)
        kept_state = jax.tree.map(
            lambda stacked: lax.dynamic_index_in_dim(stacked, source, 0, keepdims=False), kept_stack
        )
        live_factor = 1.0 if step_index < batches else 0.0
        top_grad = cotangent[min(step_index, batches - 1)].astype(jnp.float32) * live_factor
        upstream = jnp.where(section_id == sections - 1, top_grad, returned.astype(jnp.float32))
        grad_input, pieces = layer_backward(upstream, kept_state, weights_now)
        pieces_all.append(pieces)
        grad_low = grad_input.astype(jnp.bfloat16)
        consumed.append(grad_low)
        if step_index + 1 < step_count:
            returned = from_behind(grad_low, "section", -1)
    full_set = grads_from(pieces_all)
    consumed_stack = jnp.stack(consumed)
    section_result = jnp.stack(
        [
            lax.dynamic_index_in_dim(produced_stack, batch_no + section_id, 0, keepdims=False)
            for batch_no in range(batches)
        ]
    )[None]
    input_result = jnp.stack(
        [
            lax.dynamic_index_in_dim(
                consumed_stack, batch_no + sections - 1 - section_id, 0, keepdims=False
            )
            for batch_no in range(batches)
        ]
    )[None]
    return (
        section_result,
        input_result,
        lax.psum_scatter(
            full_set[0].astype(jnp.bfloat16), "ctx", scatter_dimension=0, tiled=True
        ).astype(jnp.float32)[None],
        lax.psum_scatter(full_set[4], ("tensor", "ctx"), scatter_dimension=0, tiled=True)[None],
        lax.psum_scatter(
            full_set[1].astype(jnp.bfloat16), "ctx", scatter_dimension=1, tiled=True
        ).astype(jnp.float32)[None],
        lax.psum_scatter(
            full_set[2].reshape(MODEL_WIDTH, 2, units_here).astype(jnp.bfloat16),
            "ctx",
            scatter_dimension=0,
            tiled=True,
        ).astype(jnp.float32)[None],
        lax.psum_scatter(
            full_set[3].astype(jnp.bfloat16), "ctx", scatter_dimension=1, tiled=True
        ).astype(jnp.float32)[None],
        lax.psum_scatter(full_set[5], ("tensor", "ctx"), scatter_dimension=0, tiled=True)[None],
    )


C_BIT, X_BIT, Y_BIT, Z_BIT = 1, 2, 4, 8
MESH_ID = pl.DeviceIdType.MESH
ANY = pl.BlockSpec(memory_space=pl.ANY)
VMEM = pl.BlockSpec(memory_space=pltpu.VMEM)
SMEM = pl.BlockSpec(memory_space=pltpu.SMEM)
F32 = jnp.float32
BF16 = jnp.bfloat16
GROUP = QUERY_HEADS // KEY_VALUE_HEADS
KEY_COLUMNS = KEY_VALUE_HEADS * HEAD_SIZE
QUERY_COLUMNS = QUERY_HEADS * HEAD_SIZE
SCALE = HEAD_SIZE ** (-0.5)
VMEM_BYTES = 60 * 2**20
CYCLES = ((X_BIT, Y_BIT, Z_BIT), (Y_BIT, Z_BIT, X_BIT), (Z_BIT, X_BIT, Y_BIT))
TOWARD_Z = ((X_BIT, Y_BIT, Z_BIT), (Y_BIT, X_BIT, Z_BIT))


class Place:
    def __init__(self):
        self.section = lax.axis_index("section")
        ctx = lax.axis_index("ctx")
        self.bits = (ctx % 2, (ctx // 2) % 2, ctx // 4, lax.axis_index("tensor"))

    def flipped(self, mask):
        return [1 - bit if mask & (1 << i) else bit for i, bit in enumerate(self.bits)]

    def block(self, mask=0):
        core, x, y, z = self.flipped(mask)
        return z * 8 + y * 4 + x * 2 + core

    def ctx(self, mask=0):
        core, x, y, z = self.flipped(mask)
        return y * 4 + x * 2 + core

    def peer(self, mask):
        core, x, y, z = self.flipped(mask)
        return (self.section, z, y * 4 + x * 2 + core)

    def other_section(self, section):
        core, x, y, z = self.bits
        return (section, z, y * 4 + x * 2 + core)


def remote(src, dst, send, recv, device):
    return pltpu.make_async_remote_copy(
        src_ref=src, dst_ref=dst, send_sem=send, recv_sem=recv, device_id=device, device_id_type=MESH_ID
    )


def greet(place, masks, into=None):
    barrier = pltpu.get_barrier_semaphore()
    for mask in masks:
        pl.semaphore_signal(barrier, inc=1, device_id=place.peer(mask), device_id_type=MESH_ID)
    if into is None:
        pl.semaphore_wait(barrier, len(masks))
        return

    @pl.when(place.section == into)
    def _():
        pl.semaphore_signal(barrier, inc=1, device_id=place.other_section(1 - into), device_id_type=MESH_ID)
        pl.semaphore_wait(barrier, len(masks))

    @pl.when(place.section != into)
    def _():
        pl.semaphore_wait(barrier, len(masks) + 1)


def column_pieces(widths, orders):
    start, pieces = 0, []
    for width, order in zip(widths, orders):
        pieces.append(((slice(None), pl.ds(start, width)), order))
        start += width
    return pieces


def row_pieces(heights, orders):
    start, pieces = 0, []
    for height, order in zip(heights, orders):
        pieces.append(((pl.ds(start, height), slice(None)), order))
        start += height
    return pieces


class Gather:
    def __init__(self, place, buf, pieces, send, recv):
        self.place, self.buf, self.pieces = place, buf, pieces
        self.send, self.recv = send, recv
        self.sent = []

    def _copy(self, piece, mask, dim):
        index = self.pieces[piece][0]
        block = self.place.block(mask)
        where = self.buf.at[(block,) + index]
        slot = piece * 16 + (mask ^ dim)
        return remote(where, where, self.send.at[slot], self.recv.at[slot], self.place.peer(dim))

    def _start(self, piece, mask, dim):
        copy = self._copy(piece, mask, dim)
        copy.start()
        self.sent.append(copy)

    def _arrived(self, piece, mask, dim):
        index = self.pieces[piece][0]
        where = self.buf.at[(self.place.block(mask),) + index]
        slot = piece * 16 + mask
        remote(where, where, self.send.at[slot], self.recv.at[slot], self.place.peer(dim)).wait_recv()

    def start(self):
        for piece, (_, order) in enumerate(self.pieces):
            for dim in order:
                self._start(piece, 0, dim)
        for piece in range(len(self.pieces)):
            self._start(piece, 0, C_BIT)

    def finish(self):
        pieces = list(enumerate(self.pieces))
        for piece, (_, (d0, d1, d2)) in pieces:
            self._arrived(piece, d0, d0)
            self._start(piece, d0, d1)
            self._start(piece, d0, d2)
            self._start(piece, d0, C_BIT)
        for piece, (_, (d0, d1, d2)) in pieces:
            self._arrived(piece, d1, d1)
            self._start(piece, d1, d2)
            self._start(piece, d1, C_BIT)
        for piece, (_, (d0, d1, d2)) in pieces:
            self._arrived(piece, d0 ^ d1, d1)
            self._start(piece, d0 ^ d1, d2)
            self._start(piece, d0 ^ d1, C_BIT)
        for part in (0, 1, 2, 3):
            for piece, (_, (d0, d1, d2)) in pieces:
                mask = (d2, d0 ^ d2, d1 ^ d2, d0 ^ d1 ^ d2)[part]
                self._arrived(piece, mask, d2)
                self._start(piece, mask, C_BIT)
        for piece, (_, (d0, d1, d2)) in pieces:
            for mask in (0, d0, d1, d0 ^ d1, d2, d0 ^ d2, d1 ^ d2, d0 ^ d1 ^ d2):
                self._arrived(piece, mask ^ C_BIT, C_BIT)
        for copy in self.sent:
            copy.wait_send()


class Scatter:
    MASKS = (14, 12, 10, 6, 8, 4, 2, 0)

    def __init__(self, place, part, sib_recv, landed, pieces, send, recv, put):
        self.place, self.part, self.pieces, self.put = place, part, pieces, put
        self.sib_recv, self.landed = sib_recv, landed
        self.send, self.recv = send, recv
        self.sent = []

    def _sib(self, i, mask):
        slot = 3 * 16 + i
        return remote(
            self.part.at[self.place.block(mask | C_BIT)],
            self.sib_recv.at[i],
            self.send.at[slot],
            self.recv.at[slot],
            self.place.peer(C_BIT),
        )

    def start_sibling(self):
        for i, mask in enumerate(self.MASKS):
            copy = self._sib(i, mask)
            copy.start()
            self.sent.append(copy)

    def add_sibling(self):
        for i, mask in enumerate(self.MASKS):
            self._sib(i, mask).wait_recv()
            block = self.place.block(mask)
            self.part[block] = (self.part[block].astype(F32) + self.sib_recv[i].astype(F32)).astype(BF16)

    def _copy(self, piece, mask, dim):
        index = self.pieces[piece][0]
        slot = piece * 16 + mask
        return remote(
            self.part.at[(self.place.block(mask),) + index],
            self.landed.at[(mask // 2,) + index],
            self.send.at[slot],
            self.recv.at[slot],
            self.place.peer(dim),
        )

    def _start(self, piece, mask, dim):
        copy = self._copy(piece, mask, dim)
        copy.start()
        self.sent.append(copy)

    def _sum(self, piece, mask, dim):
        self._copy(piece, mask, dim).wait_recv()
        index = self.pieces[piece][0]
        at = (self.place.block(mask ^ dim),) + index
        return at, self.part[at].astype(F32) + self.landed[(mask // 2,) + index].astype(F32)

    def _add(self, piece, mask, dim):
        at, total = self._sum(piece, mask, dim)
        self.part[at] = total.astype(BF16)

    def finish(self):
        pieces = list(enumerate(self.pieces))
        for piece, (_, (d0, d1, d2)) in pieces:
            for mask in (d0 ^ d1 ^ d2, d1 ^ d2):
                self._start(piece, mask, d2)
        for piece, (_, (d0, d1, d2)) in pieces:
            for mask in (d0 ^ d2, d2):
                self._start(piece, mask, d2)
        for piece, (_, (d0, d1, d2)) in pieces:
            for mask in (d0 ^ d1, d1):
                self._add(piece, mask ^ d2, d2)
                self._start(piece, mask, d1)
        for piece, (_, (d0, d1, d2)) in pieces:
            for mask in (d0, 0):
                self._add(piece, mask ^ d2, d2)
        for piece, (_, (d0, d1, d2)) in pieces:
            self._add(piece, d0 ^ d1, d1)
            self._start(piece, d0, d0)
        for piece, (_, (d0, d1, d2)) in pieces:
            self._add(piece, d1, d1)
        for piece, (index, (d0, d1, d2)) in pieces:
            _, total = self._sum(piece, d0, d0)
            self.put(index, total)

    def drain(self):
        for copy in self.sent:
            copy.wait_send()


def gather_sems(pieces):
    return [pltpu.SemaphoreType.DMA((16 * pieces,)), pltpu.SemaphoreType.DMA((16 * pieces,))]


def scatter_sems():
    return [pltpu.SemaphoreType.DMA((64,)), pltpu.SemaphoreType.DMA((64,))]


def kernel_params(collective):
    return pltpu.CompilerParams(collective_id=collective, has_side_effects=True, vmem_limit_bytes=VMEM_BYTES)


def weights_kernel(q_ref, kv_ref, o_ref, gu_ref, dn_ref, g_ref, q_all, kv_all, o_all, gu_mine, dn_mine, g_all,
                   q_send, q_recv, kv_send, kv_recv, o_send, o_recv, g_send, g_recv, a_send, a_recv, local):
    place = Place()
    own = place.block()
    ctx = place.ctx()
    units = dn_mine.shape[0]
    width = dn_ref.shape[1]
    others = (1, 2, 3, 4, 5, 6, 7)
    greet(place, others + (Z_BIT,))
    locals_ = []
    for i, (src, dst) in enumerate(((q_ref, q_all), (kv_ref, kv_all), (o_ref, o_all), (g_ref, g_all))):
        copy = pltpu.make_async_copy(src, dst.at[own], local.at[i])
        copy.start()
        locals_.append(copy)
    for copy in locals_:
        copy.wait()
    gathers = []
    for buf, send, recv in ((q_all, q_send, q_recv), (kv_all, kv_send, kv_recv), (o_all, o_send, o_recv)):
        half = buf.shape[1] // 2
        gathers.append(Gather(place, buf, row_pieces((half, half), TOWARD_Z), send, recv))
    gathers.append(Gather(place, g_all, row_pieces((g_ref.shape[0],), TOWARD_Z), g_send, g_recv))
    for gather in gathers:
        gather.start()

    def shares(mask, back=0):
        there = place.ctx(mask)
        rows = pl.ds(pl.multiple_of(there * units, 16), units)
        columns = pl.ds(pl.multiple_of((place.ctx(mask) if back else ctx) * width, 128), width)
        return (gu_ref.at[:, rows, :], gu_mine.at[:, :, columns]), (dn_ref.at[rows, :], dn_mine.at[:, columns])

    sent = []
    for mask in (6, 7, 2, 3, 4, 5, 1):
        for j, (src, dst) in enumerate(shares(mask)):
            slot = 2 * mask + j
            copy = remote(src, dst, a_send.at[slot], a_recv.at[slot], place.peer(mask))
            copy.start()
            sent.append(copy)
    kept = []
    for j, (src, dst) in enumerate(shares(0)):
        copy = pltpu.make_async_copy(src, dst, local.at[4 + j])
        copy.start()
        kept.append(copy)
    for gather in gathers:
        gather.finish()
    for copy in kept:
        copy.wait()
    for mask in others:
        for j, (src, dst) in enumerate(shares(mask, 1)):
            slot = 2 * mask + j
            remote(src, dst, a_send.at[slot], a_recv.at[slot], place.peer(mask)).wait_recv()
    for copy in sent:
        copy.wait_send()


def bring_weights(query, keyval, out, gateup, down, gains):
    units = down.shape[0] // 8
    width = gateup.shape[2] * 8
    shape = jax.ShapeDtypeStruct
    return pl.pallas_call(
        weights_kernel,
        out_shape=(
            shape((16,) + query.shape, BF16),
            shape((16,) + keyval.shape, BF16),
            shape((16,) + out.shape, BF16),
            shape((2, units, width), BF16),
            shape((units, width), BF16),
            shape((16,) + gains.shape, BF16),
        ),
        in_specs=[ANY] * 6,
        out_specs=[ANY] * 6,
        scratch_shapes=gather_sems(2) * 3
        + gather_sems(1)
        + [pltpu.SemaphoreType.DMA((16,)), pltpu.SemaphoreType.DMA((16,)), pltpu.SemaphoreType.DMA((6,))],
        compiler_params=kernel_params(0),
    )(query, keyval, out, gateup, down, gains)


def dot(left, right):
    return lax.dot_general(left, right, (((1,), (0,)), ((), ())), preferred_element_type=F32)


def dot_nt(left, right):
    return lax.dot_general(left, right, (((1,), (1,)), ((), ())), preferred_element_type=F32)


def dot_tn(left, right):
    return lax.dot_general(left, right, (((0,), (0,)), ((), ())), preferred_element_type=F32)


def unit_rows(values):
    inverse = lax.rsqrt(jnp.mean(values * values, axis=-1, keepdims=True) + EPSILON)
    return values * inverse, inverse


def unit_back(scaled, unit, inverse):
    return inverse * (scaled - unit * jnp.mean(scaled * unit, axis=-1, keepdims=True))


def stack_heads(values, heads):
    return jnp.concatenate([values[:, h * HEAD_SIZE : (h + 1) * HEAD_SIZE] for h in range(heads)], axis=0)


def spread_heads(values, heads):
    rows = values.shape[0] // heads
    return jnp.concatenate([values[h * rows : (h + 1) * rows] for h in range(heads)], axis=1)


def turned(values):
    half = HEAD_SIZE // 2
    return jnp.concatenate([values[:, half:], values[:, :half]], axis=1)


def tall(rows, times):
    return jnp.concatenate([rows] * times, axis=0)


def rope(values, cos, sin, heads):
    return values * tall(cos, heads) + turned(values) * tall(sin, heads)


def unrope(values, cos, sin, heads):
    return values * tall(cos, heads) - turned(values) * tall(sin, heads)


def low32(values):
    return values.astype(BF16).astype(F32)


def attention_inputs(m, rowtab, postab, bias):
    allowed = postab[m, 0:1, :] <= rowtab[m, :, 128:129]
    bias[...] = jnp.where(allowed, 0.0, -jnp.inf)


def split_keys(kv, k5, v5):
    rows = kv.shape[0] * kv.shape[1]
    for g in range(KEY_VALUE_HEADS):
        k5[g] = kv[:, :, g * HEAD_SIZE : (g + 1) * HEAD_SIZE].reshape(rows, HEAD_SIZE)
        v5[g] = kv[:, :, KEY_COLUMNS + g * HEAD_SIZE : KEY_COLUMNS + (g + 1) * HEAD_SIZE].reshape(rows, HEAD_SIZE)


def probabilities(queries, keys, bias):
    scores = dot_nt(queries, keys) + tall(bias, GROUP)
    raised = jnp.exp(scores - jnp.max(scores, axis=-1, keepdims=True))
    return raised / jnp.sum(raised, axis=-1, keepdims=True)


E_WIDTHS = (768, 640, 640)
KV_WIDTHS = (256, 256, 128)
CHUNK = 256


def load(src, dst, sem):
    copy = pltpu.make_async_copy(src, dst, sem)
    copy.start()
    return copy


def forward_kernel(m_ref, inputs_ref, received_ref, rowtab, postab, gains, q_hbm, kv_hbm, o_hbm, gu_hbm, dn_hbm,
                   result_ref, passed_ref, u_ref, h_ref, qraw_ref, kraw_ref, qrot_ref, kvall_hbm, ob_ref, e_hbm, gu_t_hbm,
                   hid_hbm,
                   wq, wkv, wo, wgu, wdn, kv, e, gu_t, hid, k5, v5, o5, bias, part, sib_recv, landed,
                   kv_send, kv_recv, e_send, e_recv, y_send, y_recv, pass_send, pass_recv, local):
    place = Place()
    own = place.block()
    loads = [
        load(src, dst, local.at[i])
        for i, (src, dst) in enumerate(((kv_hbm, wkv), (q_hbm, wq), (o_hbm, wo), (gu_hbm, wgu), (dn_hbm, wdn)))
    ]
    greet(place, (C_BIT, X_BIT, Y_BIT, Z_BIT), into=1)
    m = m_ref[0]
    rows = u_ref.shape[0]
    width = u_ref.shape[1]
    attn_gain, ffn_gain = gains[:, :width], gains[:, width : 2 * width]
    q_gain = gains[:, 2 * width : 2 * width + HEAD_SIZE]
    k_gain = gains[:, 2 * width + HEAD_SIZE : 2 * width + 2 * HEAD_SIZE]
    cos, sin = rowtab[m, :, :HEAD_SIZE], rowtab[m, :, HEAD_SIZE : 2 * HEAD_SIZE]

    u_low = jnp.where(place.section == 0, inputs_ref[m], received_ref[...])
    u_ref[...] = u_low
    u = u_low.astype(F32)
    a = (unit_rows(u)[0] * attn_gain).astype(BF16)

    loads[0].wait()
    kv_raw = dot(a, wkv[...].reshape(width, 2 * KEY_COLUMNS))
    k_raw = stack_heads(kv_raw[:, :KEY_COLUMNS], KEY_VALUE_HEADS)
    kraw_ref[...] = k_raw
    k_low = rope(unit_rows(k_raw)[0] * k_gain, cos, sin, KEY_VALUE_HEADS).astype(BF16)
    kv[own] = jnp.concatenate([spread_heads(k_low, KEY_VALUE_HEADS), kv_raw[:, KEY_COLUMNS:].astype(BF16)], axis=1)
    kv_gather = Gather(place, kv, column_pieces(KV_WIDTHS, CYCLES), kv_send, kv_recv)
    kv_gather.start()

    loads[1].wait()
    half = QUERY_COLUMNS // 2
    q_raw = jnp.concatenate([dot(a, wq[t * 8 : t * 8 + 8].reshape(width, half)) for t in range(2)], axis=1)
    q_raw = stack_heads(q_raw, QUERY_HEADS)
    qraw_ref[...] = q_raw
    q_low = (rope(unit_rows(q_raw)[0] * q_gain, cos, sin, QUERY_HEADS) * SCALE).astype(BF16)
    qrot_ref[...] = q_low.reshape(KEY_VALUE_HEADS, GROUP * rows, HEAD_SIZE)
    attention_inputs(m, rowtab, postab, bias)
    kv_gather.finish()
    saves = [load(kv, kvall_hbm, local.at[5])]
    split_keys(kv, k5, v5)

    def attend(g, _):
        low = probabilities(qrot_ref[g], k5[g], bias[...]).astype(BF16)
        o5[g] = dot(low, v5[g])
        return 0

    lax.fori_loop(0, KEY_VALUE_HEADS, attend, 0)
    mixture = spread_heads(o5[...].reshape(QUERY_HEADS * rows, HEAD_SIZE), QUERY_HEADS).astype(BF16)
    ob_ref[...] = mixture
    loads[2].wait()
    for c in range(8):
        block = pl.ds(c * (width // 8), width // 8)
        h_ref[:, block] = u_ref[:, block].astype(F32) + (
            dot(ob_ref[:, :half], wo[c]) + dot(ob_ref[:, half:], wo[8 + c])
        )
    e[own] = (unit_rows(h_ref[...])[0] * ffn_gain).astype(BF16)
    e_gather = Gather(place, e, column_pieces(E_WIDTHS, CYCLES), e_send, e_recv)
    e_gather.start()
    loads[3].wait()
    loads[4].wait()
    units = wdn.shape[0]
    e_gather.finish()
    saves.append(load(e, e_hbm, local.at[6]))

    blocks = CHUNK // rows

    def expand(i, _):
        first = pl.multiple_of(i * blocks, blocks)
        tokens = pl.ds(pl.multiple_of(i * CHUNK, CHUNK), CHUNK)
        rows_here = e[pl.ds(first, blocks)].reshape(CHUNK, width)
        both = dot_nt(wgu[...].reshape(2 * units, width), rows_here)
        gu_t[:, tokens] = both
        gate = both[:units]
        hidden = (gate * jax.nn.sigmoid(gate) * both[units:]).astype(BF16)
        hid[:, tokens] = hidden
        part[pl.ds(first, blocks)] = dot_tn(hidden, wdn[...]).astype(BF16).reshape(blocks, rows, width)
        return 0

    lax.fori_loop(0, e.shape[0] // blocks, expand, 0)
    saves.append(load(gu_t, gu_t_hbm, local.at[7]))
    saves.append(load(hid, hid_hbm, local.at[8]))

    def put(index, total):
        result_ref[index] = (h_ref[index] + total).astype(BF16)

    scatter = Scatter(place, part, sib_recv, landed, column_pieces(E_WIDTHS, CYCLES), y_send, y_recv, put)
    scatter.start_sibling()
    scatter.add_sibling()
    scatter.finish()
    onward = remote(result_ref, passed_ref, pass_send, pass_recv, place.other_section(1))

    @pl.when(place.section == 0)
    def _():
        onward.start()
        passed_ref[...] = jnp.zeros_like(passed_ref)
        onward.wait_send()

    @pl.when(place.section == 1)
    def _():
        onward.wait_recv()

    scatter.drain()
    for copy in saves:
        copy.wait()


def forward_step(m, inputs, received, rowtab, postab, gains, weights):
    q_all, kv_all, o_all, gu_mine, dn_mine = weights
    rows, width = received.shape
    units = dn_mine.shape[0]
    tokens = 16 * rows
    shape = jax.ShapeDtypeStruct
    return pl.pallas_call(
        forward_kernel,
        out_shape=(
            shape((rows, width), BF16),
            shape((rows, width), BF16),
            shape((rows, width), BF16),
            shape((rows, width), F32),
            shape((QUERY_HEADS * rows, HEAD_SIZE), F32),
            shape((KEY_VALUE_HEADS * rows, HEAD_SIZE), F32),
            shape((KEY_VALUE_HEADS, GROUP * rows, HEAD_SIZE), BF16),
            shape((16, rows, 2 * KEY_COLUMNS), BF16),
            shape((rows, QUERY_COLUMNS), BF16),
            shape((16, rows, width), BF16),
            shape((2 * units, tokens), F32),
            shape((units, tokens), BF16),
        ),
        in_specs=[SMEM] + [VMEM] * 5 + [ANY] * 5,
        out_specs=[VMEM] * 7 + [ANY, VMEM, ANY, ANY, ANY],
        scratch_shapes=[
            pltpu.VMEM(q_all.shape, BF16),
            pltpu.VMEM(kv_all.shape, BF16),
            pltpu.VMEM(o_all.shape, BF16),
            pltpu.VMEM(gu_mine.shape, BF16),
            pltpu.VMEM(dn_mine.shape, BF16),
            pltpu.VMEM((16, rows, 2 * KEY_COLUMNS), BF16),
            pltpu.VMEM((16, rows, width), BF16),
            pltpu.VMEM((2 * units, tokens), F32),
            pltpu.VMEM((units, tokens), BF16),
            pltpu.VMEM((KEY_VALUE_HEADS, tokens, HEAD_SIZE), BF16),
            pltpu.VMEM((KEY_VALUE_HEADS, tokens, HEAD_SIZE), BF16),
            pltpu.VMEM((KEY_VALUE_HEADS, GROUP * rows, HEAD_SIZE), F32),
            pltpu.VMEM((rows, tokens), F32),
            pltpu.VMEM((16, rows, width), BF16),
            pltpu.VMEM((8, rows, width), BF16),
            pltpu.VMEM((8, rows, width), BF16),
        ]
        + gather_sems(3)
        + gather_sems(3)
        + scatter_sems()
        + [pltpu.SemaphoreType.DMA, pltpu.SemaphoreType.DMA, pltpu.SemaphoreType.DMA((9,))],
        compiler_params=kernel_params(1),
    )(m, inputs, received, rowtab, postab, gains, q_all, kv_all, o_all, gu_mine, dn_mine)


def backward_kernel(m_ref, cot_ref, returned_ref, rowtab, postab, gains, q_hbm, kv_hbm, o_hbm, gu_hbm, dn_hbm,
                    u_0, h_0, qraw_0, kraw_0, qrot_0, kvall_0, gu_t_0, u_1, h_1, qraw_1, kraw_1, qrot_1, kvall_1, gu_t_1,
                    grad_ref, passed_ref, df_hbm, dgu_hbm, a_ref, da_ref, dq_ref, dkv_ref, gain_ref,
                    wq, wkv, wo, wgu, wdn, u, h, qraw, kraw, qrot, kvall, gu_t, df, dgu, dh, dx, k5, v5, do5, dq5, dk5,
                    dv5, bias, part, sib_recv, landed, part_kv, sib_recv_kv, landed_kv, dkv_own,
                    df_send, df_recv, de_send, de_recv, kv_send, kv_recv, pass_send, pass_recv, local, state):
    place = Place()
    own = place.block()
    kept = (u, h, qraw, kraw, qrot, kvall, gu_t)
    for section, held in ((0, (u_0, h_0, qraw_0, kraw_0, qrot_0, kvall_0, gu_t_0)),
                          (1, (u_1, h_1, qraw_1, kraw_1, qrot_1, kvall_1, gu_t_1))):

        @pl.when(place.section == section)
        def _(held=held):
            for i, (src, dst) in enumerate(zip(held, kept)):
                load(src, dst, state.at[i])

    loads = [
        load(src, dst, local.at[i])
        for i, (src, dst) in enumerate(((dn_hbm, wdn), (gu_hbm, wgu), (o_hbm, wo), (q_hbm, wq), (kv_hbm, wkv)))
    ]
    greet(place, (C_BIT, X_BIT, Y_BIT, Z_BIT), into=0)
    m = m_ref[0]
    rows, width = u.shape
    half = QUERY_COLUMNS // 2
    attn_gain, ffn_gain = gains[:, :width], gains[:, width : 2 * width]
    q_gain = gains[:, 2 * width : 2 * width + HEAD_SIZE]
    k_gain = gains[:, 2 * width + HEAD_SIZE : 2 * width + 2 * HEAD_SIZE]
    cos, sin = rowtab[m, :, :HEAD_SIZE], rowtab[m, :, HEAD_SIZE : 2 * HEAD_SIZE]

    dy = jnp.where(place.section == 1, cot_ref[m], returned_ref[...])
    df[own] = dy
    dh[...] = dy.astype(F32)
    df_gather = Gather(place, df, column_pieces(E_WIDTHS, CYCLES), df_send, df_recv)
    df_gather.start()
    for i, dst in enumerate(kept):
        pltpu.make_async_copy(dst, dst, state.at[i]).wait()
    attention_inputs(m, rowtab, postab, bias)
    split_keys(kvall, k5, v5)
    loads[0].wait()
    loads[1].wait()
    df_gather.finish()
    saves = [load(df, df_hbm, local.at[5])]
    units = wdn.shape[0]
    blocks = CHUNK // rows

    def shrink(i, _):
        first = pl.multiple_of(i * blocks, blocks)
        tokens = pl.ds(pl.multiple_of(i * CHUNK, CHUNK), CHUNK)
        rows_here = df[pl.ds(first, blocks)].reshape(CHUNK, width)
        dhidden = dot_nt(wdn[...], rows_here)
        gate, up = gu_t[:units, tokens], gu_t[units:, tokens]
        open_ = jax.nn.sigmoid(gate)
        dgate = dhidden * up * (open_ * (1.0 + gate * (1.0 - open_)))
        both = jnp.concatenate([dgate, dhidden * (gate * open_)], axis=0).astype(BF16)
        dgu[:, tokens] = both
        part[pl.ds(first, blocks)] = (
            dot_tn(both, wgu[...].reshape(2 * units, width)).astype(BF16).reshape(blocks, rows, width)
        )
        return 0

    lax.fori_loop(0, df.shape[0] // blocks, shrink, 0)
    saves.append(load(dgu, dgu_hbm, local.at[6]))

    def put(index, total):
        dx[index] = total

    scatter = Scatter(place, part, sib_recv, landed, column_pieces(E_WIDTHS, CYCLES), de_send, de_recv, put)
    scatter.start_sibling()
    scatter.add_sibling()
    scatter.finish()
    unit, inverse = unit_rows(h[...])
    gain_ref[:, width : 2 * width] = jnp.sum(dx[...] * unit, axis=0, keepdims=True)
    dh[...] = dh[...] + unit_back(dx[...] * ffn_gain, unit, inverse)
    da_ref[...] = dh[...].astype(BF16)
    loads[2].wait()
    for t in range(2):
        total = jnp.zeros((rows, half), F32)
        for c in range(8):
            total = total + dot_nt(da_ref[:, c * (width // 8) : (c + 1) * (width // 8)], wo[t * 8 + c])
        heads = QUERY_HEADS // 2
        stacked = stack_heads(total.astype(BF16), heads)
        do5[t * heads * rows : (t + 1) * heads * rows] = stacked

    def attend(g, _):
        at = pl.ds(pl.multiple_of(g * GROUP * rows, GROUP * rows), GROUP * rows)
        weights = probabilities(qrot[g], k5[g], bias[...])
        grads = do5[at]
        dweights = dot_nt(grads, v5[g])
        inner = jnp.sum(weights * dweights, axis=-1, keepdims=True)
        dscores = (weights * (dweights - inner)).astype(BF16)
        dq5[at] = dot(dscores, k5[g])
        dk5[g] = dot_tn(dscores, qrot[g])
        dv5[g] = dot_tn(weights.astype(BF16), grads)
        return 0

    lax.fori_loop(0, KEY_VALUE_HEADS, attend, 0)
    for b in range(16):
        at = slice(b * rows, (b + 1) * rows)
        part_kv[b] = jnp.concatenate(
            [dk5[g, at] for g in range(KEY_VALUE_HEADS)] + [dv5[g, at] for g in range(KEY_VALUE_HEADS)], axis=1
        ).astype(BF16)

    def put_kv(index, total):
        dkv_own[index] = total

    scatter_kv = Scatter(
        place, part_kv, sib_recv_kv, landed_kv, column_pieces(KV_WIDTHS, CYCLES), kv_send, kv_recv, put_kv
    )
    scatter_kv.start_sibling()
    scatter_kv.add_sibling()

    q_unit, q_inverse = unit_rows(qraw[...])
    dqhat = unrope(dq5[...] * SCALE, cos, sin, QUERY_HEADS)
    dq_gain = jnp.sum(dqhat * q_unit, axis=0, keepdims=True)
    dq_raw = unit_back(dqhat * q_gain, q_unit, q_inverse)
    dq_ref[...] = spread_heads(dq_raw, QUERY_HEADS).astype(BF16)
    loads[3].wait()
    loads[4].wait()
    dx[...] = dot_nt(dq_ref[:, :half], wq[:8].reshape(width, half)) + dot_nt(dq_ref[:, half:], wq[8:].reshape(width, half))
    scatter_kv.finish()

    k_unit, k_inverse = unit_rows(kraw[...])
    dkhat = unrope(stack_heads(dkv_own[:, :KEY_COLUMNS], KEY_VALUE_HEADS), cos, sin, KEY_VALUE_HEADS)
    dk_gain = jnp.sum(dkhat * k_unit, axis=0, keepdims=True)
    dk_raw = unit_back(dkhat * k_gain, k_unit, k_inverse)
    gain_ref[:, 2 * width :] = jnp.concatenate([dq_gain, dk_gain], axis=1)
    dkv_ref[...] = jnp.concatenate([spread_heads(dk_raw, KEY_VALUE_HEADS), dkv_own[:, KEY_COLUMNS:]], axis=1).astype(BF16)
    dx[...] = dx[...] + dot_nt(dkv_ref[...], wkv[...].reshape(width, 2 * KEY_COLUMNS))
    unit, inverse = unit_rows(u[...].astype(F32))
    a_ref[...] = (unit * attn_gain).astype(BF16)
    gain_ref[:, :width] = jnp.sum(dx[...] * unit, axis=0, keepdims=True)
    grad_ref[...] = (dh[...] + unit_back(dx[...] * attn_gain, unit, inverse)).astype(BF16)
    onward = remote(grad_ref, passed_ref, pass_send, pass_recv, place.other_section(0))

    @pl.when(place.section == 1)
    def _():
        onward.start()
        passed_ref[...] = jnp.zeros_like(passed_ref)
        onward.wait_send()

    @pl.when(place.section == 0)
    def _():
        onward.wait_recv()

    scatter.drain()
    scatter_kv.drain()
    for copy in saves:
        copy.wait()


def backward_step(m, cotangent, returned, rowtab, postab, gains, weights, state_0, state_1):
    q_all, kv_all, o_all, gu_mine, dn_mine = weights
    rows, width = returned.shape
    units = dn_mine.shape[0]
    tokens = 16 * rows
    shape = jax.ShapeDtypeStruct
    heads = KEY_VALUE_HEADS
    return pl.pallas_call(
        backward_kernel,
        out_shape=(
            shape((rows, width), BF16),
            shape((rows, width), BF16),
            shape((16, rows, width), BF16),
            shape((2 * units, tokens), BF16),
            shape((rows, width), BF16),
            shape((rows, width), BF16),
            shape((rows, QUERY_COLUMNS), BF16),
            shape((rows, 2 * KEY_COLUMNS), BF16),
            shape(gains.shape, F32),
        ),
        in_specs=[SMEM] + [VMEM] * 5 + [ANY] * 5 + [ANY] * 14,
        out_specs=[VMEM, VMEM, ANY, ANY] + [VMEM] * 5,
        scratch_shapes=[pltpu.VMEM(w.shape, w.dtype) for w in weights]
        + [pltpu.VMEM(w.shape, w.dtype) for w in state_0]
        + [
            pltpu.VMEM((16, rows, width), BF16),
            pltpu.VMEM((2 * units, tokens), BF16),
            pltpu.VMEM((rows, width), F32),
            pltpu.VMEM((rows, width), F32),
            pltpu.VMEM((heads, tokens, HEAD_SIZE), BF16),
            pltpu.VMEM((heads, tokens, HEAD_SIZE), BF16),
            pltpu.VMEM((QUERY_HEADS * rows, HEAD_SIZE), BF16),
            pltpu.VMEM((QUERY_HEADS * rows, HEAD_SIZE), F32),
            pltpu.VMEM((heads, tokens, HEAD_SIZE), F32),
            pltpu.VMEM((heads, tokens, HEAD_SIZE), F32),
            pltpu.VMEM((rows, tokens), F32),
            pltpu.VMEM((16, rows, width), BF16),
            pltpu.VMEM((8, rows, width), BF16),
            pltpu.VMEM((8, rows, width), BF16),
            pltpu.VMEM((16, rows, 2 * KEY_COLUMNS), BF16),
            pltpu.VMEM((8, rows, 2 * KEY_COLUMNS), BF16),
            pltpu.VMEM((8, rows, 2 * KEY_COLUMNS), BF16),
            pltpu.VMEM((rows, 2 * KEY_COLUMNS), F32),
        ]
        + gather_sems(3)
        + scatter_sems()
        + scatter_sems()
        + [
            pltpu.SemaphoreType.DMA,
            pltpu.SemaphoreType.DMA,
            pltpu.SemaphoreType.DMA((7,)),
            pltpu.SemaphoreType.DMA((7,)),
        ],
        compiler_params=kernel_params(2),
    )(m, cotangent, returned, rowtab, postab, gains, *weights, *state_0, *state_1)


def grads_kernel(*refs):
    batches = 2
    fwd = refs[: 2 * batches * 3]
    bwd = refs[2 * batches * 3 : 2 * batches * 10]
    (gq_ref, gkv_ref, go_ref, gu_out, dn_out, gains_ref,
     e, hid, ob, df, dgu, a, da, dq, dkv, gain, pq, pkv, po, q_sib, kv_sib, o_sib, q_land, kv_land, o_land,
     gu_stage, dn_stage, gain_all,
     q_send, q_recv, kv_send, kv_recv, o_send, o_recv, g_send, g_recv, x_send, x_recv, local, kept) = refs[2 * batches * 10 :]
    place = Place()
    own = place.block()
    ctx = place.ctx()
    held = (ob, a, da, dq, dkv, gain, e, df, hid, dgu)
    for section in (0, 1):

        @pl.when(place.section == section)
        def _():
            for b in range(batches):
                e_b, hid_b, ob_b = fwd[(section * batches + b) * 3 : (section * batches + b) * 3 + 3]
                df_b, dgu_b, a_b, da_b, dq_b, dkv_b, gain_b = bwd[
                    (section * batches + b) * 7 : (section * batches + b) * 7 + 7
                ]
                for i, src in enumerate((ob_b, a_b, da_b, dq_b, dkv_b, gain_b, e_b, df_b, hid_b, dgu_b)):
                    load(src, held[i].at[b], kept.at[2 * i + b])

    others = (1, 2, 3, 4, 5, 6, 7)
    greet(place, others + (Z_BIT,))

    def arrived(index):
        for b in range(batches):
            pltpu.make_async_copy(held[index].at[b], held[index].at[b], kept.at[2 * index + b]).wait()

    for i in range(6):
        arrived(i)
    rows, width = a.shape[1:]
    half = QUERY_COLUMNS // 2
    lines = gain_all.shape[1]
    total_gain = gain[0] + gain[1]
    lanes = total_gain.shape[1] // 128
    gain_all[own, :lanes] = jnp.concatenate([total_gain[:, i * 128 : (i + 1) * 128] for i in range(lanes)], axis=0)
    gain_all[own, lanes:] = jnp.zeros((lines - lanes, 128), F32)
    gain_gather = Gather(place, gain_all, row_pieces((lines,), TOWARD_Z), g_send, g_recv)
    gain_gather.start()

    def both(ref, columns):
        return ref[:, :, columns].reshape(batches * rows, columns.size)

    def outer(c, _):
        wide = pl.ds(pl.multiple_of(c * (width // 8), width // 8), width // 8)
        for t in range(2):
            lead = pl.ds(t * half, half)
            pq[t * 8 + c] = dot_tn(both(a, wide), both(dq, lead)).astype(BF16)
            po[t * 8 + c] = dot_tn(both(ob, lead), both(da, wide)).astype(BF16)
            narrow = pl.ds(pl.multiple_of((t * 8 + c) * (width // 16), width // 16), width // 16)
            pkv[t * 8 + c] = dot_tn(both(a, narrow), both(dkv, pl.ds(0, 2 * KEY_COLUMNS))).astype(BF16)
        return 0

    lax.fori_loop(0, 8, outer, 0)

    def putter(ref):
        def put(index, total):
            ref[index] = total

        return put

    scatters = []
    for part, sib, land, send, recv, ref in (
        (pq, q_sib, q_land, q_send, q_recv, gq_ref),
        (po, o_sib, o_land, o_send, o_recv, go_ref),
        (pkv, kv_sib, kv_land, kv_send, kv_recv, gkv_ref),
    ):
        tall_half = part.shape[1] // 2
        scatters.append(
            Scatter(place, part, sib, land, row_pieces((tall_half, tall_half), TOWARD_Z), send, recv, putter(ref))
        )
    for scatter in scatters:
        scatter.start_sibling()
    for i in range(6, 10):
        arrived(i)
    units = hid.shape[1]

    def share(mask, back=0):
        rows_there = pl.ds(pl.multiple_of((place.ctx(mask) if back else ctx) * units, 16), units)
        return (gu_stage.at[mask], gu_out.at[:, rows_there, :]), (dn_stage.at[mask], dn_out.at[rows_there, :])

    sent = []
    for mask in (6, 7, 2, 3, 4, 5, 1, 0):
        columns = pl.ds(pl.multiple_of(place.ctx(mask) * (width // 8), width // 8), width // 8)
        gu = jnp.zeros((2 * units, width // 8), F32)
        dn = jnp.zeros((units, width // 8), F32)
        for b in range(batches):
            gu = gu + dot(dgu[b], e[b, :, :, columns].reshape(16 * rows, width // 8))
            dn = dn + dot(hid[b], df[b, :, :, columns].reshape(16 * rows, width // 8))
        gu_stage[mask] = gu.astype(BF16).reshape(2, units, width // 8)
        dn_stage[mask] = dn.astype(BF16)
        for j, (src, dst) in enumerate(share(mask)):
            slot = 2 * mask + j
            if mask:
                copy = remote(src, dst, x_send.at[slot], x_recv.at[slot], place.peer(mask))
                copy.start()
            else:
                copy = load(src, dst, local.at[j])
            sent.append((mask, copy))
    for scatter in scatters:
        scatter.add_sibling()
        scatter.finish()
    gain_gather.finish()
    total = gain_all[0]
    for i in range(1, 16):
        total = total + gain_all[i]
    gains_ref[...] = total
    for mask in others:
        for j, (src, dst) in enumerate(share(mask, 1)):
            slot = 2 * mask + j
            remote(src, dst, x_send.at[slot], x_recv.at[slot], place.peer(mask)).wait_recv()
    for mask, copy in sent:
        if mask:
            copy.wait_send()
        else:
            copy.wait()
    for scatter in scatters:
        scatter.drain()


def weight_grads(forward_0, forward_1, backward_0, backward_1):
    operands = []
    for side in (forward_0, forward_1, backward_0, backward_1):
        for kept in side:
            operands.extend(kept)
    (e, hid, ob), (df, dgu, a, da, dq, dkv, gain) = forward_0[0], backward_0[0]
    rows, width = a.shape
    units = hid.shape[0]
    columns = width // 8
    lines = -(-gain.shape[1] // 1024) * 8
    shape = jax.ShapeDtypeStruct
    half = QUERY_COLUMNS // 2
    parts = [(columns, half), (width // 16, 2 * KEY_COLUMNS), (half, columns)]
    return pl.pallas_call(
        grads_kernel,
        out_shape=(
            shape(parts[0], F32),
            shape(parts[1], F32),
            shape(parts[2], F32),
            shape((2, 8 * units, columns), BF16),
            shape((8 * units, columns), BF16),
            shape((lines, 128), F32),
        ),
        in_specs=[ANY] * len(operands),
        out_specs=[VMEM] * 3 + [ANY, ANY, VMEM],
        scratch_shapes=[pltpu.VMEM((2,) + x.shape, x.dtype) for x in (e, hid, ob, df, dgu, a, da, dq, dkv, gain)]
        + [pltpu.VMEM((16,) + x, BF16) for x in parts]
        + [pltpu.VMEM((8,) + x, BF16) for x in parts] * 2
        + [
            pltpu.VMEM((8, 2, units, columns), BF16),
            pltpu.VMEM((8, units, columns), BF16),
            pltpu.VMEM((16, lines, 128), F32),
        ]
        + scatter_sems() * 3
        + gather_sems(1)
        + [pltpu.SemaphoreType.DMA((16,)), pltpu.SemaphoreType.DMA((16,)), pltpu.SemaphoreType.DMA((2,))]
        + [pltpu.SemaphoreType.DMA((20,))],
        compiler_params=kernel_params(3),
    )(*operands)


def cube_device(
    inputs,
    cotangent,
    slot_order,
    query_weight,
    key_value_matrix,
    out_weight,
    gateup_weight,
    down_weight,
    norm_gains,
):
    section_id = lax.axis_index("section")
    tensor_id = lax.axis_index("tensor")
    context_id = lax.axis_index("ctx")
    batches, rows, width = inputs.shape
    tensors, contexts = 2, 8
    span = rows * tensors
    lanes = -(-norm_gains.shape[1] // 128)
    gains_block = jnp.pad(norm_gains[0], (0, lanes * 128 - norm_gains.shape[1])).reshape(lanes, 128)
    gains_block = jnp.pad(gains_block, ((0, -lanes % 16), (0, 0)))
    gateup_rows = jnp.transpose(gateup_weight[0], (1, 2, 0))
    brought = bring_weights(
        query_weight[0], key_value_matrix[0], out_weight[0], gateup_rows, down_weight[0], gains_block
    )
    weights = brought[:5]
    gains = brought[5].reshape(16, -1)[:, : norm_gains.shape[1]].reshape(1, -1).astype(F32)
    own_slot = jnp.sum(jnp.where(jnp.arange(contexts) == context_id, slot_order, 0), axis=1)
    own_pos = own_slot[:, None] * span + tensor_id * rows + jnp.arange(rows)[None, :]
    half_width = HEAD_SIZE // 2
    frequency = ROPE_BASE ** (-(jnp.arange(half_width, dtype=F32) * 2.0) / HEAD_SIZE)
    angles = own_pos.astype(F32)[..., None] * frequency
    cosine, sine = jnp.cos(angles), jnp.sin(angles)
    rowtab = jnp.concatenate(
        [cosine, cosine, -sine, sine, jnp.broadcast_to(own_pos.astype(F32)[..., None], (batches, rows, 128))], axis=-1
    )
    within = jnp.arange(tensors)[:, None, None] * rows + jnp.arange(rows)[None, None, :]
    key_pos = (slot_order[:, None, :, None] * span + within[None]).reshape(batches, 1, -1)
    postab = jnp.broadcast_to(key_pos.astype(F32), (batches, 8, key_pos.shape[-1]))
    received = jnp.zeros_like(inputs[0])
    kept = []
    for step in range(batches + 1):
        m = jnp.clip(step - section_id, 0, batches - 1).astype(jnp.int32).reshape(1)
        out = forward_step(m, inputs, received, rowtab, postab, gains, weights)
        kept.append(out)
        received = out[1]
    section_result = jnp.stack(
        [jnp.where(section_id == 0, kept[b][0], kept[b + 1][0]) for b in range(batches)]
    )[None]
    returned = jnp.zeros_like(inputs[0])
    back = []
    for step in range(batches + 1):
        m = jnp.clip(step - 1 + section_id, 0, batches - 1).astype(jnp.int32).reshape(1)
        states = [kept[at][2:8] + (kept[at][10],) for at in (max(step - 1, 0), min(step + 1, batches))]
        out = backward_step(m, cotangent, returned, rowtab, postab, gains, weights, *states)
        back.append(out)
        returned = out[1]
    input_result = jnp.stack(
        [jnp.where(section_id == 0, back[b + 1][0], back[b][0]) for b in range(batches)]
    )[None]

    def forward_kept(out):
        return (out[9], out[11], out[8])

    grad_query, grad_keyval, grad_out, grad_gateup, grad_down, grad_gains = weight_grads(
        [forward_kept(kept[b]) for b in range(batches)],
        [forward_kept(kept[b + 1]) for b in range(batches)],
        [back[b + 1][2:] for b in range(batches)],
        [back[b][2:] for b in range(batches)],
    )
    share = norm_gains.shape[1]
    gains_own = lax.dynamic_slice(grad_gains.reshape(-1), ((tensor_id * contexts + context_id) * share,), (share,))
    return (
        section_result,
        input_result,
        grad_query[None],
        grad_keyval[None],
        grad_out[None],
        jnp.transpose(grad_gateup, (2, 0, 1)).astype(F32)[None],
        grad_down.astype(F32)[None],
        gains_own[None],
    )


def fits_cube(mesh):
    return mesh.shape["section"] == 2 and mesh.shape["tensor"] == 2 and mesh.shape["ctx"] == 8


def solution(mesh):
    return jax.shard_map(
        cube_device if fits_cube(mesh) else per_device,
        mesh=mesh,
        in_specs=(
            P(None, ("tensor", "ctx"), None),
            P(None, ("tensor", "ctx"), None),
            P(),
            P("section", "ctx", "tensor"),
            P("section", ("tensor", "ctx"), None),
            P("section", "tensor", "ctx"),
            P("section", "ctx", None, "tensor"),
            P("section", "tensor", "ctx"),
            P("section", ("tensor", "ctx")),
        ),
        out_specs=(
            P("section", None, ("tensor", "ctx"), None),
            P("section", None, ("tensor", "ctx"), None),
            P("section", "ctx", "tensor"),
            P("section", ("tensor", "ctx"), None),
            P("section", "tensor", "ctx"),
            P("section", "ctx", None, "tensor"),
            P("section", "tensor", "ctx"),
            P("section", ("tensor", "ctx")),
        ),
        check_vma=False,
    )
```

```python
import typing

import jax
import jax.numpy as jnp
from jax import lax
from jax.experimental import pallas as pl
from jax.experimental.pallas import tpu as pltpu
from jax.sharding import PartitionSpec as P

MODEL_WIDTH = 2048
QUERY_HEADS = 20
KEY_VALUE_HEADS = 5
HEAD_SIZE = 64


EPSILON = 1e-06
ROPE_BASE = 10000.0
START_PEAK = -1e30


def from_behind(x, axis, by):
    devices = lax.axis_size(axis)
    pairs = [(i, i + by) for i in range(devices) if 0 <= i + by < devices]
    return lax.ppermute(x, axis, pairs)


def rope_tables(positions, head_width):
    half_width = head_width // 2
    frequency = ROPE_BASE ** (-(jnp.arange(half_width, dtype=jnp.float32) * 2.0) / head_width)
    angles = positions.astype(jnp.float32)[:, None] * frequency[None, :]
    return (jnp.cos(angles), jnp.sin(angles))


def rope_apply(values, cosine_rows, sine_rows):
    half_width = values.shape[-1] // 2
    first_half = values[..., :half_width]
    second_half = values[..., half_width:]
    cos_part = cosine_rows[:, None, :]
    sin_part = sine_rows[:, None, :]
    return jnp.concatenate(
        [
            first_half * cos_part - second_half * sin_part,
            second_half * cos_part + first_half * sin_part,
        ],
        axis=-1,
    )


def rope_back(incoming, cosine_rows, sine_rows):
    half_width = incoming.shape[-1] // 2
    first_half = incoming[..., :half_width]
    second_half = incoming[..., half_width:]
    cos_part = cosine_rows[:, None, :]
    sin_part = sine_rows[:, None, :]
    return jnp.concatenate(
        [
            first_half * cos_part + second_half * sin_part,
            second_half * cos_part - first_half * sin_part,
        ],
        axis=-1,
    )


def norm_parts(values, scaling):
    inverse = lax.rsqrt(jnp.mean(values * values, axis=-1, keepdims=True) + EPSILON)
    unit_rows = values * inverse
    return (unit_rows * scaling, unit_rows, inverse)


def norm_back(incoming, unit_rows, inverse, scaling):
    scaled = incoming * scaling
    inner = jnp.mean(scaled * unit_rows, axis=-1, keepdims=True)
    gain_grad = jnp.sum((incoming * unit_rows).reshape(-1, unit_rows.shape[-1]), axis=0)
    return (inverse * (scaled - unit_rows * inner), gain_grad)


def row_product(pieces_list, left_index, right_index):
    left_rows = jnp.concatenate([piece[left_index] for piece in pieces_list], axis=0)
    right_rows = jnp.concatenate([piece[right_index] for piece in pieces_list], axis=0)
    return lax.dot_general(
        left_rows, right_rows, (((0,), (0,)), ((), ())), preferred_element_type=jnp.float32
    )


def grads_from(pieces_list):
    grad_down = row_product(pieces_list, 0, 1)
    grad_gateup = row_product(pieces_list, 2, 3)
    grad_outw = row_product(pieces_list, 4, 5)
    grad_query = row_product(pieces_list, 6, 7)
    grad_keyval = row_product(pieces_list, 8, 9)
    grad_gain = pieces_list[0][10]
    for piece in pieces_list[1:]:
        grad_gain = grad_gain + piece[10]
    return (grad_query, grad_outw, grad_gateup, grad_down, grad_keyval, grad_gain)


def per_device(
    inputs,
    cotangent,
    slot_order,
    query_weight,
    key_value_matrix,
    out_weight,
    gateup_weight,
    down_weight,
    norm_gains,
):
    sections = lax.axis_size("section")
    tensors = lax.axis_size("tensor")
    contexts = lax.axis_size("ctx")
    section_id = lax.axis_index("section")
    tensor_id = lax.axis_index("tensor")
    context_id = lax.axis_index("ctx")
    batches = inputs.shape[0]
    rows_halved = inputs.shape[1]
    local_rows = rows_halved * tensors
    seq_rows = local_rows * contexts
    heads_here = query_weight.shape[2] // HEAD_SIZE
    units_here = down_weight.shape[1]
    key_columns = KEY_VALUE_HEADS * HEAD_SIZE
    rows_per_block = min(512, seq_rows)
    number_of_blocks = seq_rows // rows_per_block
    scale_query = HEAD_SIZE ** (-0.5)
    query_group_width = QUERY_HEADS // KEY_VALUE_HEADS
    head_numbers = tensor_id * heads_here + jnp.arange(heads_here)
    head_picker = head_numbers[:, None] // query_group_width == jnp.arange(KEY_VALUE_HEADS)[None, :]
    select_low = head_picker.astype(jnp.bfloat16)
    select_wide = head_picker.astype(jnp.float32)
    row_half = jnp.arange(rows_halved)
    row_local = jnp.arange(local_rows)
    within_seq = jnp.arange(tensors)[:, None, None] * rows_halved + row_half[None, None, :]

    def gather_rows(values):
        return lax.all_gather(values, "tensor", axis=0, tiled=True)

    def scatter_rows(values):
        return lax.psum_scatter(
            values.astype(jnp.bfloat16), "tensor", scatter_dimension=0, tiled=True
        ).astype(jnp.float32)

    def expand(block_part):
        return jnp.einsum(
            "khd,gh->kgd", block_part, select_low, preferred_element_type=jnp.float32
        ).astype(jnp.bfloat16)

    def block_scores(query_low, block_kv, pos_block, query_pos):
        keys_here = expand(block_kv[:, 0])
        scores = jnp.einsum(
            "qgd,kgd->gqk", query_low, keys_here, preferred_element_type=jnp.float32
        )
        allowed = pos_block[None, :] <= query_pos[:, None]
        return (jnp.where(allowed[None], scores, -jnp.inf), keys_here)

    def split_blocks(key_value_gathered, key_pos):
        return (
            key_value_gathered.reshape(
                number_of_blocks, rows_per_block, 2, KEY_VALUE_HEADS, HEAD_SIZE
            ),
            key_pos.reshape(number_of_blocks, rows_per_block),
        )

    def layer_backward(upstream, kept_state, weights):
        (
            attn_unit,
            attn_inv,
            normed_own,
            normed_all,
            query_unit,
            query_inv,
            query_low,
            key_unit,
            key_inv,
            key_value_gathered,
            log_mass,
            mixture,
            mixture_low,
            ffn_unit,
            ffn_inv,
            second_all,
            gateup,
            hidden_low,
            query_cos,
            query_sin,
            own_cos,
            own_sin,
            query_pos,
            key_pos,
        ) = kept_state
        query_full, out_full, gateup_full, down_full, keyval_full, gains_full = weights
        attn_gain = gains_full[:MODEL_WIDTH]
        ffn_gain = gains_full[MODEL_WIDTH : 2 * MODEL_WIDTH]
        query_gain = gains_full[2 * MODEL_WIDTH : 2 * MODEL_WIDTH + HEAD_SIZE]
        key_gain = gains_full[2 * MODEL_WIDTH + HEAD_SIZE :]
        down_all = gather_rows(upstream.astype(jnp.bfloat16))
        hidden_grad = jnp.dot(down_all, down_full.T, preferred_element_type=jnp.float32)
        gate_values = gateup[:, :units_here]
        up_values = gateup[:, units_here:]
        sigmoid_gate = jax.nn.sigmoid(gate_values)
        gate_grad = (
            hidden_grad * up_values * (sigmoid_gate * (1.0 + gate_values * (1.0 - sigmoid_gate)))
        )
        up_grad = hidden_grad * jax.nn.silu(gate_values)
        gateup_low = jnp.concatenate([gate_grad, up_grad], axis=1).astype(jnp.bfloat16)
        normed_grad = scatter_rows(
            jnp.dot(gateup_low, gateup_full.T, preferred_element_type=jnp.float32)
        )
        residual_part, ffn_gain_grad = norm_back(normed_grad, ffn_unit, ffn_inv, ffn_gain)
        middle = upstream + residual_part
        middle_all = gather_rows(middle.astype(jnp.bfloat16))
        mixture_grad = jnp.dot(middle_all, out_full.T, preferred_element_type=jnp.float32)
        mixture_grad_low = mixture_grad.astype(jnp.bfloat16).reshape(
            local_rows, heads_here, HEAD_SIZE
        )
        offsets = jnp.sum(mixture_grad_low.astype(jnp.float32) * mixture, axis=-1).T
        blocks, pos_blocks = split_blocks(key_value_gathered, key_pos)

        def grad_step(query_grad, packed):
            scores, keys_here = block_scores(query_low, packed[0], packed[1], query_pos)
            weights_full = jnp.exp(scores - log_mass[..., None])
            weights_low = weights_full.astype(jnp.bfloat16)
            values_here = expand(packed[0][:, 1])
            weight_grad = jnp.einsum(
                "qgd,kgd->gqk", mixture_grad_low, values_here, preferred_element_type=jnp.float32
            )
            score_low = (weights_full * (weight_grad - offsets[..., None])).astype(jnp.bfloat16)
            query_grad = query_grad + jnp.einsum(
                "gqk,kgd->qgd", score_low, keys_here, preferred_element_type=jnp.float32
            )
            key_grad = jnp.einsum(
                "gqk,qgd->kgd", score_low, query_low, preferred_element_type=jnp.float32
            )
            value_grad = jnp.einsum(
                "gqk,qgd->kgd", weights_low, mixture_grad_low, preferred_element_type=jnp.float32
            )
            pair_rows = jnp.stack(
                [
                    jnp.einsum("kgd,gh->khd", key_grad, select_wide),
                    jnp.einsum("kgd,gh->khd", value_grad, select_wide),
                ],
                axis=1,
            )
            return (query_grad, pair_rows.reshape(rows_per_block, 2 * key_columns))

        query_grad, pair_blocks = lax.scan(
            grad_step,
            jnp.zeros((local_rows, heads_here, HEAD_SIZE), jnp.float32),
            (blocks, pos_blocks),
        )
        key_value_gradient = lax.psum_scatter(
            pair_blocks.reshape(seq_rows, 2 * key_columns),
            ("tensor", "ctx"),
            scatter_dimension=0,
            tiled=True,
        )
        rotated_key_gradient = key_value_gradient[:, :key_columns].reshape(
            rows_halved, KEY_VALUE_HEADS, HEAD_SIZE
        )
        key_raw_grad, key_gain_grad = norm_back(
            rope_back(rotated_key_gradient, own_cos, own_sin), key_unit, key_inv, key_gain
        )
        keyval_low = jnp.concatenate(
            [key_raw_grad.reshape(rows_halved, key_columns), key_value_gradient[:, key_columns:]],
            axis=1,
        ).astype(jnp.bfloat16)
        own_grad = jnp.dot(keyval_low, keyval_full.T, preferred_element_type=jnp.float32)
        query_raw_grad, query_gain_grad = norm_back(
            rope_back(query_grad * scale_query, query_cos, query_sin),
            query_unit,
            query_inv,
            query_gain,
        )
        query_grad_low = query_raw_grad.reshape(local_rows, heads_here * HEAD_SIZE).astype(
            jnp.bfloat16
        )
        normed_grad = (
            scatter_rows(jnp.dot(query_grad_low, query_full.T, preferred_element_type=jnp.float32))
            + own_grad
        )
        residual_part, attn_gain_grad = norm_back(normed_grad, attn_unit, attn_inv, attn_gain)
        gain_grad = jnp.concatenate([attn_gain_grad, ffn_gain_grad, query_gain_grad, key_gain_grad])
        pieces = (
            hidden_low,
            down_all,
            second_all,
            gateup_low,
            mixture_low,
            middle_all,
            normed_all,
            query_grad_low,
            normed_own,
            keyval_low,
            gain_grad,
        )
        return (middle + residual_part, pieces)

    step_count = batches + sections - 1
    query_full = lax.all_gather(query_weight[0], "ctx", axis=0, tiled=True)
    out_full = lax.all_gather(out_weight[0], "ctx", axis=1, tiled=True)
    gateup_full = lax.all_gather(gateup_weight[0], "ctx", axis=0, tiled=True)
    down_full = lax.all_gather(down_weight[0], "ctx", axis=1, tiled=True)
    keyval_full = lax.all_gather(key_value_matrix[0], ("tensor", "ctx"), axis=0, tiled=True)
    gains_full = lax.all_gather(norm_gains[0], ("tensor", "ctx"), axis=0, tiled=True)
    weights_now = (
        query_full,
        out_full,
        gateup_full.reshape(MODEL_WIDTH, 2 * units_here),
        down_full,
        keyval_full,
        gains_full.astype(jnp.float32),
    )
    received = jnp.zeros_like(inputs[0])
    produced = []
    kept_all = []
    for step_index in range(step_count):
        batch_index = jnp.clip(step_index - section_id, 0, batches - 1)
        first_in = inputs[min(step_index, batches - 1)]
        residual = jnp.where(section_id == 0, first_in, received).astype(jnp.float32)
        layer_residual = residual
        (
            layer_query_full,
            layer_out_full,
            layer_gateup_full,
            layer_down_full,
            layer_keyval_full,
            layer_gains_full,
        ) = weights_now
        layer_attn_gain = layer_gains_full[:MODEL_WIDTH]
        layer_ffn_gain = layer_gains_full[MODEL_WIDTH : 2 * MODEL_WIDTH]
        layer_query_gain = layer_gains_full[2 * MODEL_WIDTH : 2 * MODEL_WIDTH + HEAD_SIZE]
        layer_key_gain = layer_gains_full[2 * MODEL_WIDTH + HEAD_SIZE :]
        slot_row = jnp.sum(
            jnp.where(jnp.arange(batches)[:, None] == batch_index, slot_order, 0), axis=0
        )
        own_slot = jnp.sum(jnp.where(jnp.arange(contexts) == context_id, slot_row, 0))
        positions_query_pos = own_slot * local_rows + row_local
        positions_key_pos = (slot_row[None, :, None] * local_rows + within_seq).reshape(seq_rows)
        own_pos = own_slot * local_rows + tensor_id * rows_halved + row_half
        layer_query_cos, layer_query_sin = rope_tables(positions_query_pos, HEAD_SIZE)
        layer_own_cos, layer_own_sin = rope_tables(own_pos, HEAD_SIZE)
        normed, layer_attn_unit, layer_attn_inv = norm_parts(layer_residual, layer_attn_gain)
        layer_normed_own = normed.astype(jnp.bfloat16)
        layer_normed_all = gather_rows(layer_normed_own)
        query_raw = jnp.dot(
            layer_normed_all, layer_query_full, preferred_element_type=jnp.float32
        ).reshape(local_rows, heads_here, HEAD_SIZE)
        query_hat, layer_query_unit, layer_query_inv = norm_parts(query_raw, layer_query_gain)
        layer_query_low = (
            rope_apply(query_hat, layer_query_cos, layer_query_sin) * scale_query
        ).astype(jnp.bfloat16)
        key_value_projected = jnp.dot(
            layer_normed_own, layer_keyval_full, preferred_element_type=jnp.float32
        )
        key_hat, layer_key_unit, layer_key_inv = norm_parts(
            key_value_projected[:, :key_columns].reshape(rows_halved, KEY_VALUE_HEADS, HEAD_SIZE),
            layer_key_gain,
        )
        key_low = (
            rope_apply(key_hat, layer_own_cos, layer_own_sin)
            .astype(jnp.bfloat16)
            .reshape(rows_halved, key_columns)
        )
        keyval_own = jnp.concatenate(
            [key_low, key_value_projected[:, key_columns:].astype(jnp.bfloat16)], axis=1
        )
        layer_key_value_gathered = lax.all_gather(keyval_own, ("tensor", "ctx"), axis=0, tiled=True)
        attend_query_low = layer_query_low
        attend_query_pos = positions_query_pos
        attend_blocks, attend_pos_blocks = split_blocks(layer_key_value_gathered, positions_key_pos)

        def peak_step(carry, packed):
            old_peak, mass_sum = carry
            scores, unused = block_scores(attend_query_low, packed[0], packed[1], attend_query_pos)
            new_peak = jnp.maximum(old_peak, jnp.max(scores, axis=-1))
            mass_sum = mass_sum * jnp.exp(old_peak - new_peak) + jnp.sum(
                jnp.exp(scores - new_peak[..., None]), axis=-1
            )
            return ((new_peak, mass_sum), None)

        initial = (
            jnp.full((heads_here, local_rows), START_PEAK, jnp.float32),
            jnp.zeros((heads_here, local_rows), jnp.float32),
        )
        (peak_value, mass_sum), unused = lax.scan(
            peak_step, initial, (attend_blocks, attend_pos_blocks)
        )
        attend_log_mass = peak_value + jnp.log(mass_sum)

        def value_step(running, packed):
            scores, unused = block_scores(attend_query_low, packed[0], packed[1], attend_query_pos)
            weights_low = jnp.exp(scores - attend_log_mass[..., None]).astype(jnp.bfloat16)
            values_here = expand(packed[0][:, 1])
            return (
                running
                + jnp.einsum(
                    "gqk,kgd->qgd", weights_low, values_here, preferred_element_type=jnp.float32
                ),
                None,
            )

        attend_mixture, unused = lax.scan(
            value_step,
            jnp.zeros((local_rows, heads_here, HEAD_SIZE), jnp.float32),
            (attend_blocks, attend_pos_blocks),
        )
        layer_mixture_low = attend_mixture.reshape(local_rows, heads_here * HEAD_SIZE).astype(
            jnp.bfloat16
        )
        layer_residual = layer_residual + scatter_rows(
            jnp.dot(layer_mixture_low, layer_out_full, preferred_element_type=jnp.float32)
        )
        normed, layer_ffn_unit, layer_ffn_inv = norm_parts(layer_residual, layer_ffn_gain)
        layer_second_all = gather_rows(normed.astype(jnp.bfloat16))
        layer_gateup = jnp.dot(
            layer_second_all, layer_gateup_full, preferred_element_type=jnp.float32
        )
        layer_hidden_low = (
            jax.nn.silu(layer_gateup[:, :units_here]) * layer_gateup[:, units_here:]
        ).astype(jnp.bfloat16)
        result = layer_residual + scatter_rows(
            jnp.dot(layer_hidden_low, layer_down_full, preferred_element_type=jnp.float32)
        )
        layer_kept_state = (
            layer_attn_unit,
            layer_attn_inv,
            layer_normed_own,
            layer_normed_all,
            layer_query_unit,
            layer_query_inv,
            layer_query_low,
            layer_key_unit,
            layer_key_inv,
            layer_key_value_gathered,
            attend_log_mass,
            attend_mixture,
            layer_mixture_low,
            layer_ffn_unit,
            layer_ffn_inv,
            layer_second_all,
            layer_gateup,
            layer_hidden_low,
            layer_query_cos,
            layer_query_sin,
            layer_own_cos,
            layer_own_sin,
            positions_query_pos,
            positions_key_pos,
        )
        result, kept_state = (result, layer_kept_state)
        result_low = result.astype(jnp.bfloat16)
        produced.append(result_low)
        kept_all.append(kept_state)
        if step_index + 1 < step_count:
            received = from_behind(result_low, "section", 1)
    kept_stack = jax.tree.map(lambda *parts: jnp.stack(parts), *kept_all)
    produced_stack = jnp.stack(produced)
    returned = jnp.zeros_like(inputs[0])
    consumed = []
    pieces_all = []
    for step_index in range(step_count):
        source = jnp.clip(step_index - (sections - 1) + 2 * section_id, 0, step_count - 1)
        kept_state = jax.tree.map(
            lambda stacked: lax.dynamic_index_in_dim(stacked, source, 0, keepdims=False), kept_stack
        )
        live_factor = 1.0 if step_index < batches else 0.0
        top_grad = cotangent[min(step_index, batches - 1)].astype(jnp.float32) * live_factor
        upstream = jnp.where(section_id == sections - 1, top_grad, returned.astype(jnp.float32))
        grad_input, pieces = layer_backward(upstream, kept_state, weights_now)
        pieces_all.append(pieces)
        grad_low = grad_input.astype(jnp.bfloat16)
        consumed.append(grad_low)
        if step_index + 1 < step_count:
            returned = from_behind(grad_low, "section", -1)
    full_set = grads_from(pieces_all)
    consumed_stack = jnp.stack(consumed)
    section_result = jnp.stack(
        [
            lax.dynamic_index_in_dim(produced_stack, batch_no + section_id, 0, keepdims=False)
            for batch_no in range(batches)
        ]
    )[None]
    input_result = jnp.stack(
        [
            lax.dynamic_index_in_dim(
                consumed_stack, batch_no + sections - 1 - section_id, 0, keepdims=False
            )
            for batch_no in range(batches)
        ]
    )[None]
    return (
        section_result,
        input_result,
        lax.psum_scatter(
            full_set[0].astype(jnp.bfloat16), "ctx", scatter_dimension=0, tiled=True
        ).astype(jnp.float32)[None],
        lax.psum_scatter(full_set[4], ("tensor", "ctx"), scatter_dimension=0, tiled=True)[None],
        lax.psum_scatter(
            full_set[1].astype(jnp.bfloat16), "ctx", scatter_dimension=1, tiled=True
        ).astype(jnp.float32)[None],
        lax.psum_scatter(
            full_set[2].reshape(MODEL_WIDTH, 2, units_here).astype(jnp.bfloat16),
            "ctx",
            scatter_dimension=0,
            tiled=True,
        ).astype(jnp.float32)[None],
        lax.psum_scatter(
            full_set[3].astype(jnp.bfloat16), "ctx", scatter_dimension=1, tiled=True
        ).astype(jnp.float32)[None],
        lax.psum_scatter(full_set[5], ("tensor", "ctx"), scatter_dimension=0, tiled=True)[None],
    )


C_BIT, X_BIT, Y_BIT, Z_BIT = 1, 2, 4, 8
MESH_ID = pl.DeviceIdType.MESH
F32 = jnp.float32
BF16 = jnp.bfloat16
GROUP = QUERY_HEADS // KEY_VALUE_HEADS
KEY_COLUMNS = KEY_VALUE_HEADS * HEAD_SIZE
QUERY_COLUMNS = QUERY_HEADS * HEAD_SIZE
HALF_COLUMNS = QUERY_COLUMNS // 2
SCALE = HEAD_SIZE ** (-0.5)
VMEM_BYTES = 62 * 2**20
CYCLES = ((X_BIT, Y_BIT, Z_BIT), (Y_BIT, Z_BIT, X_BIT), (Z_BIT, X_BIT, Y_BIT))
TOWARD_Z = ((X_BIT, Y_BIT, Z_BIT), (Y_BIT, X_BIT, Z_BIT))
ROW_WIDTHS = (768, 640, 640)
KV_WIDTHS = (256, 256, 128)
class Place:
    def __init__(self):
        self.section = lax.axis_index("section")
        ctx = lax.axis_index("ctx")
        self.bits = (ctx % 2, (ctx // 2) % 2, ctx // 4, lax.axis_index("tensor"))

    def flipped(self, mask):
        return [1 - bit if mask & (1 << i) else bit for i, bit in enumerate(self.bits)]

    def block(self, mask=0):
        core, x, y, z = self.flipped(mask)
        return z * 8 + y * 4 + x * 2 + core

    def chip(self, mask=0):
        _, x, y, z = self.flipped(mask)
        return z * 4 + y * 2 + x

    def ctx(self, mask=0):
        core, x, y, _ = self.flipped(mask)
        return y * 4 + x * 2 + core

    def peer(self, mask):
        core, x, y, z = self.flipped(mask)
        return (self.section, z, y * 4 + x * 2 + core)

    def other_section(self, section):
        core, x, y, z = self.bits
        return (section, z, y * 4 + x * 2 + core)


def remote(src, dst, send, recv, device):
    return pltpu.make_async_remote_copy(
        src_ref=src, dst_ref=dst, send_sem=send, recv_sem=recv, device_id=device, device_id_type=MESH_ID
    )


def load(src, dst, sem):
    copy = pltpu.make_async_copy(src, dst, sem)
    copy.start()
    return copy


def landed(ref, sem):
    pltpu.make_async_copy(ref, ref, sem).wait()


def greet(place, masks, into=None):
    barrier = pltpu.get_barrier_semaphore()
    for mask in masks:
        pl.semaphore_signal(barrier, inc=1, device_id=place.peer(mask), device_id_type=MESH_ID)
    if into is None:
        pl.semaphore_wait(barrier, len(masks))
        return
    if into == "both":
        pl.semaphore_signal(
            barrier, inc=1, device_id=place.other_section(1 - place.section), device_id_type=MESH_ID
        )
        pl.semaphore_wait(barrier, len(masks) + 1)
        return

    @pl.when(place.section == into)
    def _():
        pl.semaphore_signal(barrier, inc=1, device_id=place.other_section(1 - into), device_id_type=MESH_ID)
        pl.semaphore_wait(barrier, len(masks))

    @pl.when(place.section != into)
    def _():
        pl.semaphore_wait(barrier, len(masks) + 1)


def column_pieces(widths, orders):
    start, pieces = 0, []
    for width, order in zip(widths, orders):
        pieces.append(((slice(None), pl.ds(start, width)), order))
        start += width
    return pieces


def row_pieces(heights, orders):
    start, pieces = 0, []
    for height, order in zip(heights, orders):
        pieces.append(((pl.ds(start, height), slice(None)), order))
        start += height
    return pieces


def halves(rows):
    return row_pieces((rows // 2, rows // 2), TOWARD_Z)


class Gather:
    def __init__(self, place, buf, pieces, sems, siblings):
        self.place, self.buf, self.pieces, self.siblings = place, buf, list(enumerate(pieces)), siblings
        self.send, self.recv = sems

    def _where(self, piece, mask):
        block = self.place.block(mask) if self.siblings else self.place.chip(mask)
        return self.buf.at[(block,) + self.pieces[piece][1][0]]

    def _copy(self, piece, mask, dim):
        where = self._where(piece, mask)
        return remote(where, where, self.send, self.recv.at[self._slot(piece, mask ^ dim)], self.place.peer(dim))

    def _slot(self, piece, mask):
        return piece * 15 + mask - 1 if self.siblings else piece * 7 + mask // 2 - 1

    def _start(self, piece, mask, dim):
        self._copy(piece, mask, dim).start()

    def _arrived(self, piece, mask, dim):
        where = self._where(piece, mask)
        remote(where, where, self.send, self.recv.at[self._slot(piece, mask)], self.place.peer(dim)).wait_recv()

    def _pass(self, piece, mask, dims):
        for dim in dims:
            self._start(piece, mask, dim)
        if self.siblings:
            self._start(piece, mask, C_BIT)

    def start(self):
        for turn in range(3):
            for piece, (_, order) in self.pieces:
                self._start(piece, 0, order[turn])
        if self.siblings:
            for piece, _ in self.pieces:
                self._start(piece, 0, C_BIT)

    def first(self):
        for piece, (_, (d0, d1, d2)) in self.pieces:
            self._arrived(piece, d0, d0)
            self._pass(piece, d0, (d1, d2))

    def second(self):
        for part in (0, 1):
            for piece, (_, (d0, d1, d2)) in self.pieces:
                mask = (d1, d0 ^ d1)[part]
                self._arrived(piece, mask, d1)
                self._pass(piece, mask, (d2,))

    def third(self):
        for part in (0, 1, 2, 3):
            for piece, (_, (d0, d1, d2)) in self.pieces:
                mask = (d2, d0 ^ d2, d1 ^ d2, d0 ^ d1 ^ d2)[part]
                self._arrived(piece, mask, d2)
                self._pass(piece, mask, ())

    def last(self):
        if self.siblings:
            for piece, _ in self.pieces:
                for mask in range(0, 16, 2):
                    self._arrived(piece, mask ^ C_BIT, C_BIT)

    def finish(self):
        self.first()
        self.second()
        self.third()
        self.last()

    def drain(self):
        landed(self.buf.at[pl.ds(0, 15 if self.siblings else 7)], self.send)


class Scatter:
    def __init__(self, place, part, land, pieces, sems, put, sib_land=None):
        self.place, self.part, self.land, self.sib_land = place, part, land, sib_land
        self.pieces, self.put = list(enumerate(pieces)), put
        self.send, self.recv = sems

    def _block(self, mask):
        return self.place.chip(mask) if self.sib_land is None else self.place.block(mask)

    def _sib(self, i, mask):
        return remote(
            self.part.at[self.place.block(mask | C_BIT)],
            self.sib_land.at[i],
            self.send,
            self.recv.at[len(self.pieces) * 7 + i],
            self.place.peer(C_BIT),
        )

    def siblings(self):
        masks = (14, 12, 10, 6, 8, 4, 2, 0)
        for i, mask in enumerate(masks):
            self._sib(i, mask).start()
        for i, mask in enumerate(masks):
            self._sib(i, mask).wait_recv()
            block = self.place.block(mask)
            self.part[block] = (self.part[block].astype(F32) + self.sib_land[i].astype(F32)).astype(BF16)

    def _copy(self, piece, mask, dim):
        index = self.pieces[piece][1][0]
        return remote(
            self.part.at[(self._block(mask),) + index],
            self.land.at[(mask // 2 - 1,) + index],
            self.send,
            self.recv.at[piece * 7 + mask // 2 - 1],
            self.place.peer(dim),
        )

    def _start(self, piece, mask, dim):
        self._copy(piece, mask, dim).start()

    def _sum(self, piece, mask, dim):
        self._copy(piece, mask, dim).wait_recv()
        index = self.pieces[piece][1][0]
        at = (self._block(mask ^ dim),) + index
        return at, self.part[at].astype(F32) + self.land[(mask // 2 - 1,) + index].astype(F32)

    def _add(self, piece, mask, dim):
        at, total = self._sum(piece, mask, dim)
        self.part[at] = total.astype(BF16)

    def start(self, ready=range(16), pieces=None):
        for part in (0, 1, 2, 3):
            for piece, (_, (d0, d1, d2)) in self.pieces if pieces is None else [self.pieces[i] for i in pieces]:
                mask = (d0 ^ d1 ^ d2, d1 ^ d2, d0 ^ d2, d2)[part]
                if mask in ready:
                    self._start(piece, mask, d2)

    def second(self):
        for part in (0, 1):
            for piece, (_, (d0, d1, d2)) in self.pieces:
                mask = (d0 ^ d1, d1)[part]
                self._add(piece, mask ^ d2, d2)
                self._start(piece, mask, d1)
        for piece, (_, (d0, d1, d2)) in self.pieces:
            self._add(piece, d0 ^ d2, d2)

    def third(self):
        for piece, (_, (d0, d1, d2)) in self.pieces:
            self._add(piece, d0 ^ d1, d1)
            self._start(piece, d0, d0)
        for piece, (_, (d0, d1, d2)) in self.pieces:
            self._add(piece, d2, d2)
        for piece, (_, (d0, d1, d2)) in self.pieces:
            self._add(piece, d1, d1)

    def last(self):
        for piece, (index, (d0, d1, d2)) in self.pieces:
            _, total = self._sum(piece, d0, d0)
            self.put(index, total)

    def finish(self):
        self.second()
        self.third()
        self.last()

    def drain(self):
        landed(self.part.at[pl.ds(0, 7 if self.sib_land is None else 15)], self.send)


def sems(count):
    return [pltpu.SemaphoreType.DMA((count,)), pltpu.SemaphoreType.DMA((count,))]


def pair(count):
    return [pltpu.SemaphoreType.DMA, pltpu.SemaphoreType.DMA((count,))]


class Refs(dict):
    __getattr__ = dict.__getitem__


class Out(typing.NamedTuple):
    shape: tuple
    dtype: typing.Any
    far: bool


class In(typing.NamedTuple):
    array: typing.Any
    far: bool


def named(tree):
    if isinstance(tree, dict):
        return Refs({name: named(value) for name, value in tree.items()})
    return [named(value) for value in tree] if isinstance(tree, list) else tree


def near(**arrays):
    return {name: In(array, False) for name, array in arrays.items()}


def far(**arrays):
    return {name: In(array, True) for name, array in arrays.items()}


def run(body, collective, inputs, outputs, scratch):
    def is_leaf(value):
        return not isinstance(value, (dict, list))

    trees = [jax.tree.flatten(tree, is_leaf=is_leaf) for tree in (inputs, outputs, scratch)]
    (given, made, held) = [leaves for leaves, _ in trees]

    def kernel(*refs):
        parts, start = [], 0
        for leaves, tree in trees:
            parts.append(named(jax.tree.unflatten(tree, refs[start : start + len(leaves)])))
            start += len(leaves)
        body(*parts)

    def specs(leaves):
        return [pl.BlockSpec(memory_space=pl.ANY if leaf.far else pltpu.VMEM) for leaf in leaves]

    results = pl.pallas_call(
        kernel,
        out_shape=tuple(jax.ShapeDtypeStruct(leaf.shape, leaf.dtype) for leaf in made),
        in_specs=specs(given),
        out_specs=tuple(specs(made)),
        scratch_shapes=held,
        compiler_params=pltpu.CompilerParams(
            collective_id=collective, has_side_effects=True, vmem_limit_bytes=VMEM_BYTES
        ),
    )(*[leaf.array for leaf in given])
    return jax.tree.unflatten(trees[1][1], results)


def dot(left, right):
    return lax.dot_general(left, right, (((1,), (0,)), ((), ())), preferred_element_type=F32)


def dot_nt(left, right):
    return lax.dot_general(left, right, (((1,), (1,)), ((), ())), preferred_element_type=F32)


def dot_tn(left, right):
    return lax.dot_general(left, right, (((0,), (0,)), ((), ())), preferred_element_type=F32)


def unit_rows(values):
    inverse = lax.rsqrt(jnp.mean(values * values, axis=-1, keepdims=True) + EPSILON)
    return values * inverse, inverse


def unit_back(scaled, unit, inverse):
    return inverse * (scaled - unit * jnp.mean(scaled * unit, axis=-1, keepdims=True))


def stack_heads(values, heads):
    return jnp.concatenate([values[:, h * HEAD_SIZE : (h + 1) * HEAD_SIZE] for h in range(heads)], axis=0)


def spread_heads(values, heads):
    rows = values.shape[0] // heads
    return jnp.concatenate([values[h * rows : (h + 1) * rows] for h in range(heads)], axis=1)


def turned(values):
    half = HEAD_SIZE // 2
    return jnp.concatenate([values[:, half:], values[:, :half]], axis=1)


def tall(rows, times):
    return jnp.concatenate([rows] * times, axis=0)


def rope(values, cos, sin, heads):
    return values * tall(cos, heads) + turned(values) * tall(sin, heads)


def unrope(values, cos, sin, heads):
    return values * tall(cos, heads) - turned(values) * tall(sin, heads)


def mask_bias(m, r, bias):
    bias[...] = jnp.where(r.postab[m, 0:1, :] <= r.rowtab[m, :, 2 * HEAD_SIZE : 2 * HEAD_SIZE + 1], 0.0, -jnp.inf)


def split_keys(kv, k5, v5):
    rows = kv.shape[0] * kv.shape[1]
    for g in range(KEY_VALUE_HEADS):
        k5[g] = kv[:, :, g * HEAD_SIZE : (g + 1) * HEAD_SIZE].reshape(rows, HEAD_SIZE)
        v5[g] = kv[:, :, KEY_COLUMNS + g * HEAD_SIZE : KEY_COLUMNS + (g + 1) * HEAD_SIZE].reshape(rows, HEAD_SIZE)


def probabilities(queries, keys, bias):
    scores = dot_nt(queries, keys) + tall(bias, GROUP)
    raised = jnp.exp(scores - jnp.max(scores, axis=-1, keepdims=True))
    return raised / jnp.sum(raised, axis=-1, keepdims=True)


def gain_parts(r, width):
    return (
        r.gains[:, :width],
        r.gains[:, width : 2 * width],
        r.gains[:, 2 * width : 2 * width + HEAD_SIZE],
        r.gains[:, 2 * width + HEAD_SIZE :],
    )


class Courier:
    def __init__(self, place, source, target, pair, into):
        self.place, self.into = place, into
        self.copy = remote(source, target, pair[0], pair[1], place.other_section(into))

    def start(self):
        @pl.when(self.place.section != self.into)
        def _():
            self.copy.start()

    def arrive(self):
        @pl.when(self.place.section == self.into)
        def _():
            self.copy.wait_recv()

    def leave(self):
        @pl.when(self.place.section != self.into)
        def _():
            self.copy.wait_send()


BLOCKS = 8
KEY_PADDED = -(-KEY_COLUMNS // 128) * 128


def unit_blocks(units):
    return [pl.ds(half * (units // 2), units // 2) for half in (0, 1)]


def column_blocks(width):
    return [pl.ds(part * (width // 4), width // 4) for part in range(4)]


def forward_kept(rows, width, units):
    tokens = BLOCKS * rows
    return dict(
        u=Out((rows, width), BF16, True),
        h=Out((rows, width), F32, True),
        qraw=Out((rows, QUERY_COLUMNS), F32, True),
        kraw=Out((rows, KEY_PADDED), F32, True),
        q=Out((rows, QUERY_COLUMNS), BF16, True),
        kv=Out((2 * BLOCKS, rows, 2 * KEY_COLUMNS), BF16, True),
        gu=Out((2 * units, tokens), F32, True),
        ob=Out((rows, QUERY_COLUMNS), BF16, True),
        e=Out((BLOCKS, rows, width), BF16, True),
        hid=Out((units, tokens), BF16, True),
    )


def held_like(outs):
    return {name: pltpu.VMEM(out.shape, out.dtype) for name, out in outs.items()}


def forward_scratch(rows, width, units):
    return held_like(forward_kept(rows, width, units)) | dict(
        q5=pltpu.VMEM((KEY_VALUE_HEADS, GROUP * rows, HEAD_SIZE), BF16),
        part=pltpu.VMEM((BLOCKS, rows, width), BF16),
        land=pltpu.VMEM((BLOCKS - 1, rows, width), BF16),
        kv_sems=pair(45),
        e_sems=pair(21),
        y_sems=pair(21),
        keep=pltpu.SemaphoreType.DMA((10,)),
    )


def forward_steps(r, place, m, need):
    rows, width = r.u.shape
    units = r.hid.shape[0]
    attn_gain, ffn_gain, q_gain, k_gain = gain_parts(r, width)
    cos, sin = r.rowtab[m, :, :HEAD_SIZE], r.rowtab[m, :, HEAD_SIZE : 2 * HEAD_SIZE]
    saves = []

    def keep(name):
        saves.append(load(r[name], r.kept[name], r.keep.at[len(saves)]))

    r.u[...] = r.inputs[m] if r.received is None else jnp.where(place.section == 0, r.inputs[m], r.received[...])
    keep("u")
    a = (unit_rows(r.u[...].astype(F32))[0] * attn_gain).astype(BF16)
    need("keyval")
    kv_raw = dot(a, r.w.keyval[...].reshape(width, 2 * KEY_COLUMNS))
    r.kraw[...] = kv_raw[:, :KEY_PADDED]
    k_raw = stack_heads(kv_raw[:, :KEY_COLUMNS], KEY_VALUE_HEADS)
    k_low = rope(unit_rows(k_raw)[0] * k_gain, cos, sin, KEY_VALUE_HEADS).astype(BF16)
    r.kv[place.block()] = jnp.concatenate(
        [spread_heads(k_low, KEY_VALUE_HEADS), kv_raw[:, KEY_COLUMNS:].astype(BF16)], axis=1
    )
    kv_gather = Gather(place, r.kv, column_pieces(KV_WIDTHS, CYCLES), r.kv_sems, True)
    kv_gather.start()
    keep("kraw")
    need("query")
    q_raw = jnp.concatenate([dot(a, r.w.query[8 * t : 8 * t + 8].reshape(width, HALF_COLUMNS)) for t in range(2)], axis=1)
    r.qraw[...] = q_raw
    keep("qraw")
    q_unit = unit_rows(stack_heads(q_raw, QUERY_HEADS))[0]
    q_low = (rope(q_unit * q_gain, cos, sin, QUERY_HEADS) * SCALE).astype(BF16)
    r.q5[...] = q_low.reshape(KEY_VALUE_HEADS, GROUP * rows, HEAD_SIZE)
    r.q[...] = spread_heads(q_low, QUERY_HEADS)
    keep("q")
    yield
    kv_gather.first()
    yield
    kv_gather.second()
    yield
    kv_gather.third()
    kv_gather.last()
    keep("kv")

    def attention(k5, v5, o5, bias):
        mask_bias(m, r, bias)
        split_keys(r.kv, k5, v5)

        def attend(g, _):
            low = probabilities(r.q5[g], k5[g], bias[...]).astype(BF16)
            o5[g] = dot(low, v5[g])
            return 0

        lax.fori_loop(0, KEY_VALUE_HEADS, attend, 0)
        r.ob[...] = spread_heads(o5[...].reshape(QUERY_HEADS * rows, HEAD_SIZE), QUERY_HEADS).astype(BF16)

    keys = 2 * BLOCKS * rows
    group = pltpu.VMEM((KEY_VALUE_HEADS, keys, HEAD_SIZE), BF16)
    mixed_heads = pltpu.VMEM((KEY_VALUE_HEADS, GROUP * rows, HEAD_SIZE), F32)
    pl.run_scoped(attention, group, group, mixed_heads, pltpu.VMEM((rows, keys), F32))
    keep("ob")
    need("out")
    for c in range(8):
        block = pl.ds(c * (width // 8), width // 8)
        mixed = dot(r.ob[:, :HALF_COLUMNS], r.w.out[c]) + dot(r.ob[:, HALF_COLUMNS:], r.w.out[8 + c])
        r.h[:, block] = r.u[:, block].astype(F32) + mixed
    keep("h")
    r.e[place.chip()] = (unit_rows(r.h[...])[0] * ffn_gain).astype(BF16)
    e_gather = Gather(place, r.e, column_pieces(ROW_WIDTHS, CYCLES), r.e_sems, False)
    e_gather.start()
    need("ffn")
    yield
    e_gather.first()
    yield
    e_gather.second()
    yield
    e_gather.third()
    keep("e")

    def put(index, total):
        r.result[index] = (r.h[index] + total).astype(BF16)

    scatter = Scatter(place, r.part, r.land, column_pieces(ROW_WIDTHS, CYCLES), r.y_sems, put)
    for flip in (Z_BIT, 0):
        first = place.chip(flip) // 4 * 4
        tokens = pl.ds(pl.multiple_of(first * rows, 4 * rows), 4 * rows)
        here = pl.ds(first, 4)
        for some in unit_blocks(units):
            gate = dot_nt(r.w.ffn[0, some], r.e[here].reshape(4 * rows, width))
            up = dot_nt(r.w.ffn[1, some], r.e[here].reshape(4 * rows, width))
            r.gu[some, tokens] = gate
            r.gu[pl.ds(units + some.start, some.size), tokens] = up
            r.hid[some, tokens] = (gate * jax.nn.sigmoid(gate) * up).astype(BF16)
        for some in column_blocks(width):
            outward = dot_tn(r.hid[:, tokens], r.w.ffn[2, :, some])
            r.part[here, :, some] = outward.astype(BF16).reshape(4, rows, some.size)
        yield
        scatter.start([flip ^ mask for mask in (0, X_BIT, Y_BIT, X_BIT | Y_BIT)])
        yield
    keep("gu")
    keep("hid")
    scatter.second()
    yield
    scatter.third()
    yield
    scatter.last()
    yield "result"
    for gather in (kv_gather, e_gather):
        gather.drain()
    scatter.drain()
    for copy in saves:
        copy.wait()


def take(steps, count):
    for _ in range(count):
        next(steps, None)


def until(steps, what):
    for said in steps:
        if what is not None and said == what:
            return


def backward_kept(rows, width, units):
    tokens = BLOCKS * rows
    return dict(
        df=Out((BLOCKS, rows, width), BF16, True),
        dgu=Out((2 * units, tokens), BF16, True),
        a=Out((rows, width), BF16, True),
        da=Out((rows, width), BF16, True),
        dq=Out((rows, QUERY_COLUMNS), BF16, True),
        dkv=Out((rows, 2 * KEY_COLUMNS), BF16, True),
        gain=Out((1, 2 * width + 2 * HEAD_SIZE), F32, True),
    )


def backward_scratch(rows, width, units):
    past = held_like(forward_kept(rows, width, units))
    return held_like(backward_kept(rows, width, units)) | dict(
        u=past["u"],
        qraw=past["qraw"],
        kraw=past["kraw"],
        q=past["q"],
        dh=pltpu.VMEM((rows, width), F32),
        dx=pltpu.VMEM((rows, width), F32),
        do5=pltpu.VMEM((QUERY_HEADS * rows, HEAD_SIZE), BF16),
        dq5=pltpu.VMEM((QUERY_HEADS * rows, HEAD_SIZE), F32),
        dkv_own=pltpu.VMEM((rows, 2 * KEY_COLUMNS), F32),
        part=pltpu.VMEM((BLOCKS, rows, width), BF16),
        land=pltpu.VMEM((BLOCKS - 1, rows, width), BF16),
        part_kv=pltpu.VMEM((2 * BLOCKS, rows, 2 * KEY_COLUMNS), BF16),
        sib_kv=pltpu.VMEM((BLOCKS, rows, 2 * KEY_COLUMNS), BF16),
        land_kv=pltpu.VMEM((BLOCKS - 1, rows, 2 * KEY_COLUMNS), BF16),
        df_sems=pair(21),
        de_sems=pair(21),
        kv_sems=pair(29),
        held=pltpu.SemaphoreType.DMA((7,)),
    )


class BackwardLayer:
    def __init__(self, r, place, m, need, past, source, kv_pieces=(KV_WIDTHS, CYCLES)):
        self.r, self.place, self.m, self.need, self.kv_pieces = r, place, m, need, kv_pieces
        self.past, self.source = past, source

    def targets(self):
        r = self.r
        return dict(u=r.u, h=r.dh, qraw=r.qraw, kraw=r.kraw, q=r.q, kv=r.part_kv)

    def _fetch(self, targets, start):
        for section, past in enumerate(self.past):
            if past is not None:

                @pl.when(self.place.section == section)
                def _(past=past):
                    for i, (name, target) in enumerate(targets.items()):
                        load(past[name], target, self.r.held.at[start + i])

    def fetch(self):
        self._fetch(self.targets(), 0)

    def fetch_gu(self, gu):
        self._fetch(dict(gu=gu), 6)

    def rows_out(self):
        r, place = self.r, self.place
        first, second = self.source
        if first is None:
            dy = second[...]
        elif second is None:
            dy = first[...]
        else:
            dy = jnp.where(place.section == 0, first[...], second[...])
        r.df[place.chip()] = dy
        self.gather = Gather(place, r.df, column_pieces(ROW_WIDTHS, CYCLES), r.df_sems, False)
        self.gather.start()

        def put(index, total):
            r.dx[index] = total

        self.scatter = Scatter(place, r.get("part"), r.land, column_pieces(ROW_WIDTHS, CYCLES), r.de_sems, put)

    def chunk(self, gu, flip):
        r, place = self.r, self.place
        rows, width = r.u.shape
        units = r.dgu.shape[0] // 2
        first = place.chip(flip) // 4 * 4
        tokens = pl.ds(pl.multiple_of(first * rows, 4 * rows), 4 * rows)
        here = pl.ds(first, 4)
        for some in unit_blocks(units):
            beyond = pl.ds(units + some.start, some.size)
            dhidden = dot_nt(r.w.ffn[2, some], r.df[here].reshape(4 * rows, width))
            gate, up = gu[some, tokens], gu[beyond, tokens]
            shut = jax.nn.sigmoid(gate)
            r.dgu[some, tokens] = (dhidden * up * (shut * (1.0 + gate * (1.0 - shut)))).astype(BF16)
            r.dgu[beyond, tokens] = (dhidden * (gate * shut)).astype(BF16)
        for some in column_blocks(width):
            inward = dot_tn(r.dgu[:, tokens], r.w.ffn[:2, :, some].reshape(2 * units, some.size))
            r.part[here, :, some] = inward.astype(BF16).reshape(4, rows, some.size)

    def send(self, flip):
        self.scatter.start([flip ^ mask for mask in (0, X_BIT, Y_BIT, X_BIT | Y_BIT)])

    def feed_forward(self):
        def inner(gu):
            self.fetch_gu(gu)
            self.need("ffn")
            self.gather.finish()
            landed(gu, self.r.held.at[6])
            for flip in (Z_BIT, 0):
                self.chunk(gu, flip)
                self.send(flip)

        units, tokens = self.r.dgu.shape
        pl.run_scoped(inner, pltpu.VMEM((units, tokens), F32))

    def steps(self, gu):
        self.rows_out()
        yield
        self.gather.first()
        yield
        self.gather.second()
        yield
        self.need("ffn")
        self.gather.third()
        landed(gu, self.r.held.at[6])
        self.chunk(gu, Z_BIT)
        yield
        self.send(Z_BIT)
        yield
        self.chunk(gu, 0)
        yield
        self.send(0)
        yield
        self.scatter.second()
        yield
        self.scatter.third()
        yield
        self.scatter.last()
        self.middle()
        yield
        self.mixture()
        yield
        self.weights()
        yield
        self.key_siblings()
        yield
        self.queries()
        yield
        self.scatter_kv.second()
        yield
        self.scatter_kv.third()
        yield
        self.keys()
        yield "result"

    def middle(self):
        r = self.r
        rows, width = r.u.shape
        ffn_gain = gain_parts(r, width)[1]
        for i, target in enumerate(self.targets().values()):
            landed(target, r.held.at[i])
        unit, inverse = unit_rows(r.dh[...])
        r.gain[:, width : 2 * width] = jnp.sum(r.dx[...] * unit, axis=0, keepdims=True)
        r.dh[...] = r.df[self.place.chip()].astype(F32) + unit_back(r.dx[...] * ffn_gain, unit, inverse)
        r.da[...] = r.dh[...].astype(BF16)
        unit, _ = unit_rows(r.u[...].astype(F32))
        r.a[...] = (unit * gain_parts(r, width)[0]).astype(BF16)

    def attention(self):
        self.mixture()
        self.weights()
        self.key_siblings()

    def mixture(self):
        r = self.r
        rows, width = r.u.shape
        self.need("out")
        heads = QUERY_HEADS // 2
        for t in range(2):
            total = jnp.zeros((rows, HALF_COLUMNS), F32)
            for c in range(8):
                total = total + dot_nt(r.da[:, c * (width // 8) : (c + 1) * (width // 8)], r.w.out[t * 8 + c])
            r.do5[t * heads * rows : (t + 1) * heads * rows] = stack_heads(total.astype(BF16), heads)

    def weights(self):
        r, m = self.r, self.m
        rows = r.u.shape[0]
        keys = 2 * BLOCKS * rows

        def inner(q5, k5, v5, bias):
            mask_bias(m, r, bias)
            q5[...] = stack_heads(r.q[...], QUERY_HEADS).reshape(KEY_VALUE_HEADS, GROUP * rows, HEAD_SIZE)
            split_keys(r.part_kv, k5, v5)

            def attend(g, _):
                at = pl.ds(pl.multiple_of(g * GROUP * rows, GROUP * rows), GROUP * rows)
                weights = probabilities(q5[g], k5[g], bias[...])
                grads = r.do5[at]
                dweights = dot_nt(grads, v5[g])
                mean = jnp.sum(weights * dweights, axis=-1, keepdims=True)
                dscores = (weights * (dweights - mean)).astype(BF16)
                r.dq5[at] = dot(dscores, k5[g])
                k5[g] = dot_tn(dscores, q5[g]).astype(BF16)
                v5[g] = dot_tn(weights.astype(BF16), grads).astype(BF16)
                return 0

            lax.fori_loop(0, KEY_VALUE_HEADS, attend, 0)
            for b in range(2 * BLOCKS):
                at = slice(b * rows, (b + 1) * rows)
                r.part_kv[b] = jnp.concatenate(
                    [k5[g, at] for g in range(KEY_VALUE_HEADS)] + [v5[g, at] for g in range(KEY_VALUE_HEADS)], axis=1
                )

        kind = pltpu.VMEM((KEY_VALUE_HEADS, keys, HEAD_SIZE), BF16)
        grouped = pltpu.VMEM((KEY_VALUE_HEADS, GROUP * rows, HEAD_SIZE), BF16)
        pl.run_scoped(inner, grouped, kind, kind, pltpu.VMEM((rows, keys), F32))

    def key_siblings(self):
        r, place = self.r, self.place

        def put(index, total):
            r.dkv_own[index] = total

        pieces = column_pieces(*self.kv_pieces)
        self.scatter_kv = Scatter(place, r.part_kv, r.land_kv, pieces, r.kv_sems, put, r.sib_kv)
        self.scatter_kv.siblings()
        self.scatter_kv.start()

    def queries(self):
        r, m = self.r, self.m
        width = r.u.shape[1]
        q_gain = gain_parts(r, width)[2]
        cos, sin = r.rowtab[m, :, :HEAD_SIZE], r.rowtab[m, :, HEAD_SIZE : 2 * HEAD_SIZE]
        unit, inverse = unit_rows(stack_heads(r.qraw[...], QUERY_HEADS))
        dhat = unrope(r.dq5[...] * SCALE, cos, sin, QUERY_HEADS)
        r.gain[:, 2 * width : 2 * width + HEAD_SIZE] = jnp.sum(dhat * unit, axis=0, keepdims=True)
        r.dq[...] = spread_heads(unit_back(dhat * q_gain, unit, inverse), QUERY_HEADS).astype(BF16)
        self.need("query")
        r.dx[...] = dot_nt(r.dq[:, :HALF_COLUMNS], r.w.query[:8].reshape(width, HALF_COLUMNS)) + dot_nt(
            r.dq[:, HALF_COLUMNS:], r.w.query[8:].reshape(width, HALF_COLUMNS)
        )

    def key_sums(self):
        self.scatter_kv.second()
        self.scatter_kv.third()

    def keys(self):
        r, m = self.r, self.m
        width = r.u.shape[1]
        attn_gain, _, _, k_gain = gain_parts(r, width)
        cos, sin = r.rowtab[m, :, :HEAD_SIZE], r.rowtab[m, :, HEAD_SIZE : 2 * HEAD_SIZE]
        self.need("keyval")
        self.scatter_kv.last()
        unit, inverse = unit_rows(stack_heads(r.kraw[:, :KEY_COLUMNS], KEY_VALUE_HEADS))
        dhat = unrope(stack_heads(r.dkv_own[:, :KEY_COLUMNS], KEY_VALUE_HEADS), cos, sin, KEY_VALUE_HEADS)
        r.gain[:, 2 * width + HEAD_SIZE :] = jnp.sum(dhat * unit, axis=0, keepdims=True)
        dk_raw = spread_heads(unit_back(dhat * k_gain, unit, inverse), KEY_VALUE_HEADS)
        r.dkv[...] = jnp.concatenate([dk_raw, r.dkv_own[:, KEY_COLUMNS:]], axis=1).astype(BF16)
        r.dx[...] = r.dx[...] + dot_nt(r.dkv[...], r.w.keyval[...].reshape(width, 2 * KEY_COLUMNS))
        unit, inverse = unit_rows(r.u[...].astype(F32))
        r.gain[:, :width] = jnp.sum(r.dx[...] * unit, axis=0, keepdims=True)
        r.grad[...] = (r.dh[...] + unit_back(r.dx[...] * attn_gain, unit, inverse)).astype(BF16)

    def drain(self):
        for sent in (self.gather, self.scatter, self.scatter_kv):
            sent.drain()


WEIGHTS = ("keyval", "query", "out", "ffn")
SCHEDULE = "bbbsbbbbrfbfbfbfbfbfbffbffbbbofff"
NEIGHBOURS = (C_BIT, X_BIT, Y_BIT, Z_BIT)
AWAY = (X_BIT | Y_BIT, X_BIT, Y_BIT)


class Arrival:
    def __init__(self, place, i, s, store):
        self.place, self.i, self.s, self.store = place, i, s, store
        self.columns = i.down.shape[1]
        self.units = s.w.ffn.shape[1]
        own = place.block()
        self.fetched = [
            load(src, dst, s.fetch.at[n])
            for n, (src, dst) in enumerate(
                (
                    (i.gains, s.gains_all.at[own]),
                    (i.keyval, s.w.keyval.at[own]),
                    (i.query, s.w.query.at[own]),
                    (i.out, s.w.out.at[own]),
                    (i.gateup.at[:, self._units(0), :], s.w.ffn.at[pl.ds(0, 2), :, self._columns(0)]),
                    (i.down.at[self._units(0), :], s.w.ffn.at[2, :, self._columns(0)]),
                )
            )
        ]
        self.gains = Gather(place, s.gains_all, row_pieces((16,), TOWARD_Z), s.gains_sems, True)
        self.keyval, self.query, self.out = (
            Gather(place, buf, halves(buf.shape[1]), pair_, True)
            for buf, pair_ in (
                (s.w.keyval, s.keyval_sems),
                (s.w.query, s.query_sems),
                (s.w.out, s.out_sems),
            )
        )

    def _units(self, mask):
        return pl.ds(pl.multiple_of((self.place.chip(mask) % 4) * self.units, self.units), self.units)

    def _columns(self, mask):
        return pl.ds(pl.multiple_of(self.place.ctx(mask) * self.columns, self.columns), self.columns)

    def _spread(self, mask, j):
        i, s, mine = self.i, self.s, self._columns(0)
        src, dst = (
            (i.gateup.at[:, self._units(mask), :], s.w.ffn.at[pl.ds(0, 2), :, mine]),
            (i.down.at[self._units(mask), :], s.w.ffn.at[2, :, mine]),
        )[j]
        return remote(src, dst, s.ffn_send.at[mask + j], s.ffn_recv.at[mask + j], self.place.peer(mask))

    def _came(self, mask, j):
        s, there = self.s, self._columns(mask)
        dst = s.w.ffn.at[2, :, there] if j else s.w.ffn.at[pl.ds(0, 2), :, there]
        remote(dst, dst, s.ffn_send.at[mask + j], s.ffn_recv.at[mask + j], self.place.peer(mask)).wait_recv()

    def _sibling(self, mask, back=0):
        s = self.s
        where = s.w.ffn.at[:, :, self._columns(mask | back)]
        slot = 8 + mask // 2
        return remote(where, where, s.ffn_send.at[slot], s.ffn_recv.at[slot], self.place.peer(C_BIT))

    def spread(self, masks):
        for mask in masks:
            for j in (0, 1):
                self._spread(mask, j).start()

    def begin(self):
        for n, gather in enumerate((self.gains, self.keyval, self.query)):
            self.fetched[n].wait()
            gather.start()
        for n in (3, 4, 5):
            self.fetched[n].wait()
        self._sibling(0).start()
        for gather in (self.gains, self.keyval, self.query):
            gather.first()
        for gather in (self.gains, self.keyval, self.query):
            gather.second()
        self.out.start()
        self.spread((X_BIT | Y_BIT,))
        self.gains.third()
        self.gains.last()

    def keys_moving(self, phase):
        if phase == 0:
            self.out.first()
        if phase == 1:
            self.out.second()
            self.spread((X_BIT, Y_BIT))

    def need(self, name):
        if name == "keyval":
            self.keyval.third()
            self.keyval.last()
        if name == "query":
            self.query.third()
            self.query.last()
        if name == "out":
            self.out.third()
            self.out.last()
        if name == "ffn":
            for mask in AWAY:
                for j in (0, 1):
                    self._came(mask, j)
                self._sibling(mask).start()
            for mask in (0,) + AWAY:
                self._sibling(mask, C_BIT).wait_recv()
        n = WEIGHTS.index(name)
        load(self.s.w[name], self.store[name], self.s.store.at[n])

    def drain(self):
        for gather in (self.gains, self.keyval, self.query, self.out):
            gather.drain()
        for mask in AWAY:
            for j in (0, 1):
                self._spread(mask, j).wait_send()
        for mask in (0,) + AWAY:
            self._sibling(mask).wait_send()
        for n, name in enumerate(WEIGHTS):
            landed(self.store[name], self.s.store.at[n])


def most_layers(inputs, cotangent, shards, tables):
    rows, width = inputs.shape[1:]
    units = shards["down"].shape[0] // 4
    entries = 2 * width + 2 * HEAD_SIZE
    share = entries // 16
    steps = inputs.shape[0] + 1
    shapes = dict(zip(WEIGHTS, [(16,) + shards[name].shape for name in WEIGHTS[:3]] + [(3, units, width)]))
    own = (rows, width)

    def body(i, o, s):
        place = Place()
        arrival = Arrival(place, i.shards, s, o.weights)
        greet(place, NEIGHBOURS + (X_BIT | Y_BIT,), into="both")
        arrival.begin()
        s.gains[...] = jnp.concatenate([s.gains_all[n, 0:1, :share].astype(F32) for n in range(16)], axis=1)

        def ahead(step, need):
            m = jnp.clip(step - place.section, 0, inputs.shape[0] - 1)
            r = Refs(
                s.f | i.tables,
                w=s.w,
                gains=s.gains,
                inputs=i.inputs,
                received=None if step == 0 else s.received.at[step - 1],
                result=s.result.at[step],
                kept=o.fwd[step],
            )
            return forward_steps(r, place, m, need)

        def back(step, m, past, source):
            r = Refs(s.b | i.tables, w=s.w, gains=s.gains, grad=s.grad.at[step])
            return BackwardLayer(r, place, m, lambda name: None, past, source)

        def save_back(step):
            return [load(s.b[name], o.back[step][name], s.keep.at[n]) for n, name in enumerate(o.back[step])]

        def publish(sources, target, slots, section):
            @pl.when(place.section == section)
            def _():
                for n, (source, slot) in enumerate(zip(sources, slots)):
                    load(source, target.at[slot], s.publish.at[n])
                for n, (source, slot) in enumerate(zip(sources, slots)):
                    landed(target.at[slot], s.publish.at[n])

        def courier(source, target, n, into):
            return Courier(place, source, target, (s.pass_send.at[n], s.pass_recv.at[n]), into)

        def tell(n):
            for mask in NEIGHBOURS:
                pl.semaphore_signal(s.steps.at[n], inc=1, device_id=place.peer(mask), device_id_type=MESH_ID)

        def hear(n):
            pl.semaphore_wait(s.steps.at[n], len(NEIGHBOURS))

        first = ahead(0, arrival.need)
        take(first, 1)
        for phase in (0, 1):
            take(first, 1)
            arrival.keys_moving(phase)
        until(first, "result")
        passes = [courier(s.result.at[0], s.received.at[0], 0, 1)]
        passes[0].start()
        until(first, None)
        tell(0)
        store_gains = load(s.gains, o.gains, s.store.at[4])

        passes[0].arrive()
        hear(0)
        second = ahead(1, lambda name: None)
        until(second, "result")
        passes.append(courier(s.result.at[1], s.received.at[1], 1, 1))
        until(second, None)
        tell(1)
        hear(1)

        layer = back(0, 0, (o.fwd[1], o.fwd[1]), (None, i.cotangent.at[0]))
        layer.fetch()
        layer.fetch_gu(s.gu_back)
        passes.append(courier(s.grad.at[0], s.returned, 2, 0))
        one, other = layer.steps(s.gu_back), ahead(2, lambda name: None)
        for turn in SCHEDULE:
            if turn == "s":
                passes[1].start()
            elif turn == "r":
                passes[1].arrive()
            elif turn == "o":
                passes[2].start()
                saves = save_back(0)
            else:
                take(one if turn == "b" else other, 1)
        until(one, None)
        until(other, None)
        layer.drain()
        for copy in saves:
            copy.wait()
        tell(2)

        layer = back(1, place.section, (o.fwd[0], o.fwd[2]), (s.returned, i.cotangent.at[1]))
        layer.fetch()
        layer.fetch_gu(s.gu_back)
        passes[2].arrive()
        hear(2)
        until(layer.steps(s.gu_back), "result")
        passes.append(courier(s.grad.at[1], o.passed, 3, 0))
        passes[3].start()
        saves = save_back(1)
        publish([s.result.at[0], s.result.at[1]], o.section, (0, 1), 0)
        publish([s.result.at[1], s.result.at[2]], o.section, (0, 1), 1)
        publish([s.grad.at[1]], o.grads, (0,), 0)
        publish([s.grad.at[0], s.grad.at[1]], o.grads, (0, 1), 1)
        layer.drain()
        arrival.drain()
        store_gains.wait()
        for copy in saves:
            copy.wait()
        passes[3].arrive()
        for taken in passes:
            taken.leave()

    outputs = dict(
        section=Out((2,) + own, BF16, True),
        grads=Out((2,) + own, BF16, True),
        passed=Out(own, BF16, True),
        weights={name: Out(shape, BF16, True) for name, shape in shapes.items()},
        gains=Out((1, entries), F32, True),
        fwd=[forward_kept(rows, width, units) for _ in range(steps)],
        back=[backward_kept(rows, width, units) for _ in range(steps - 1)],
    )
    scratch = dict(
        f=forward_scratch(rows, width, units),
        b=backward_scratch(rows, width, units),
        w={name: pltpu.VMEM(shape, BF16) for name, shape in shapes.items()},
        gains=pltpu.VMEM((1, entries), F32),
        gains_all=pltpu.VMEM((16,) + shards["gains"].shape, BF16),
        gu_back=pltpu.VMEM((2 * units, BLOCKS * rows), F32),
        result=pltpu.VMEM((steps,) + own, BF16),
        grad=pltpu.VMEM((steps - 1,) + own, BF16),
        received=pltpu.VMEM((steps - 1,) + own, BF16),
        returned=pltpu.VMEM(own, BF16),
        gains_sems=pair(15),
        keyval_sems=pair(30),
        query_sems=pair(30),
        out_sems=pair(30),
        ffn_send=pltpu.SemaphoreType.DMA((12,)),
        ffn_recv=pltpu.SemaphoreType.DMA((12,)),
        fetch=pltpu.SemaphoreType.DMA((6,)),
        store=pltpu.SemaphoreType.DMA((5,)),
        keep=pltpu.SemaphoreType.DMA((7,)),
        publish=pltpu.SemaphoreType.DMA((2,)),
        pass_send=pltpu.SemaphoreType.DMA((4,)),
        pass_recv=pltpu.SemaphoreType.DMA((4,)),
        steps=pltpu.SemaphoreType.REGULAR((3,)),
    )
    operands = near(inputs=inputs, cotangent=cotangent) | dict(tables=near(**tables), shards=far(**shards))
    return run(body, 0, operands, outputs, scratch)


GRAD_ROWS = ("a", "da", "ob", "dq", "dkv")


def last_layer(returned, grads, weights, gains, tables, past, kept):
    rows, width = returned.shape
    units = weights["ffn"].shape[1]
    tokens = BLOCKS * rows
    columns = width // 8
    entries = 2 * width + 2 * HEAD_SIZE
    last = len(kept[0]) - 1
    parts = dict(query=(columns, HALF_COLUMNS), keyval=(width // 16, 2 * KEY_COLUMNS), out=(HALF_COLUMNS, columns))
    lines = -(-entries // 1024) * 8

    def body(i, o, s):
        place = Place()
        core = place.bits[0]

        def on(section):
            return pl.when(place.section == section)

        r = Refs(
            s.b | {name: s.x[name].at[0, last] for name in ("a", "da", "dq", "dkv")} | i.tables,
            w=dict(s.w),
            gains=i.gains,
            grad=o.grads.at[last],
        )
        r["w"] = Refs(s.w)
        layer = BackwardLayer(
            r, place, last, lambda name: None, (i.past, None), (i.returned, None), ((384, 256), TOWARD_Z)
        )
        greet(place, NEIGHBOURS + (X_BIT | Y_BIT,))

        @on(0)
        def _():
            layer.rows_out()
            layer.fetch()
            load(i.grads.at[0], o.grads.at[0], s.turn.at[0])

        @on(1)
        def _():
            for m in range(2):
                load(i.grads.at[m], o.grads.at[m], s.turn.at[m])
            load(i.kept[1][1].df, r.df, r.held.at[0])
            load(i.kept[1][1].dgu, r.dgu, r.held.at[1])

        loads = {name: load(i.weights[name], s.w[name], s.fetch.at[n]) for n, name in enumerate(s.w)}

        def own_rows(start):
            for n, name in enumerate(GRAD_ROWS):
                for m in range(2):
                    for section in (0, 1):
                        if name in i.kept[section][m]:

                            @on(section)
                            def _():
                                source, target = i.kept[section][m][name], s.x[name].at[0, m]
                                if start:
                                    load(source, target, s.rows.at[2 * n + m])
                                else:
                                    landed(target, s.rows.at[2 * n + m])

        own_rows(True)
        for section in (0, 1):

            @on(section)
            def _():
                load(i.kept[section][0].gain, s.gain_kept, s.rows.at[10])
                if section == 1:
                    load(i.kept[1][1].gain, r.gain, s.rows.at[11])

        def exchange(name, m):
            n = 2 * GRAD_ROWS.index(name) + m
            buf = s.x[name]
            return remote(buf.at[0, m], buf.at[1, m], s.x_send.at[n], s.x_recv.at[n], place.peer(C_BIT))

        loads["ffn"].wait()

        def at(mask):
            return pl.ds(pl.multiple_of(place.ctx(mask) * columns, columns), columns)

        def units_at(mask):
            return pl.ds(pl.multiple_of((place.chip(mask) % 4) * units, units), units)

        def to_sibling(n, mask):
            where = s.w.ffn.at[:, :, at(mask | C_BIT)]
            return remote(where, s.sib_ffn.at[n], s.sib_send.at[n], s.sib_recv.at[n], place.peer(C_BIT))

        def to_owner(mask):
            n = mask // 2
            source, target = s.w.ffn.at[:, :, at(mask)], o.ffn.at[:, units_at(0), :]
            return remote(source, target, s.ffn_send.at[n], s.ffn_recv.at[n], place.peer(mask))

        def from_owner(mask):
            n = mask // 2
            where = o.ffn.at[:, units_at(mask), :]
            remote(where, where, s.ffn_send.at[n], s.ffn_recv.at[n], place.peer(mask)).wait_recv()

        def ffn_grads(e, hid, df_0, dgu_0):
            for section in (0, 1):

                @on(section)
                def _():
                    for m, kept_m in enumerate(i.kept[section]):
                        load(kept_m.e, e.at[m], s.wide.at[m])
                        load(kept_m.hid, hid.at[m], s.wide.at[2 + m])
                    load(i.kept[section][0].df, df_0, s.wide.at[4])
                    load(i.kept[section][0].dgu, dgu_0, s.wide.at[5])

            @on(1)
            def _():
                landed(r.df, r.held.at[0])
                landed(r.dgu, r.held.at[1])

            for m in range(2):
                landed(e.at[m], s.wide.at[m])
                landed(hid.at[m], s.wide.at[2 + m])
            landed(df_0, s.wide.at[4])
            landed(dgu_0, s.wide.at[5])

            def partial(mask):
                where = at(mask)
                up = jnp.zeros((2 * units, columns), F32)
                down = jnp.zeros((units, columns), F32)
                for m, (dgu, df) in enumerate(((dgu_0, df_0), (r.dgu, r.df))):
                    up = up + dot(dgu[...], e[m, :, :, where].reshape(tokens, columns))
                    down = down + dot(hid[m], df[:, :, where].reshape(tokens, columns))
                return up, down

            def store(mask, up, down):
                s.w.ffn[:2, :, at(mask)] = up.astype(BF16).reshape(2, units, columns)
                s.w.ffn[2, :, at(mask)] = down.astype(BF16)

            for n, mask in enumerate(AWAY + (0,)):
                store(mask | C_BIT, *partial(mask | C_BIT))
                to_sibling(n, mask).start()

            @on(0)
            def _():
                layer.scatter.second()

            for n, mask in enumerate(AWAY + (0,)):
                up, down = partial(mask)
                to_sibling(n, mask).wait_recv()
                up = up + s.sib_ffn[n, :2].astype(F32).reshape(2 * units, columns)
                store(mask, up, down + s.sib_ffn[n, 2].astype(F32))
                if n == 2:

                    @on(0)
                    def _():
                        layer.scatter.third()

            to_owner(X_BIT | Y_BIT).start()
            load(s.w.ffn.at[:, :, at(0)], o.ffn.at[:, units_at(0), :], s.fetch.at[4])

            @on(0)
            def _():
                layer.scatter.last()

        def front(part):
            r["part"] = part

            @on(0)
            def _():
                layer.scatter.part = part
                layer.feed_forward()

            pl.run_scoped(
                ffn_grads,
                pltpu.VMEM((2, BLOCKS, rows, width), BF16),
                pltpu.VMEM((2, units, tokens), BF16),
                pltpu.VMEM((BLOCKS, rows, width), BF16),
                pltpu.VMEM((2 * units, tokens), BF16),
            )

            @on(0)
            def _():
                layer.scatter.drain()

        pl.run_scoped(front, pltpu.VMEM((BLOCKS, rows, width), BF16))

        @on(0)
        def _():
            layer.middle()

        own_rows(False)

        def swap(names, ms):
            for name in names:
                for m in ms:
                    exchange(name, m).start()

        swap(("ob", "da", "a"), (0, 1))
        swap(("dq", "dkv"), (0,))

        def both(name, where):
            return s.x[name][:, :, :, where].reshape(4 * rows, where.size)

        def got(names, ms):
            for name in names:
                for m in ms:
                    exchange(name, m).wait_recv()

        def putter(ref):
            def put(index, total):
                ref[index] = total

            return put

        scatters = Refs()
        for name in parts:
            pieces = row_pieces((48, 48, 32), CYCLES) if name == "keyval" else halves(parts[name][0])
            scatters[name] = Scatter(place, s.part[name], s.land[name], pieces, s.sums[name], putter(o.attention[name]))

        def wide_columns(c):
            return pl.ds(pl.multiple_of((2 * c + core) * columns, columns), columns)

        def half(z):
            return pl.ds(z * HALF_COLUMNS, HALF_COLUMNS)

        got(("ob", "da"), (0, 1))
        for z in (0, 1):
            for c in range(4):
                s.part.out[4 * z + c] = dot_tn(both("ob", half(z)), both("da", wide_columns(c))).astype(BF16)
        scatters.out.start(pieces=(0,))

        def rest(w_keyval, w_query, do5, dq5):
            r.update(do5=do5, dq5=dq5)
            r.w.update(keyval=w_keyval, query=w_query)
            load(i.weights.keyval, w_keyval, s.fetch.at[3])
            load(i.weights.query, w_query, s.fetch.at[2])
            loads["out"].wait()

            @on(0)
            def _():
                layer.attention()

            scatters.out.start(pieces=(1,))
            landed(w_query, s.fetch.at[2])
            landed(w_keyval, s.fetch.at[3])

            @on(0)
            def _():
                layer.queries()

            swap(("dq",), (1,))
            got(("a", "dq"), (0, 1))
            for z in (0, 1):
                for c in range(4):
                    s.part.query[4 * z + c] = dot_tn(both("a", wide_columns(c)), both("dq", half(z))).astype(BF16)
            scatters.query.start()

            @on(0)
            def _():
                layer.key_sums()

            to_owner(X_BIT).start()
            to_owner(Y_BIT).start()

            @on(0)
            def _():
                layer.keys()

            swap(("dkv",), (1,))

        pl.run_scoped(
            rest,
            pltpu.VMEM(weights["keyval"].shape, BF16),
            pltpu.VMEM(weights["query"].shape, BF16),
            pltpu.VMEM((QUERY_HEADS * rows, HEAD_SIZE), BF16),
            pltpu.VMEM((QUERY_HEADS * rows, HEAD_SIZE), F32),
        )
        got(("dkv",), (0, 1))
        narrow = width // 16
        for z in (0, 1):
            for c in range(4):
                where = pl.ds(pl.multiple_of((8 * z + 2 * c + core) * narrow, narrow), narrow)
                every = pl.ds(0, 2 * KEY_COLUMNS)
                s.part.keyval[4 * z + c] = dot_tn(both("a", where), both("dkv", every)).astype(BF16)
        scatters.keyval.start()

        landed(s.gain_kept, s.rows.at[10])

        @on(1)
        def _():
            landed(r.gain, s.rows.at[11])

        total = s.gain_kept[...] + r.gain[...]
        lanes = entries // 128
        padding = jnp.zeros((lines - lanes, 128), F32)
        s.gain_all[place.block()] = jnp.concatenate(
            [total[:, n * 128 : (n + 1) * 128] for n in range(lanes)] + [padding], axis=0
        )
        gain_gather = Gather(place, s.gain_all, row_pieces((lines,), TOWARD_Z), s.gain_sems, True)
        gain_gather.start()
        scatters.out.second()
        gain_gather.first()
        gain_gather.second()
        scatters.query.second()
        scatters.out.third()
        scatters.keyval.second()
        scatters.query.third()
        scatters.out.last()
        scatters.keyval.third()
        gain_gather.third()
        scatters.query.last()
        scatters.keyval.last()
        gain_gather.last()
        total = s.gain_all[0]
        for n in range(1, 16):
            total = total + s.gain_all[n]
        o.gains[...] = total
        for mask in AWAY:
            from_owner(mask)
        for mask in AWAY:
            to_owner(mask).wait_send()
        landed(o.ffn.at[:, units_at(0), :], s.fetch.at[4])
        for n, mask in enumerate(AWAY + (0,)):
            to_sibling(n, mask).wait_send()
        for name in GRAD_ROWS:
            for m in range(2):
                exchange(name, m).wait_send()
        for scatter in scatters.values():
            scatter.drain()
        gain_gather.drain()
        landed(o.grads.at[0], s.turn.at[0])

        @on(0)
        def _():
            layer.gather.drain()
            layer.scatter_kv.drain()

        @on(1)
        def _():
            landed(o.grads.at[1], s.turn.at[1])

    outputs = dict(
        grads=Out((2, rows, width), BF16, False),
        attention={name: Out(shape, F32, False) for name, shape in parts.items()},
        ffn=Out((3, 4 * units, columns), BF16, True),
        gains=Out((lines, 128), F32, False),
    )
    b = backward_scratch(rows, width, units)
    row_widths = dict(zip(GRAD_ROWS, (width, width, QUERY_COLUMNS, QUERY_COLUMNS, 2 * KEY_COLUMNS)))
    for name in ("a", "da", "dq", "dkv", "do5", "dq5", "part"):
        del b[name]
    scratch = dict(
        b=b,
        w={name: pltpu.VMEM(weights[name].shape, BF16) for name in ("ffn", "out")},
        gain_kept=pltpu.VMEM((1, entries), F32),
        gain_all=pltpu.VMEM((16, lines, 128), F32),
        sib_ffn=pltpu.VMEM((4, 3, units, columns), BF16),
        x={name: pltpu.VMEM((2, 2, rows, size), BF16) for name, size in row_widths.items()},
        part={name: pltpu.VMEM((BLOCKS,) + shape, BF16) for name, shape in parts.items()},
        land={name: pltpu.VMEM((BLOCKS - 1,) + shape, BF16) for name, shape in parts.items()},
        sums={name: pair(21) for name in parts},
        gain_sems=pair(15),
        ffn_send=pltpu.SemaphoreType.DMA((4,)),
        ffn_recv=pltpu.SemaphoreType.DMA((4,)),
        sib_send=pltpu.SemaphoreType.DMA((4,)),
        sib_recv=pltpu.SemaphoreType.DMA((4,)),
        x_send=pltpu.SemaphoreType.DMA((10,)),
        x_recv=pltpu.SemaphoreType.DMA((10,)),
        fetch=pltpu.SemaphoreType.DMA((5,)),
        rows=pltpu.SemaphoreType.DMA((12,)),
        wide=pltpu.SemaphoreType.DMA((6,)),
        turn=pltpu.SemaphoreType.DMA((2,)),
    )
    operands = near(returned=returned, gains=gains) | far(grads=grads) | dict(tables=near(**tables))
    operands |= dict(weights=far(**weights), past=far(**{name: past[name] for name in BACK_NEEDS}))
    operands["kept"] = [[far(**{n: x for n, x in one.items() if n in GRAD_NEEDS}) for one in side] for side in kept]
    return run(body, 1, operands, outputs, scratch)


BACK_NEEDS = ("u", "h", "qraw", "kraw", "q", "kv", "gu")
GRAD_NEEDS = ("e", "hid", "df", "dgu", "gain") + GRAD_ROWS


def gradients_out(ffn):
    units, columns = ffn.shape[1:]
    steps = 4
    some = units // steps

    def body(source, gateup, down):
        for j in range(2):
            gateup[:, j, :] = jnp.transpose(source[j]).astype(F32)
        down[...] = source[2].astype(F32)

    return pl.pallas_call(
        body,
        grid=(steps,),
        in_specs=[pl.BlockSpec((3, some, columns), lambda i: (0, i, 0))],
        out_specs=(
            pl.BlockSpec((columns, 2, some), lambda i: (0, 0, i)),
            pl.BlockSpec((some, columns), lambda i: (i, 0)),
        ),
        out_shape=(
            jax.ShapeDtypeStruct((columns, 2, units), F32),
            jax.ShapeDtypeStruct((units, columns), F32),
        ),
        compiler_params=pltpu.CompilerParams(vmem_limit_bytes=VMEM_BYTES),
    )(ffn)


def cube_device(
    inputs,
    cotangent,
    slot_order,
    query_weight,
    key_value_matrix,
    out_weight,
    gateup_weight,
    down_weight,
    norm_gains,
):
    tensor_id = lax.axis_index("tensor")
    context_id = lax.axis_index("ctx")
    batches, rows, width = inputs.shape
    tensors, contexts = 2, 8
    span = rows * tensors
    share = norm_gains.shape[1]
    shards = dict(
        query=query_weight[0],
        keyval=key_value_matrix[0],
        out=out_weight[0],
        gateup=jnp.transpose(gateup_weight[0], (1, 2, 0)),
        down=down_weight[0],
        gains=jnp.pad(norm_gains, ((0, 15), (0, -share % 128))),
    )
    own_slot = jnp.sum(jnp.where(jnp.arange(contexts) == context_id, slot_order, 0), axis=1)
    own_pos = own_slot[:, None] * span + tensor_id * rows + jnp.arange(rows)[None, :]
    half_width = HEAD_SIZE // 2
    frequency = ROPE_BASE ** (-(jnp.arange(half_width, dtype=F32) * 2.0) / HEAD_SIZE)
    angles = own_pos.astype(F32)[..., None] * frequency
    cosine, sine = jnp.cos(angles), jnp.sin(angles)
    rowtab = jnp.concatenate(
        [cosine, cosine, -sine, sine, jnp.broadcast_to(own_pos.astype(F32)[..., None], (batches, rows, 128))], axis=-1
    )
    within = jnp.arange(tensors)[:, None, None] * rows + jnp.arange(rows)[None, None, :]
    key_pos = (slot_order[:, None, :, None] * span + within[None]).reshape(batches, 1, -1)
    tables = dict(rowtab=rowtab, postab=key_pos.astype(F32))
    layers = most_layers(inputs, cotangent, shards, tables)
    fwd, back = layers["fwd"], layers["back"]
    kept = [[fwd[0] | back[1], fwd[1]], [fwd[1] | back[0], fwd[2] | back[1]]]
    last = last_layer(layers["passed"], layers["grads"], layers["weights"], layers["gains"], tables, fwd[1], kept)
    start = (tensor_id * contexts + context_id) * share
    attention = last["attention"]
    grad_gateup, grad_down = gradients_out(last["ffn"])
    return (
        layers["section"][None],
        last["grads"][None],
        attention["query"][None],
        attention["keyval"][None],
        attention["out"][None],
        grad_gateup[None],
        grad_down[None],
        lax.dynamic_slice(last["gains"].reshape(-1), (start,), (share,))[None],
    )


def fits_cube(mesh):
    return mesh.shape["section"] == 2 and mesh.shape["tensor"] == 2 and mesh.shape["ctx"] == 8


def solution(mesh):
    return jax.shard_map(
        cube_device if fits_cube(mesh) else per_device,
        mesh=mesh,
        in_specs=(
            P(None, ("tensor", "ctx"), None),
            P(None, ("tensor", "ctx"), None),
            P(),
            P("section", "ctx", "tensor"),
            P("section", ("tensor", "ctx"), None),
            P("section", "tensor", "ctx"),
            P("section", "ctx", None, "tensor"),
            P("section", "tensor", "ctx"),
            P("section", ("tensor", "ctx")),
        ),
        out_specs=(
            P("section", None, ("tensor", "ctx"), None),
            P("section", None, ("tensor", "ctx"), None),
            P("section", "ctx", "tensor"),
            P("section", ("tensor", "ctx"), None),
            P("section", "tensor", "ctx"),
            P("section", "ctx", None, "tensor"),
            P("section", "tensor", "ctx"),
            P("section", ("tensor", "ctx")),
        ),
        check_vma=False,
    )
```

```python
import typing

import jax
import jax.numpy as jnp
from jax import lax
from jax.experimental import pallas as pl
from jax.experimental.pallas import tpu as pltpu
from jax.sharding import PartitionSpec as P

MODEL_WIDTH = 2048
QUERY_HEADS = 20
KEY_VALUE_HEADS = 5
HEAD_SIZE = 64


EPSILON = 1e-06
ROPE_BASE = 10000.0
START_PEAK = -1e30


def from_behind(x, axis, by):
    devices = lax.axis_size(axis)
    pairs = [(i, i + by) for i in range(devices) if 0 <= i + by < devices]
    return lax.ppermute(x, axis, pairs)


def rope_tables(positions, head_width):
    half_width = head_width // 2
    frequency = ROPE_BASE ** (-(jnp.arange(half_width, dtype=jnp.float32) * 2.0) / head_width)
    angles = positions.astype(jnp.float32)[:, None] * frequency[None, :]
    return (jnp.cos(angles), jnp.sin(angles))


def rope_apply(values, cosine_rows, sine_rows):
    half_width = values.shape[-1] // 2
    first_half = values[..., :half_width]
    second_half = values[..., half_width:]
    cos_part = cosine_rows[:, None, :]
    sin_part = sine_rows[:, None, :]
    return jnp.concatenate(
        [
            first_half * cos_part - second_half * sin_part,
            second_half * cos_part + first_half * sin_part,
        ],
        axis=-1,
    )


def rope_back(incoming, cosine_rows, sine_rows):
    half_width = incoming.shape[-1] // 2
    first_half = incoming[..., :half_width]
    second_half = incoming[..., half_width:]
    cos_part = cosine_rows[:, None, :]
    sin_part = sine_rows[:, None, :]
    return jnp.concatenate(
        [
            first_half * cos_part + second_half * sin_part,
            second_half * cos_part - first_half * sin_part,
        ],
        axis=-1,
    )


def norm_parts(values, scaling):
    inverse = lax.rsqrt(jnp.mean(values * values, axis=-1, keepdims=True) + EPSILON)
    unit_rows = values * inverse
    return (unit_rows * scaling, unit_rows, inverse)


def norm_back(incoming, unit_rows, inverse, scaling):
    scaled = incoming * scaling
    inner = jnp.mean(scaled * unit_rows, axis=-1, keepdims=True)
    gain_grad = jnp.sum((incoming * unit_rows).reshape(-1, unit_rows.shape[-1]), axis=0)
    return (inverse * (scaled - unit_rows * inner), gain_grad)


def row_product(pieces_list, left_index, right_index):
    left_rows = jnp.concatenate([piece[left_index] for piece in pieces_list], axis=0)
    right_rows = jnp.concatenate([piece[right_index] for piece in pieces_list], axis=0)
    return lax.dot_general(
        left_rows, right_rows, (((0,), (0,)), ((), ())), preferred_element_type=jnp.float32
    )


def grads_from(pieces_list):
    grad_down = row_product(pieces_list, 0, 1)
    grad_gateup = row_product(pieces_list, 2, 3)
    grad_outw = row_product(pieces_list, 4, 5)
    grad_query = row_product(pieces_list, 6, 7)
    grad_keyval = row_product(pieces_list, 8, 9)
    grad_gain = pieces_list[0][10]
    for piece in pieces_list[1:]:
        grad_gain = grad_gain + piece[10]
    return (grad_query, grad_outw, grad_gateup, grad_down, grad_keyval, grad_gain)


def per_device(
    inputs,
    cotangent,
    slot_order,
    query_weight,
    key_value_matrix,
    out_weight,
    gateup_weight,
    down_weight,
    norm_gains,
):
    sections = lax.axis_size("section")
    tensors = lax.axis_size("tensor")
    contexts = lax.axis_size("ctx")
    section_id = lax.axis_index("section")
    tensor_id = lax.axis_index("tensor")
    context_id = lax.axis_index("ctx")
    batches = inputs.shape[0]
    rows_halved = inputs.shape[1]
    local_rows = rows_halved * tensors
    seq_rows = local_rows * contexts
    heads_here = query_weight.shape[2] // HEAD_SIZE
    units_here = down_weight.shape[1]
    key_columns = KEY_VALUE_HEADS * HEAD_SIZE
    rows_per_block = min(512, seq_rows)
    number_of_blocks = seq_rows // rows_per_block
    scale_query = HEAD_SIZE ** (-0.5)
    query_group_width = QUERY_HEADS // KEY_VALUE_HEADS
    head_numbers = tensor_id * heads_here + jnp.arange(heads_here)
    head_picker = head_numbers[:, None] // query_group_width == jnp.arange(KEY_VALUE_HEADS)[None, :]
    select_low = head_picker.astype(jnp.bfloat16)
    select_wide = head_picker.astype(jnp.float32)
    row_half = jnp.arange(rows_halved)
    row_local = jnp.arange(local_rows)
    within_seq = jnp.arange(tensors)[:, None, None] * rows_halved + row_half[None, None, :]

    def gather_rows(values):
        return lax.all_gather(values, "tensor", axis=0, tiled=True)

    def scatter_rows(values):
        return lax.psum_scatter(
            values.astype(jnp.bfloat16), "tensor", scatter_dimension=0, tiled=True
        ).astype(jnp.float32)

    def expand(block_part):
        return jnp.einsum(
            "khd,gh->kgd", block_part, select_low, preferred_element_type=jnp.float32
        ).astype(jnp.bfloat16)

    def block_scores(query_low, block_kv, pos_block, query_pos):
        keys_here = expand(block_kv[:, 0])
        scores = jnp.einsum(
            "qgd,kgd->gqk", query_low, keys_here, preferred_element_type=jnp.float32
        )
        allowed = pos_block[None, :] <= query_pos[:, None]
        return (jnp.where(allowed[None], scores, -jnp.inf), keys_here)

    def split_blocks(key_value_gathered, key_pos):
        return (
            key_value_gathered.reshape(
                number_of_blocks, rows_per_block, 2, KEY_VALUE_HEADS, HEAD_SIZE
            ),
            key_pos.reshape(number_of_blocks, rows_per_block),
        )

    def layer_backward(upstream, kept_state, weights):
        (
            attn_unit,
            attn_inv,
            normed_own,
            normed_all,
            query_unit,
            query_inv,
            query_low,
            key_unit,
            key_inv,
            key_value_gathered,
            log_mass,
            mixture,
            mixture_low,
            ffn_unit,
            ffn_inv,
            second_all,
            gateup,
            hidden_low,
            query_cos,
            query_sin,
            own_cos,
            own_sin,
            query_pos,
            key_pos,
        ) = kept_state
        query_full, out_full, gateup_full, down_full, keyval_full, gains_full = weights
        attn_gain = gains_full[:MODEL_WIDTH]
        ffn_gain = gains_full[MODEL_WIDTH : 2 * MODEL_WIDTH]
        query_gain = gains_full[2 * MODEL_WIDTH : 2 * MODEL_WIDTH + HEAD_SIZE]
        key_gain = gains_full[2 * MODEL_WIDTH + HEAD_SIZE :]
        down_all = gather_rows(upstream.astype(jnp.bfloat16))
        hidden_grad = jnp.dot(down_all, down_full.T, preferred_element_type=jnp.float32)
        gate_values = gateup[:, :units_here]
        up_values = gateup[:, units_here:]
        sigmoid_gate = jax.nn.sigmoid(gate_values)
        gate_grad = (
            hidden_grad * up_values * (sigmoid_gate * (1.0 + gate_values * (1.0 - sigmoid_gate)))
        )
        up_grad = hidden_grad * jax.nn.silu(gate_values)
        gateup_low = jnp.concatenate([gate_grad, up_grad], axis=1).astype(jnp.bfloat16)
        normed_grad = scatter_rows(
            jnp.dot(gateup_low, gateup_full.T, preferred_element_type=jnp.float32)
        )
        residual_part, ffn_gain_grad = norm_back(normed_grad, ffn_unit, ffn_inv, ffn_gain)
        middle = upstream + residual_part
        middle_all = gather_rows(middle.astype(jnp.bfloat16))
        mixture_grad = jnp.dot(middle_all, out_full.T, preferred_element_type=jnp.float32)
        mixture_grad_low = mixture_grad.astype(jnp.bfloat16).reshape(
            local_rows, heads_here, HEAD_SIZE
        )
        offsets = jnp.sum(mixture_grad_low.astype(jnp.float32) * mixture, axis=-1).T
        blocks, pos_blocks = split_blocks(key_value_gathered, key_pos)

        def grad_step(query_grad, packed):
            scores, keys_here = block_scores(query_low, packed[0], packed[1], query_pos)
            weights_full = jnp.exp(scores - log_mass[..., None])
            weights_low = weights_full.astype(jnp.bfloat16)
            values_here = expand(packed[0][:, 1])
            weight_grad = jnp.einsum(
                "qgd,kgd->gqk", mixture_grad_low, values_here, preferred_element_type=jnp.float32
            )
            score_low = (weights_full * (weight_grad - offsets[..., None])).astype(jnp.bfloat16)
            query_grad = query_grad + jnp.einsum(
                "gqk,kgd->qgd", score_low, keys_here, preferred_element_type=jnp.float32
            )
            key_grad = jnp.einsum(
                "gqk,qgd->kgd", score_low, query_low, preferred_element_type=jnp.float32
            )
            value_grad = jnp.einsum(
                "gqk,qgd->kgd", weights_low, mixture_grad_low, preferred_element_type=jnp.float32
            )
            pair_rows = jnp.stack(
                [
                    jnp.einsum("kgd,gh->khd", key_grad, select_wide),
                    jnp.einsum("kgd,gh->khd", value_grad, select_wide),
                ],
                axis=1,
            )
            return (query_grad, pair_rows.reshape(rows_per_block, 2 * key_columns))

        query_grad, pair_blocks = lax.scan(
            grad_step,
            jnp.zeros((local_rows, heads_here, HEAD_SIZE), jnp.float32),
            (blocks, pos_blocks),
        )
        key_value_gradient = lax.psum_scatter(
            pair_blocks.reshape(seq_rows, 2 * key_columns),
            ("tensor", "ctx"),
            scatter_dimension=0,
            tiled=True,
        )
        rotated_key_gradient = key_value_gradient[:, :key_columns].reshape(
            rows_halved, KEY_VALUE_HEADS, HEAD_SIZE
        )
        key_raw_grad, key_gain_grad = norm_back(
            rope_back(rotated_key_gradient, own_cos, own_sin), key_unit, key_inv, key_gain
        )
        keyval_low = jnp.concatenate(
            [key_raw_grad.reshape(rows_halved, key_columns), key_value_gradient[:, key_columns:]],
            axis=1,
        ).astype(jnp.bfloat16)
        own_grad = jnp.dot(keyval_low, keyval_full.T, preferred_element_type=jnp.float32)
        query_raw_grad, query_gain_grad = norm_back(
            rope_back(query_grad * scale_query, query_cos, query_sin),
            query_unit,
            query_inv,
            query_gain,
        )
        query_grad_low = query_raw_grad.reshape(local_rows, heads_here * HEAD_SIZE).astype(
            jnp.bfloat16
        )
        normed_grad = (
            scatter_rows(jnp.dot(query_grad_low, query_full.T, preferred_element_type=jnp.float32))
            + own_grad
        )
        residual_part, attn_gain_grad = norm_back(normed_grad, attn_unit, attn_inv, attn_gain)
        gain_grad = jnp.concatenate([attn_gain_grad, ffn_gain_grad, query_gain_grad, key_gain_grad])
        pieces = (
            hidden_low,
            down_all,
            second_all,
            gateup_low,
            mixture_low,
            middle_all,
            normed_all,
            query_grad_low,
            normed_own,
            keyval_low,
            gain_grad,
        )
        return (middle + residual_part, pieces)

    step_count = batches + sections - 1
    query_full = lax.all_gather(query_weight[0], "ctx", axis=0, tiled=True)
    out_full = lax.all_gather(out_weight[0], "ctx", axis=1, tiled=True)
    gateup_full = lax.all_gather(gateup_weight[0], "ctx", axis=0, tiled=True)
    down_full = lax.all_gather(down_weight[0], "ctx", axis=1, tiled=True)
    keyval_full = lax.all_gather(key_value_matrix[0], ("tensor", "ctx"), axis=0, tiled=True)
    gains_full = lax.all_gather(norm_gains[0], ("tensor", "ctx"), axis=0, tiled=True)
    weights_now = (
        query_full,
        out_full,
        gateup_full.reshape(MODEL_WIDTH, 2 * units_here),
        down_full,
        keyval_full,
        gains_full.astype(jnp.float32),
    )
    received = jnp.zeros_like(inputs[0])
    produced = []
    kept_all = []
    for step_index in range(step_count):
        batch_index = jnp.clip(step_index - section_id, 0, batches - 1)
        first_in = inputs[min(step_index, batches - 1)]
        residual = jnp.where(section_id == 0, first_in, received).astype(jnp.float32)
        layer_residual = residual
        (
            layer_query_full,
            layer_out_full,
            layer_gateup_full,
            layer_down_full,
            layer_keyval_full,
            layer_gains_full,
        ) = weights_now
        layer_attn_gain = layer_gains_full[:MODEL_WIDTH]
        layer_ffn_gain = layer_gains_full[MODEL_WIDTH : 2 * MODEL_WIDTH]
        layer_query_gain = layer_gains_full[2 * MODEL_WIDTH : 2 * MODEL_WIDTH + HEAD_SIZE]
        layer_key_gain = layer_gains_full[2 * MODEL_WIDTH + HEAD_SIZE :]
        slot_row = jnp.sum(
            jnp.where(jnp.arange(batches)[:, None] == batch_index, slot_order, 0), axis=0
        )
        own_slot = jnp.sum(jnp.where(jnp.arange(contexts) == context_id, slot_row, 0))
        positions_query_pos = own_slot * local_rows + row_local
        positions_key_pos = (slot_row[None, :, None] * local_rows + within_seq).reshape(seq_rows)
        own_pos = own_slot * local_rows + tensor_id * rows_halved + row_half
        layer_query_cos, layer_query_sin = rope_tables(positions_query_pos, HEAD_SIZE)
        layer_own_cos, layer_own_sin = rope_tables(own_pos, HEAD_SIZE)
        normed, layer_attn_unit, layer_attn_inv = norm_parts(layer_residual, layer_attn_gain)
        layer_normed_own = normed.astype(jnp.bfloat16)
        layer_normed_all = gather_rows(layer_normed_own)
        query_raw = jnp.dot(
            layer_normed_all, layer_query_full, preferred_element_type=jnp.float32
        ).reshape(local_rows, heads_here, HEAD_SIZE)
        query_hat, layer_query_unit, layer_query_inv = norm_parts(query_raw, layer_query_gain)
        layer_query_low = (
            rope_apply(query_hat, layer_query_cos, layer_query_sin) * scale_query
        ).astype(jnp.bfloat16)
        key_value_projected = jnp.dot(
            layer_normed_own, layer_keyval_full, preferred_element_type=jnp.float32
        )
        key_hat, layer_key_unit, layer_key_inv = norm_parts(
            key_value_projected[:, :key_columns].reshape(rows_halved, KEY_VALUE_HEADS, HEAD_SIZE),
            layer_key_gain,
        )
        key_low = (
            rope_apply(key_hat, layer_own_cos, layer_own_sin)
            .astype(jnp.bfloat16)
            .reshape(rows_halved, key_columns)
        )
        keyval_own = jnp.concatenate(
            [key_low, key_value_projected[:, key_columns:].astype(jnp.bfloat16)], axis=1
        )
        layer_key_value_gathered = lax.all_gather(keyval_own, ("tensor", "ctx"), axis=0, tiled=True)
        attend_query_low = layer_query_low
        attend_query_pos = positions_query_pos
        attend_blocks, attend_pos_blocks = split_blocks(layer_key_value_gathered, positions_key_pos)

        def peak_step(carry, packed):
            old_peak, mass_sum = carry
            scores, unused = block_scores(attend_query_low, packed[0], packed[1], attend_query_pos)
            new_peak = jnp.maximum(old_peak, jnp.max(scores, axis=-1))
            mass_sum = mass_sum * jnp.exp(old_peak - new_peak) + jnp.sum(
                jnp.exp(scores - new_peak[..., None]), axis=-1
            )
            return ((new_peak, mass_sum), None)

        initial = (
            jnp.full((heads_here, local_rows), START_PEAK, jnp.float32),
            jnp.zeros((heads_here, local_rows), jnp.float32),
        )
        (peak_value, mass_sum), unused = lax.scan(
            peak_step, initial, (attend_blocks, attend_pos_blocks)
        )
        attend_log_mass = peak_value + jnp.log(mass_sum)

        def value_step(running, packed):
            scores, unused = block_scores(attend_query_low, packed[0], packed[1], attend_query_pos)
            weights_low = jnp.exp(scores - attend_log_mass[..., None]).astype(jnp.bfloat16)
            values_here = expand(packed[0][:, 1])
            return (
                running
                + jnp.einsum(
                    "gqk,kgd->qgd", weights_low, values_here, preferred_element_type=jnp.float32
                ),
                None,
            )

        attend_mixture, unused = lax.scan(
            value_step,
            jnp.zeros((local_rows, heads_here, HEAD_SIZE), jnp.float32),
            (attend_blocks, attend_pos_blocks),
        )
        layer_mixture_low = attend_mixture.reshape(local_rows, heads_here * HEAD_SIZE).astype(
            jnp.bfloat16
        )
        layer_residual = layer_residual + scatter_rows(
            jnp.dot(layer_mixture_low, layer_out_full, preferred_element_type=jnp.float32)
        )
        normed, layer_ffn_unit, layer_ffn_inv = norm_parts(layer_residual, layer_ffn_gain)
        layer_second_all = gather_rows(normed.astype(jnp.bfloat16))
        layer_gateup = jnp.dot(
            layer_second_all, layer_gateup_full, preferred_element_type=jnp.float32
        )
        layer_hidden_low = (
            jax.nn.silu(layer_gateup[:, :units_here]) * layer_gateup[:, units_here:]
        ).astype(jnp.bfloat16)
        result = layer_residual + scatter_rows(
            jnp.dot(layer_hidden_low, layer_down_full, preferred_element_type=jnp.float32)
        )
        layer_kept_state = (
            layer_attn_unit,
            layer_attn_inv,
            layer_normed_own,
            layer_normed_all,
            layer_query_unit,
            layer_query_inv,
            layer_query_low,
            layer_key_unit,
            layer_key_inv,
            layer_key_value_gathered,
            attend_log_mass,
            attend_mixture,
            layer_mixture_low,
            layer_ffn_unit,
            layer_ffn_inv,
            layer_second_all,
            layer_gateup,
            layer_hidden_low,
            layer_query_cos,
            layer_query_sin,
            layer_own_cos,
            layer_own_sin,
            positions_query_pos,
            positions_key_pos,
        )
        result, kept_state = (result, layer_kept_state)
        result_low = result.astype(jnp.bfloat16)
        produced.append(result_low)
        kept_all.append(kept_state)
        if step_index + 1 < step_count:
            received = from_behind(result_low, "section", 1)
    kept_stack = jax.tree.map(lambda *parts: jnp.stack(parts), *kept_all)
    produced_stack = jnp.stack(produced)
    returned = jnp.zeros_like(inputs[0])
    consumed = []
    pieces_all = []
    for step_index in range(step_count):
        source = jnp.clip(step_index - (sections - 1) + 2 * section_id, 0, step_count - 1)
        kept_state = jax.tree.map(
            lambda stacked: lax.dynamic_index_in_dim(stacked, source, 0, keepdims=False), kept_stack
        )
        live_factor = 1.0 if step_index < batches else 0.0
        top_grad = cotangent[min(step_index, batches - 1)].astype(jnp.float32) * live_factor
        upstream = jnp.where(section_id == sections - 1, top_grad, returned.astype(jnp.float32))
        grad_input, pieces = layer_backward(upstream, kept_state, weights_now)
        pieces_all.append(pieces)
        grad_low = grad_input.astype(jnp.bfloat16)
        consumed.append(grad_low)
        if step_index + 1 < step_count:
            returned = from_behind(grad_low, "section", -1)
    full_set = grads_from(pieces_all)
    consumed_stack = jnp.stack(consumed)
    section_result = jnp.stack(
        [
            lax.dynamic_index_in_dim(produced_stack, batch_no + section_id, 0, keepdims=False)
            for batch_no in range(batches)
        ]
    )[None]
    input_result = jnp.stack(
        [
            lax.dynamic_index_in_dim(
                consumed_stack, batch_no + sections - 1 - section_id, 0, keepdims=False
            )
            for batch_no in range(batches)
        ]
    )[None]
    return (
        section_result,
        input_result,
        lax.psum_scatter(
            full_set[0].astype(jnp.bfloat16), "ctx", scatter_dimension=0, tiled=True
        ).astype(jnp.float32)[None],
        lax.psum_scatter(full_set[4], ("tensor", "ctx"), scatter_dimension=0, tiled=True)[None],
        lax.psum_scatter(
            full_set[1].astype(jnp.bfloat16), "ctx", scatter_dimension=1, tiled=True
        ).astype(jnp.float32)[None],
        lax.psum_scatter(
            full_set[2].reshape(MODEL_WIDTH, 2, units_here).astype(jnp.bfloat16),
            "ctx",
            scatter_dimension=0,
            tiled=True,
        ).astype(jnp.float32)[None],
        lax.psum_scatter(
            full_set[3].astype(jnp.bfloat16), "ctx", scatter_dimension=1, tiled=True
        ).astype(jnp.float32)[None],
        lax.psum_scatter(full_set[5], ("tensor", "ctx"), scatter_dimension=0, tiled=True)[None],
    )


C_BIT, X_BIT, Y_BIT, Z_BIT = 1, 2, 4, 8
MESH_ID = pl.DeviceIdType.MESH
F32 = jnp.float32
BF16 = jnp.bfloat16
GROUP = QUERY_HEADS // KEY_VALUE_HEADS
KEY_COLUMNS = KEY_VALUE_HEADS * HEAD_SIZE
QUERY_COLUMNS = QUERY_HEADS * HEAD_SIZE
HALF_COLUMNS = QUERY_COLUMNS // 2
SCALE = HEAD_SIZE ** (-0.5)
VMEM_BYTES = 62 * 2**20
CYCLES = ((X_BIT, Y_BIT, Z_BIT), (Y_BIT, Z_BIT, X_BIT), (Z_BIT, X_BIT, Y_BIT))
TOWARD_Z = ((X_BIT, Y_BIT, Z_BIT), (Y_BIT, X_BIT, Z_BIT))
ROW_WIDTHS = (768, 640, 640)
KV_WIDTHS = (256, 256, 128)
class Place:
    def __init__(self):
        self.section = lax.axis_index("section")
        ctx = lax.axis_index("ctx")
        self.bits = (ctx % 2, (ctx // 2) % 2, ctx // 4, lax.axis_index("tensor"))

    def flipped(self, mask):
        return [1 - bit if mask & (1 << i) else bit for i, bit in enumerate(self.bits)]

    def block(self, mask=0):
        core, x, y, z = self.flipped(mask)
        return z * 8 + y * 4 + x * 2 + core

    def chip(self, mask=0):
        _, x, y, z = self.flipped(mask)
        return z * 4 + y * 2 + x

    def ctx(self, mask=0):
        core, x, y, _ = self.flipped(mask)
        return y * 4 + x * 2 + core

    def peer(self, mask):
        core, x, y, z = self.flipped(mask)
        return (self.section, z, y * 4 + x * 2 + core)

    def other_section(self, section):
        core, x, y, z = self.bits
        return (section, z, y * 4 + x * 2 + core)


def remote(src, dst, send, recv, device):
    return pltpu.make_async_remote_copy(
        src_ref=src, dst_ref=dst, send_sem=send, recv_sem=recv, device_id=device, device_id_type=MESH_ID
    )


def load(src, dst, sem):
    copy = pltpu.make_async_copy(src, dst, sem)
    copy.start()
    return copy


def landed(ref, sem):
    pltpu.make_async_copy(ref, ref, sem).wait()


def greet(place, masks, into=None):
    barrier = pltpu.get_barrier_semaphore()
    for mask in masks:
        pl.semaphore_signal(barrier, inc=1, device_id=place.peer(mask), device_id_type=MESH_ID)
    if into is None:
        pl.semaphore_wait(barrier, len(masks))
        return
    if into == "both":
        pl.semaphore_signal(
            barrier, inc=1, device_id=place.other_section(1 - place.section), device_id_type=MESH_ID
        )
        pl.semaphore_wait(barrier, len(masks) + 1)
        return

    @pl.when(place.section == into)
    def _():
        pl.semaphore_signal(barrier, inc=1, device_id=place.other_section(1 - into), device_id_type=MESH_ID)
        pl.semaphore_wait(barrier, len(masks))

    @pl.when(place.section != into)
    def _():
        pl.semaphore_wait(barrier, len(masks) + 1)


def column_pieces(widths, orders):
    start, pieces = 0, []
    for width, order in zip(widths, orders):
        pieces.append(((slice(None), pl.ds(start, width)), order))
        start += width
    return pieces


def row_pieces(heights, orders):
    start, pieces = 0, []
    for height, order in zip(heights, orders):
        pieces.append(((pl.ds(start, height), slice(None)), order))
        start += height
    return pieces


def halves(rows):
    return row_pieces((rows // 2, rows // 2), TOWARD_Z)


class Gather:
    def __init__(self, place, buf, pieces, sems, siblings):
        self.place, self.buf, self.pieces, self.siblings = place, buf, list(enumerate(pieces)), siblings
        self.send, self.recv = sems

    def _where(self, piece, mask):
        block = self.place.block(mask) if self.siblings else self.place.chip(mask)
        return self.buf.at[(block,) + self.pieces[piece][1][0]]

    def _copy(self, piece, mask, dim):
        where = self._where(piece, mask)
        return remote(where, where, self.send, self.recv.at[self._slot(piece, mask ^ dim)], self.place.peer(dim))

    def _slot(self, piece, mask):
        return piece * 15 + mask - 1 if self.siblings else piece * 7 + mask // 2 - 1

    def _start(self, piece, mask, dim):
        self._copy(piece, mask, dim).start()

    def _arrived(self, piece, mask, dim):
        where = self._where(piece, mask)
        remote(where, where, self.send, self.recv.at[self._slot(piece, mask)], self.place.peer(dim)).wait_recv()

    def _pass(self, piece, mask, dims):
        for dim in dims:
            self._start(piece, mask, dim)
        if self.siblings:
            self._start(piece, mask, C_BIT)

    def start(self):
        for turn in range(3):
            for piece, (_, order) in self.pieces:
                self._start(piece, 0, order[turn])
        if self.siblings:
            for piece, _ in self.pieces:
                self._start(piece, 0, C_BIT)

    def first(self):
        for piece, (_, (d0, d1, d2)) in self.pieces:
            self._arrived(piece, d0, d0)
            self._pass(piece, d0, (d1, d2))

    def second(self):
        for part in (0, 1):
            for piece, (_, (d0, d1, d2)) in self.pieces:
                mask = (d1, d0 ^ d1)[part]
                self._arrived(piece, mask, d1)
                self._pass(piece, mask, (d2,))

    def third(self):
        for part in (0, 1, 2, 3):
            for piece, (_, (d0, d1, d2)) in self.pieces:
                mask = (d2, d0 ^ d2, d1 ^ d2, d0 ^ d1 ^ d2)[part]
                self._arrived(piece, mask, d2)
                self._pass(piece, mask, ())

    def last(self):
        if self.siblings:
            for piece, _ in self.pieces:
                for mask in range(0, 16, 2):
                    self._arrived(piece, mask ^ C_BIT, C_BIT)

    def finish(self):
        self.first()
        self.second()
        self.third()
        self.last()

    def drain(self):
        landed(self.buf.at[pl.ds(0, 15 if self.siblings else 7)], self.send)


class Scatter:
    def __init__(self, place, part, land, pieces, sems, put, sib_land=None):
        self.place, self.part, self.land, self.sib_land = place, part, land, sib_land
        self.pieces, self.put = list(enumerate(pieces)), put
        self.send, self.recv = sems

    def _block(self, mask):
        return self.place.chip(mask) if self.sib_land is None else self.place.block(mask)

    def _sib(self, i, mask):
        return remote(
            self.part.at[self.place.block(mask | C_BIT)],
            self.sib_land.at[i],
            self.send,
            self.recv.at[len(self.pieces) * 7 + i],
            self.place.peer(C_BIT),
        )

    def siblings(self):
        masks = (14, 12, 10, 6, 8, 4, 2, 0)
        for i, mask in enumerate(masks):
            self._sib(i, mask).start()
        for i, mask in enumerate(masks):
            self._sib(i, mask).wait_recv()
            block = self.place.block(mask)
            self.part[block] = (self.part[block].astype(F32) + self.sib_land[i].astype(F32)).astype(BF16)

    def _copy(self, piece, mask, dim):
        index = self.pieces[piece][1][0]
        return remote(
            self.part.at[(self._block(mask),) + index],
            self.land.at[(mask // 2 - 1,) + index],
            self.send,
            self.recv.at[piece * 7 + mask // 2 - 1],
            self.place.peer(dim),
        )

    def _start(self, piece, mask, dim):
        self._copy(piece, mask, dim).start()

    def _sum(self, piece, mask, dim):
        self._copy(piece, mask, dim).wait_recv()
        index = self.pieces[piece][1][0]
        at = (self._block(mask ^ dim),) + index
        return at, self.part[at].astype(F32) + self.land[(mask // 2 - 1,) + index].astype(F32)

    def _add(self, piece, mask, dim):
        at, total = self._sum(piece, mask, dim)
        self.part[at] = total.astype(BF16)

    def start(self, ready=range(16), pieces=None):
        for part in (0, 1, 2, 3):
            for piece, (_, (d0, d1, d2)) in self.pieces if pieces is None else [self.pieces[i] for i in pieces]:
                mask = (d0 ^ d1 ^ d2, d1 ^ d2, d0 ^ d2, d2)[part]
                if mask in ready:
                    self._start(piece, mask, d2)

    def second(self):
        for part in (0, 1):
            for piece, (_, (d0, d1, d2)) in self.pieces:
                mask = (d0 ^ d1, d1)[part]
                self._add(piece, mask ^ d2, d2)
                self._start(piece, mask, d1)
        for piece, (_, (d0, d1, d2)) in self.pieces:
            self._add(piece, d0 ^ d2, d2)

    def third(self):
        for piece, (_, (d0, d1, d2)) in self.pieces:
            self._add(piece, d0 ^ d1, d1)
            self._start(piece, d0, d0)
        for piece, (_, (d0, d1, d2)) in self.pieces:
            self._add(piece, d2, d2)
        for piece, (_, (d0, d1, d2)) in self.pieces:
            self._add(piece, d1, d1)

    def last(self):
        for piece, (index, (d0, d1, d2)) in self.pieces:
            _, total = self._sum(piece, d0, d0)
            self.put(index, total)

    def finish(self):
        self.second()
        self.third()
        self.last()

    def drain(self):
        landed(self.part.at[pl.ds(0, 7 if self.sib_land is None else 15)], self.send)


def sems(count):
    return [pltpu.SemaphoreType.DMA((count,)), pltpu.SemaphoreType.DMA((count,))]


def pair(count):
    return [pltpu.SemaphoreType.DMA, pltpu.SemaphoreType.DMA((count,))]


class Refs(dict):
    __getattr__ = dict.__getitem__


class Out(typing.NamedTuple):
    shape: tuple
    dtype: typing.Any
    far: bool


class In(typing.NamedTuple):
    array: typing.Any
    far: bool


def named(tree):
    if isinstance(tree, dict):
        return Refs({name: named(value) for name, value in tree.items()})
    return [named(value) for value in tree] if isinstance(tree, list) else tree


def near(**arrays):
    return {name: In(array, False) for name, array in arrays.items()}


def far(**arrays):
    return {name: In(array, True) for name, array in arrays.items()}


def run(body, collective, inputs, outputs, scratch):
    def is_leaf(value):
        return not isinstance(value, (dict, list))

    trees = [jax.tree.flatten(tree, is_leaf=is_leaf) for tree in (inputs, outputs, scratch)]
    (given, made, held) = [leaves for leaves, _ in trees]

    def kernel(*refs):
        parts, start = [], 0
        for leaves, tree in trees:
            parts.append(named(jax.tree.unflatten(tree, refs[start : start + len(leaves)])))
            start += len(leaves)
        body(*parts)

    def specs(leaves):
        return [pl.BlockSpec(memory_space=pl.ANY if leaf.far else pltpu.VMEM) for leaf in leaves]

    results = pl.pallas_call(
        kernel,
        out_shape=tuple(jax.ShapeDtypeStruct(leaf.shape, leaf.dtype) for leaf in made),
        in_specs=specs(given),
        out_specs=tuple(specs(made)),
        scratch_shapes=held,
        compiler_params=pltpu.CompilerParams(
            collective_id=collective, has_side_effects=True, vmem_limit_bytes=VMEM_BYTES
        ),
    )(*[leaf.array for leaf in given])
    return jax.tree.unflatten(trees[1][1], results)


def dot(left, right):
    return lax.dot_general(left, right, (((1,), (0,)), ((), ())), preferred_element_type=F32)


def dot_nt(left, right):
    return lax.dot_general(left, right, (((1,), (1,)), ((), ())), preferred_element_type=F32)


def dot_tn(left, right):
    return lax.dot_general(left, right, (((0,), (0,)), ((), ())), preferred_element_type=F32)


def unit_rows(values):
    inverse = lax.rsqrt(jnp.mean(values * values, axis=-1, keepdims=True) + EPSILON)
    return values * inverse, inverse


def unit_back(scaled, unit, inverse):
    return inverse * (scaled - unit * jnp.mean(scaled * unit, axis=-1, keepdims=True))


def stack_heads(values, heads):
    return jnp.concatenate([values[:, h * HEAD_SIZE : (h + 1) * HEAD_SIZE] for h in range(heads)], axis=0)


def spread_heads(values, heads):
    rows = values.shape[0] // heads
    return jnp.concatenate([values[h * rows : (h + 1) * rows] for h in range(heads)], axis=1)


def turned(values):
    half = HEAD_SIZE // 2
    return jnp.concatenate([values[:, half:], values[:, :half]], axis=1)


def tall(rows, times):
    return jnp.concatenate([rows] * times, axis=0)


def rope(values, cos, sin, heads):
    return values * tall(cos, heads) + turned(values) * tall(sin, heads)


def unrope(values, cos, sin, heads):
    return values * tall(cos, heads) - turned(values) * tall(sin, heads)


def mask_bias(m, r, bias):
    bias[...] = jnp.where(r.postab[m, 0:1, :] <= r.rowtab[m, :, 2 * HEAD_SIZE : 2 * HEAD_SIZE + 1], 0.0, -jnp.inf)


def split_keys(kv, k5, v5):
    rows = kv.shape[0] * kv.shape[1]
    for g in range(KEY_VALUE_HEADS):
        k5[g] = kv[:, :, g * HEAD_SIZE : (g + 1) * HEAD_SIZE].reshape(rows, HEAD_SIZE)
        v5[g] = kv[:, :, KEY_COLUMNS + g * HEAD_SIZE : KEY_COLUMNS + (g + 1) * HEAD_SIZE].reshape(rows, HEAD_SIZE)


def probabilities(queries, keys, bias):
    scores = dot_nt(queries, keys) + tall(bias, GROUP)
    raised = jnp.exp(scores - jnp.max(scores, axis=-1, keepdims=True))
    return raised / jnp.sum(raised, axis=-1, keepdims=True)


def gain_parts(r, width):
    return (
        r.gains[:, :width],
        r.gains[:, width : 2 * width],
        r.gains[:, 2 * width : 2 * width + HEAD_SIZE],
        r.gains[:, 2 * width + HEAD_SIZE :],
    )


class Courier:
    def __init__(self, place, source, target, pair, into):
        self.place, self.into = place, into
        self.copy = remote(source, target, pair[0], pair[1], place.other_section(into))

    def start(self):
        @pl.when(self.place.section != self.into)
        def _():
            self.copy.start()

    def arrive(self):
        @pl.when(self.place.section == self.into)
        def _():
            self.copy.wait_recv()

    def leave(self):
        @pl.when(self.place.section != self.into)
        def _():
            self.copy.wait_send()


BLOCKS = 8
KEY_PADDED = -(-KEY_COLUMNS // 128) * 128


def unit_blocks(units):
    return [pl.ds(half * (units // 2), units // 2) for half in (0, 1)]


def column_blocks(width):
    return [pl.ds(part * (width // 4), width // 4) for part in range(4)]


def forward_kept(rows, width, units):
    tokens = BLOCKS * rows
    return dict(
        u=Out((rows, width), BF16, True),
        h=Out((rows, width), F32, True),
        qraw=Out((rows, QUERY_COLUMNS), F32, True),
        kraw=Out((rows, KEY_PADDED), F32, True),
        q=Out((rows, QUERY_COLUMNS), BF16, True),
        kv=Out((2 * BLOCKS, rows, 2 * KEY_COLUMNS), BF16, True),
        gu=Out((2 * units, tokens), F32, True),
        ob=Out((rows, QUERY_COLUMNS), BF16, True),
        e=Out((BLOCKS, rows, width), BF16, True),
        hid=Out((units, tokens), BF16, True),
    )


def held_like(outs):
    return {name: pltpu.VMEM(out.shape, out.dtype) for name, out in outs.items()}


def forward_scratch(rows, width, units):
    return held_like(forward_kept(rows, width, units)) | dict(
        q5=pltpu.VMEM((KEY_VALUE_HEADS, GROUP * rows, HEAD_SIZE), BF16),
        part=pltpu.VMEM((BLOCKS, rows, width), BF16),
        land=pltpu.VMEM((BLOCKS - 1, rows, width), BF16),
        kv_sems=pair(45),
        e_sems=pair(21),
        y_sems=pair(21),
        keep=pltpu.SemaphoreType.DMA((10,)),
    )


def forward_steps(r, place, m, need):
    rows, width = r.u.shape
    units = r.hid.shape[0]
    attn_gain, ffn_gain, q_gain, k_gain = gain_parts(r, width)
    cos, sin = r.rowtab[m, :, :HEAD_SIZE], r.rowtab[m, :, HEAD_SIZE : 2 * HEAD_SIZE]
    saves = []

    def keep(name):
        saves.append(load(r[name], r.kept[name], r.keep.at[len(saves)]))

    r.u[...] = r.inputs[m] if r.received is None else jnp.where(place.section == 0, r.inputs[m], r.received[...])
    keep("u")
    a = (unit_rows(r.u[...].astype(F32))[0] * attn_gain).astype(BF16)
    need("keyval")
    kv_raw = dot(a, r.w.keyval[...].reshape(width, 2 * KEY_COLUMNS))
    r.kraw[...] = kv_raw[:, :KEY_PADDED]
    k_raw = stack_heads(kv_raw[:, :KEY_COLUMNS], KEY_VALUE_HEADS)
    k_low = rope(unit_rows(k_raw)[0] * k_gain, cos, sin, KEY_VALUE_HEADS).astype(BF16)
    r.kv[place.block()] = jnp.concatenate(
        [spread_heads(k_low, KEY_VALUE_HEADS), kv_raw[:, KEY_COLUMNS:].astype(BF16)], axis=1
    )
    kv_gather = Gather(place, r.kv, column_pieces(KV_WIDTHS, CYCLES), r.kv_sems, True)
    kv_gather.start()
    keep("kraw")
    need("query")
    q_raw = jnp.concatenate([dot(a, r.w.query[8 * t : 8 * t + 8].reshape(width, HALF_COLUMNS)) for t in range(2)], axis=1)
    r.qraw[...] = q_raw
    keep("qraw")
    q_unit = unit_rows(stack_heads(q_raw, QUERY_HEADS))[0]
    q_low = (rope(q_unit * q_gain, cos, sin, QUERY_HEADS) * SCALE).astype(BF16)
    r.q5[...] = q_low.reshape(KEY_VALUE_HEADS, GROUP * rows, HEAD_SIZE)
    r.q[...] = spread_heads(q_low, QUERY_HEADS)
    keep("q")
    yield
    kv_gather.first()
    yield
    kv_gather.second()
    yield
    kv_gather.third()
    kv_gather.last()
    keep("kv")

    def attention(k5, v5, o5, bias):
        mask_bias(m, r, bias)
        split_keys(r.kv, k5, v5)

        def attend(g, _):
            low = probabilities(r.q5[g], k5[g], bias[...]).astype(BF16)
            o5[g] = dot(low, v5[g])
            return 0

        lax.fori_loop(0, KEY_VALUE_HEADS, attend, 0)
        r.ob[...] = spread_heads(o5[...].reshape(QUERY_HEADS * rows, HEAD_SIZE), QUERY_HEADS).astype(BF16)

    keys = 2 * BLOCKS * rows
    group = pltpu.VMEM((KEY_VALUE_HEADS, keys, HEAD_SIZE), BF16)
    mixed_heads = pltpu.VMEM((KEY_VALUE_HEADS, GROUP * rows, HEAD_SIZE), F32)
    pl.run_scoped(attention, group, group, mixed_heads, pltpu.VMEM((rows, keys), F32))
    keep("ob")
    need("out")
    for c in range(8):
        block = pl.ds(c * (width // 8), width // 8)
        mixed = dot(r.ob[:, :HALF_COLUMNS], r.w.out[c]) + dot(r.ob[:, HALF_COLUMNS:], r.w.out[8 + c])
        r.h[:, block] = r.u[:, block].astype(F32) + mixed
    keep("h")
    r.e[place.chip()] = (unit_rows(r.h[...])[0] * ffn_gain).astype(BF16)
    e_gather = Gather(place, r.e, column_pieces(ROW_WIDTHS, CYCLES), r.e_sems, False)
    e_gather.start()
    need("ffn")
    yield
    e_gather.first()
    yield
    e_gather.second()
    yield
    e_gather.third()
    keep("e")

    def put(index, total):
        r.result[index] = (r.h[index] + total).astype(BF16)

    scatter = Scatter(place, r.part, r.land, column_pieces(ROW_WIDTHS, CYCLES), r.y_sems, put)
    for flip in (Z_BIT, 0):
        first = place.chip(flip) // 4 * 4
        tokens = pl.ds(pl.multiple_of(first * rows, 4 * rows), 4 * rows)
        here = pl.ds(first, 4)
        for some in unit_blocks(units):
            gate = dot_nt(r.w.ffn[0, some], r.e[here].reshape(4 * rows, width))
            up = dot_nt(r.w.ffn[1, some], r.e[here].reshape(4 * rows, width))
            r.gu[some, tokens] = gate
            r.gu[pl.ds(units + some.start, some.size), tokens] = up
            r.hid[some, tokens] = (gate * jax.nn.sigmoid(gate) * up).astype(BF16)
        for some in column_blocks(width):
            outward = dot_tn(r.hid[:, tokens], r.w.ffn[2, :, some])
            r.part[here, :, some] = outward.astype(BF16).reshape(4, rows, some.size)
        yield
        scatter.start([flip ^ mask for mask in (0, X_BIT, Y_BIT, X_BIT | Y_BIT)])
        yield
    keep("gu")
    keep("hid")
    scatter.second()
    yield
    scatter.third()
    yield
    scatter.last()
    yield "result"
    for gather in (kv_gather, e_gather):
        gather.drain()
    scatter.drain()
    for copy in saves:
        copy.wait()


def take(steps, count):
    for _ in range(count):
        next(steps, None)


def until(steps, what):
    for said in steps:
        if what is not None and said == what:
            return


def backward_kept(rows, width, units):
    tokens = BLOCKS * rows
    return dict(
        df=Out((BLOCKS, rows, width), BF16, True),
        dgu=Out((2 * units, tokens), BF16, True),
        a=Out((rows, width), BF16, True),
        da=Out((rows, width), BF16, True),
        dq=Out((rows, QUERY_COLUMNS), BF16, True),
        dkv=Out((rows, 2 * KEY_COLUMNS), BF16, True),
        gain=Out((1, 2 * width + 2 * HEAD_SIZE), F32, True),
    )


def backward_scratch(rows, width, units):
    past = held_like(forward_kept(rows, width, units))
    return held_like(backward_kept(rows, width, units)) | dict(
        u=past["u"],
        qraw=past["qraw"],
        kraw=past["kraw"],
        q=past["q"],
        dh=pltpu.VMEM((rows, width), F32),
        dx=pltpu.VMEM((rows, width), F32),
        do5=pltpu.VMEM((QUERY_HEADS * rows, HEAD_SIZE), BF16),
        dq5=pltpu.VMEM((QUERY_HEADS * rows, HEAD_SIZE), F32),
        dkv_own=pltpu.VMEM((rows, 2 * KEY_COLUMNS), F32),
        part=pltpu.VMEM((BLOCKS, rows, width), BF16),
        land=pltpu.VMEM((BLOCKS - 1, rows, width), BF16),
        part_kv=pltpu.VMEM((2 * BLOCKS, rows, 2 * KEY_COLUMNS), BF16),
        sib_kv=pltpu.VMEM((BLOCKS, rows, 2 * KEY_COLUMNS), BF16),
        land_kv=pltpu.VMEM((BLOCKS - 1, rows, 2 * KEY_COLUMNS), BF16),
        df_sems=pair(21),
        de_sems=pair(21),
        kv_sems=pair(29),
        held=pltpu.SemaphoreType.DMA((7,)),
    )


class BackwardLayer:
    def __init__(self, r, place, m, need, past, source, kv_pieces=(KV_WIDTHS, CYCLES)):
        self.r, self.place, self.m, self.need, self.kv_pieces = r, place, m, need, kv_pieces
        self.past, self.source = past, source

    def targets(self):
        r = self.r
        return dict(u=r.u, h=r.dh, qraw=r.qraw, kraw=r.kraw, q=r.q, kv=r.part_kv)

    def _fetch(self, targets, start):
        for section, past in enumerate(self.past):
            if past is not None:

                @pl.when(self.place.section == section)
                def _(past=past):
                    for i, (name, target) in enumerate(targets.items()):
                        load(past[name], target, self.r.held.at[start + i])

    def fetch(self):
        self._fetch(self.targets(), 0)

    def fetch_gu(self, gu):
        self._fetch(dict(gu=gu), 6)

    def rows_out(self):
        r, place = self.r, self.place
        first, second = self.source
        if first is None:
            dy = second[...]
        elif second is None:
            dy = first[...]
        else:
            dy = jnp.where(place.section == 0, first[...], second[...])
        r.df[place.chip()] = dy
        self.gather = Gather(place, r.df, column_pieces(ROW_WIDTHS, CYCLES), r.df_sems, False)
        self.gather.start()

        def put(index, total):
            r.dx[index] = total

        self.scatter = Scatter(place, r.get("part"), r.land, column_pieces(ROW_WIDTHS, CYCLES), r.de_sems, put)

    def chunk(self, gu, flip):
        r, place = self.r, self.place
        rows, width = r.u.shape
        units = r.dgu.shape[0] // 2
        first = place.chip(flip) // 4 * 4
        tokens = pl.ds(pl.multiple_of(first * rows, 4 * rows), 4 * rows)
        here = pl.ds(first, 4)
        for some in unit_blocks(units):
            beyond = pl.ds(units + some.start, some.size)
            dhidden = dot_nt(r.w.ffn[2, some], r.df[here].reshape(4 * rows, width))
            gate, up = gu[some, tokens], gu[beyond, tokens]
            shut = jax.nn.sigmoid(gate)
            r.dgu[some, tokens] = (dhidden * up * (shut * (1.0 + gate * (1.0 - shut)))).astype(BF16)
            r.dgu[beyond, tokens] = (dhidden * (gate * shut)).astype(BF16)
        for some in column_blocks(width):
            inward = dot_tn(r.dgu[:, tokens], r.w.ffn[:2, :, some].reshape(2 * units, some.size))
            r.part[here, :, some] = inward.astype(BF16).reshape(4, rows, some.size)

    def send(self, flip):
        self.scatter.start([flip ^ mask for mask in (0, X_BIT, Y_BIT, X_BIT | Y_BIT)])

    def feed_forward(self):
        def inner(gu):
            self.fetch_gu(gu)
            self.need("ffn")
            self.gather.finish()
            landed(gu, self.r.held.at[6])
            for flip in (Z_BIT, 0):
                self.chunk(gu, flip)
                self.send(flip)

        units, tokens = self.r.dgu.shape
        pl.run_scoped(inner, pltpu.VMEM((units, tokens), F32))

    def steps(self, gu):
        self.rows_out()
        yield
        self.gather.first()
        yield
        self.gather.second()
        yield
        self.need("ffn")
        self.gather.third()
        landed(gu, self.r.held.at[6])
        self.chunk(gu, Z_BIT)
        yield
        self.send(Z_BIT)
        yield
        self.chunk(gu, 0)
        yield
        self.send(0)
        yield
        self.scatter.second()
        yield
        self.scatter.third()
        yield
        self.scatter.last()
        self.middle()
        yield
        self.mixture()
        yield
        self.weights()
        yield
        self.key_siblings()
        yield
        self.queries()
        yield
        self.scatter_kv.second()
        yield
        self.scatter_kv.third()
        yield
        self.keys()
        yield "result"

    def middle(self):
        r = self.r
        rows, width = r.u.shape
        ffn_gain = gain_parts(r, width)[1]
        for i, target in enumerate(self.targets().values()):
            landed(target, r.held.at[i])
        unit, inverse = unit_rows(r.dh[...])
        r.gain[:, width : 2 * width] = jnp.sum(r.dx[...] * unit, axis=0, keepdims=True)
        r.dh[...] = r.df[self.place.chip()].astype(F32) + unit_back(r.dx[...] * ffn_gain, unit, inverse)
        r.da[...] = r.dh[...].astype(BF16)
        unit, _ = unit_rows(r.u[...].astype(F32))
        r.a[...] = (unit * gain_parts(r, width)[0]).astype(BF16)

    def attention(self):
        self.mixture()
        self.weights()
        self.key_siblings()

    def mixture(self):
        r = self.r
        rows, width = r.u.shape
        self.need("out")
        heads = QUERY_HEADS // 2
        for t in range(2):
            total = jnp.zeros((rows, HALF_COLUMNS), F32)
            for c in range(8):
                total = total + dot_nt(r.da[:, c * (width // 8) : (c + 1) * (width // 8)], r.w.out[t * 8 + c])
            r.do5[t * heads * rows : (t + 1) * heads * rows] = stack_heads(total.astype(BF16), heads)

    def weights(self):
        r, m = self.r, self.m
        rows = r.u.shape[0]
        keys = 2 * BLOCKS * rows

        def inner(q5, k5, v5, bias):
            mask_bias(m, r, bias)
            q5[...] = stack_heads(r.q[...], QUERY_HEADS).reshape(KEY_VALUE_HEADS, GROUP * rows, HEAD_SIZE)
            split_keys(r.part_kv, k5, v5)

            def attend(g, _):
                at = pl.ds(pl.multiple_of(g * GROUP * rows, GROUP * rows), GROUP * rows)
                weights = probabilities(q5[g], k5[g], bias[...])
                grads = r.do5[at]
                dweights = dot_nt(grads, v5[g])
                mean = jnp.sum(weights * dweights, axis=-1, keepdims=True)
                dscores = (weights * (dweights - mean)).astype(BF16)
                r.dq5[at] = dot(dscores, k5[g])
                k5[g] = dot_tn(dscores, q5[g]).astype(BF16)
                v5[g] = dot_tn(weights.astype(BF16), grads).astype(BF16)
                return 0

            lax.fori_loop(0, KEY_VALUE_HEADS, attend, 0)
            for b in range(2 * BLOCKS):
                at = slice(b * rows, (b + 1) * rows)
                r.part_kv[b] = jnp.concatenate(
                    [k5[g, at] for g in range(KEY_VALUE_HEADS)] + [v5[g, at] for g in range(KEY_VALUE_HEADS)], axis=1
                )

        kind = pltpu.VMEM((KEY_VALUE_HEADS, keys, HEAD_SIZE), BF16)
        grouped = pltpu.VMEM((KEY_VALUE_HEADS, GROUP * rows, HEAD_SIZE), BF16)
        pl.run_scoped(inner, grouped, kind, kind, pltpu.VMEM((rows, keys), F32))

    def key_siblings(self):
        r, place = self.r, self.place

        def put(index, total):
            r.dkv_own[index] = total

        pieces = column_pieces(*self.kv_pieces)
        self.scatter_kv = Scatter(place, r.part_kv, r.land_kv, pieces, r.kv_sems, put, r.sib_kv)
        self.scatter_kv.siblings()
        self.scatter_kv.start()

    def queries(self):
        r, m = self.r, self.m
        width = r.u.shape[1]
        q_gain = gain_parts(r, width)[2]
        cos, sin = r.rowtab[m, :, :HEAD_SIZE], r.rowtab[m, :, HEAD_SIZE : 2 * HEAD_SIZE]
        unit, inverse = unit_rows(stack_heads(r.qraw[...], QUERY_HEADS))
        dhat = unrope(r.dq5[...] * SCALE, cos, sin, QUERY_HEADS)
        r.gain[:, 2 * width : 2 * width + HEAD_SIZE] = jnp.sum(dhat * unit, axis=0, keepdims=True)
        r.dq[...] = spread_heads(unit_back(dhat * q_gain, unit, inverse), QUERY_HEADS).astype(BF16)
        self.need("query")
        r.dx[...] = dot_nt(r.dq[:, :HALF_COLUMNS], r.w.query[:8].reshape(width, HALF_COLUMNS)) + dot_nt(
            r.dq[:, HALF_COLUMNS:], r.w.query[8:].reshape(width, HALF_COLUMNS)
        )

    def key_sums(self):
        self.scatter_kv.second()
        self.scatter_kv.third()

    def keys(self):
        r, m = self.r, self.m
        width = r.u.shape[1]
        attn_gain, _, _, k_gain = gain_parts(r, width)
        cos, sin = r.rowtab[m, :, :HEAD_SIZE], r.rowtab[m, :, HEAD_SIZE : 2 * HEAD_SIZE]
        self.need("keyval")
        self.scatter_kv.last()
        unit, inverse = unit_rows(stack_heads(r.kraw[:, :KEY_COLUMNS], KEY_VALUE_HEADS))
        dhat = unrope(stack_heads(r.dkv_own[:, :KEY_COLUMNS], KEY_VALUE_HEADS), cos, sin, KEY_VALUE_HEADS)
        r.gain[:, 2 * width + HEAD_SIZE :] = jnp.sum(dhat * unit, axis=0, keepdims=True)
        dk_raw = spread_heads(unit_back(dhat * k_gain, unit, inverse), KEY_VALUE_HEADS)
        r.dkv[...] = jnp.concatenate([dk_raw, r.dkv_own[:, KEY_COLUMNS:]], axis=1).astype(BF16)
        r.dx[...] = r.dx[...] + dot_nt(r.dkv[...], r.w.keyval[...].reshape(width, 2 * KEY_COLUMNS))
        unit, inverse = unit_rows(r.u[...].astype(F32))
        r.gain[:, :width] = jnp.sum(r.dx[...] * unit, axis=0, keepdims=True)
        r.grad[...] = (r.dh[...] + unit_back(r.dx[...] * attn_gain, unit, inverse)).astype(BF16)

    def drain(self):
        for sent in (self.gather, self.scatter, self.scatter_kv):
            sent.drain()


WEIGHTS = ("keyval", "query", "out", "ffn")
SCHEDULE = "sbbbrfbfbbfbfbfbfbffbffbfbfbbbbof"
NEIGHBOURS = (C_BIT, X_BIT, Y_BIT, Z_BIT)
AWAY = (X_BIT | Y_BIT, X_BIT, Y_BIT)


class Arrival:
    def __init__(self, place, i, s, store):
        self.place, self.i, self.s, self.store = place, i, s, store
        self.columns = i.down.shape[1]
        self.units = s.w.ffn.shape[1]
        own = place.block()
        self.fetched = [
            load(src, dst, s.fetch.at[n])
            for n, (src, dst) in enumerate(
                (
                    (i.gains, s.gains_all.at[own]),
                    (i.keyval, s.w.keyval.at[own]),
                    (i.query, s.w.query.at[own]),
                    (i.out, s.w.out.at[own]),
                    (i.gateup.at[:, self._units(0), :], s.w.ffn.at[pl.ds(0, 2), :, self._columns(0)]),
                    (i.down.at[self._units(0), :], s.w.ffn.at[2, :, self._columns(0)]),
                )
            )
        ]
        self.gains = Gather(place, s.gains_all, row_pieces((16,), TOWARD_Z), s.gains_sems, True)
        self.keyval, self.query, self.out = (
            Gather(place, buf, halves(buf.shape[1]), pair_, True)
            for buf, pair_ in (
                (s.w.keyval, s.keyval_sems),
                (s.w.query, s.query_sems),
                (s.w.out, s.out_sems),
            )
        )

    def _units(self, mask):
        return pl.ds(pl.multiple_of((self.place.chip(mask) % 4) * self.units, self.units), self.units)

    def _columns(self, mask):
        return pl.ds(pl.multiple_of(self.place.ctx(mask) * self.columns, self.columns), self.columns)

    def _spread(self, mask, j):
        i, s, mine = self.i, self.s, self._columns(0)
        src, dst = (
            (i.gateup.at[:, self._units(mask), :], s.w.ffn.at[pl.ds(0, 2), :, mine]),
            (i.down.at[self._units(mask), :], s.w.ffn.at[2, :, mine]),
        )[j]
        return remote(src, dst, s.ffn_send.at[mask + j], s.ffn_recv.at[mask + j], self.place.peer(mask))

    def _came(self, mask, j):
        s, there = self.s, self._columns(mask)
        dst = s.w.ffn.at[2, :, there] if j else s.w.ffn.at[pl.ds(0, 2), :, there]
        remote(dst, dst, s.ffn_send.at[mask + j], s.ffn_recv.at[mask + j], self.place.peer(mask)).wait_recv()

    def _sibling(self, mask, back=0):
        s = self.s
        where = s.w.ffn.at[:, :, self._columns(mask | back)]
        slot = 8 + mask // 2
        return remote(where, where, s.ffn_send.at[slot], s.ffn_recv.at[slot], self.place.peer(C_BIT))

    def spread(self, masks):
        for mask in masks:
            for j in (0, 1):
                self._spread(mask, j).start()

    def begin(self):
        for n, gather in enumerate((self.gains, self.keyval, self.query)):
            self.fetched[n].wait()
            gather.start()
        for n in (3, 4, 5):
            self.fetched[n].wait()
        self._sibling(0).start()
        for gather in (self.gains, self.keyval, self.query):
            gather.first()
        for gather in (self.gains, self.keyval, self.query):
            gather.second()
        self.out.start()
        self.spread((X_BIT | Y_BIT,))
        self.gains.third()
        self.gains.last()

    def keys_moving(self, phase):
        if phase == 0:
            self.out.first()
        if phase == 1:
            self.out.second()
            self.spread((X_BIT, Y_BIT))

    def need(self, name):
        if name == "keyval":
            self.keyval.third()
            self.keyval.last()
        if name == "query":
            self.query.third()
            self.query.last()
        if name == "out":
            self.out.third()
            self.out.last()
        if name == "ffn":
            for mask in AWAY:
                for j in (0, 1):
                    self._came(mask, j)
                self._sibling(mask).start()
            for mask in (0,) + AWAY:
                self._sibling(mask, C_BIT).wait_recv()
        n = WEIGHTS.index(name)
        load(self.s.w[name], self.store[name], self.s.store.at[n])

    def drain(self):
        for gather in (self.gains, self.keyval, self.query, self.out):
            gather.drain()
        for mask in AWAY:
            for j in (0, 1):
                self._spread(mask, j).wait_send()
        for mask in (0,) + AWAY:
            self._sibling(mask).wait_send()
        for n, name in enumerate(WEIGHTS):
            landed(self.store[name], self.s.store.at[n])


def most_layers(inputs, cotangent, shards, tables):
    rows, width = inputs.shape[1:]
    units = shards["down"].shape[0] // 4
    entries = 2 * width + 2 * HEAD_SIZE
    share = entries // 16
    steps = inputs.shape[0] + 1
    shapes = dict(zip(WEIGHTS, [(16,) + shards[name].shape for name in WEIGHTS[:3]] + [(3, units, width)]))
    own = (rows, width)

    def body(i, o, s):
        place = Place()
        arrival = Arrival(place, i.shards, s, o.weights)
        greet(place, NEIGHBOURS + (X_BIT | Y_BIT,), into="both")
        arrival.begin()
        s.gains[...] = jnp.concatenate([s.gains_all[n, 0:1, :share].astype(F32) for n in range(16)], axis=1)

        def ahead(step, need):
            m = jnp.clip(step - place.section, 0, inputs.shape[0] - 1)
            r = Refs(
                s.f | i.tables,
                w=s.w,
                gains=s.gains,
                inputs=i.inputs,
                received=None if step == 0 else s.received.at[step - 1],
                result=s.result.at[step],
                kept=o.fwd[step],
            )
            return forward_steps(r, place, m, need)

        def back(step, m, past, source):
            r = Refs(s.b | i.tables, w=s.w, gains=s.gains, grad=s.grad.at[step])
            return BackwardLayer(r, place, m, lambda name: None, past, source)

        def save_back(step):
            return [load(s.b[name], o.back[step][name], s.keep.at[n]) for n, name in enumerate(o.back[step])]

        def publish(sources, target, slots, section):
            @pl.when(place.section == section)
            def _():
                for n, (source, slot) in enumerate(zip(sources, slots)):
                    load(source, target.at[slot], s.publish.at[n])
                for n, (source, slot) in enumerate(zip(sources, slots)):
                    landed(target.at[slot], s.publish.at[n])

        def courier(source, target, n, into):
            return Courier(place, source, target, (s.pass_send.at[n], s.pass_recv.at[n]), into)

        def tell(n):
            for mask in NEIGHBOURS:
                pl.semaphore_signal(s.steps.at[n], inc=1, device_id=place.peer(mask), device_id_type=MESH_ID)

        def hear(n):
            pl.semaphore_wait(s.steps.at[n], len(NEIGHBOURS))

        first = ahead(0, arrival.need)
        take(first, 1)
        for phase in (0, 1):
            take(first, 1)
            arrival.keys_moving(phase)
        until(first, "result")
        passes = [courier(s.result.at[0], s.received.at[0], 0, 1)]
        passes[0].start()
        until(first, None)
        tell(0)
        store_gains = load(s.gains, o.gains, s.store.at[4])

        passes[0].arrive()
        hear(0)
        second = ahead(1, lambda name: None)
        until(second, "result")
        passes.append(courier(s.result.at[1], s.received.at[1], 1, 1))
        until(second, None)
        tell(1)
        hear(1)

        layer = back(0, 0, (o.fwd[1], o.fwd[1]), (None, i.cotangent.at[0]))
        layer.fetch()
        layer.fetch_gu(s.gu_back)
        passes.append(courier(s.grad.at[0], s.returned, 2, 0))
        one, other = layer.steps(s.gu_back), ahead(2, lambda name: None)
        for turn in SCHEDULE:
            if turn == "s":
                passes[1].start()
            elif turn == "r":
                passes[1].arrive()
            elif turn == "o":
                passes[2].start()
                saves = save_back(0)
            else:
                take(one if turn == "b" else other, 1)
        until(one, None)
        until(other, None)
        layer.drain()
        for copy in saves:
            copy.wait()
        tell(2)

        layer = back(1, place.section, (o.fwd[0], o.fwd[2]), (s.returned, i.cotangent.at[1]))
        layer.fetch()
        layer.fetch_gu(s.gu_back)
        passes[2].arrive()
        hear(2)
        until(layer.steps(s.gu_back), "result")
        passes.append(courier(s.grad.at[1], o.passed, 3, 0))
        passes[3].start()
        saves = save_back(1)
        publish([s.result.at[0], s.result.at[1]], o.section, (0, 1), 0)
        publish([s.result.at[1], s.result.at[2]], o.section, (0, 1), 1)
        publish([s.grad.at[1]], o.grads, (0,), 0)
        publish([s.grad.at[0], s.grad.at[1]], o.grads, (0, 1), 1)
        layer.drain()
        arrival.drain()
        store_gains.wait()
        for copy in saves:
            copy.wait()
        passes[3].arrive()
        for taken in passes:
            taken.leave()

    outputs = dict(
        section=Out((2,) + own, BF16, True),
        grads=Out((2,) + own, BF16, True),
        passed=Out(own, BF16, True),
        weights={name: Out(shape, BF16, True) for name, shape in shapes.items()},
        gains=Out((1, entries), F32, True),
        fwd=[forward_kept(rows, width, units) for _ in range(steps)],
        back=[backward_kept(rows, width, units) for _ in range(steps - 1)],
    )
    scratch = dict(
        f=forward_scratch(rows, width, units),
        b=backward_scratch(rows, width, units),
        w={name: pltpu.VMEM(shape, BF16) for name, shape in shapes.items()},
        gains=pltpu.VMEM((1, entries), F32),
        gains_all=pltpu.VMEM((16,) + shards["gains"].shape, BF16),
        gu_back=pltpu.VMEM((2 * units, BLOCKS * rows), F32),
        result=pltpu.VMEM((steps,) + own, BF16),
        grad=pltpu.VMEM((steps - 1,) + own, BF16),
        received=pltpu.VMEM((steps - 1,) + own, BF16),
        returned=pltpu.VMEM(own, BF16),
        gains_sems=pair(15),
        keyval_sems=pair(30),
        query_sems=pair(30),
        out_sems=pair(30),
        ffn_send=pltpu.SemaphoreType.DMA((12,)),
        ffn_recv=pltpu.SemaphoreType.DMA((12,)),
        fetch=pltpu.SemaphoreType.DMA((6,)),
        store=pltpu.SemaphoreType.DMA((5,)),
        keep=pltpu.SemaphoreType.DMA((7,)),
        publish=pltpu.SemaphoreType.DMA((2,)),
        pass_send=pltpu.SemaphoreType.DMA((4,)),
        pass_recv=pltpu.SemaphoreType.DMA((4,)),
        steps=pltpu.SemaphoreType.REGULAR((3,)),
    )
    operands = near(inputs=inputs, cotangent=cotangent) | dict(tables=near(**tables), shards=far(**shards))
    return run(body, 0, operands, outputs, scratch)


GRAD_ROWS = ("a", "da", "ob", "dq", "dkv")


def last_layer(returned, grads, weights, gains, tables, past, kept):
    rows, width = returned.shape
    units = weights["ffn"].shape[1]
    tokens = BLOCKS * rows
    columns = width // 8
    entries = 2 * width + 2 * HEAD_SIZE
    last = len(kept[0]) - 1
    parts = dict(query=(columns, HALF_COLUMNS), keyval=(width // 16, 2 * KEY_COLUMNS), out=(HALF_COLUMNS, columns))
    lines = -(-entries // 1024) * 8

    def body(i, o, s):
        place = Place()
        core = place.bits[0]

        def on(section):
            return pl.when(place.section == section)

        r = Refs(
            s.b | {name: s.x[name].at[0, last] for name in ("a", "da", "dq", "dkv")} | i.tables,
            w=dict(s.w),
            gains=i.gains,
            grad=o.grads.at[last],
        )
        r["w"] = Refs(s.w)
        layer = BackwardLayer(
            r, place, last, lambda name: None, (i.past, None), (i.returned, None), ((384, 256), TOWARD_Z)
        )
        greet(place, NEIGHBOURS + (X_BIT | Y_BIT,))

        @on(0)
        def _():
            layer.rows_out()
            layer.fetch()
            load(i.grads.at[0], o.grads.at[0], s.turn.at[0])

        @on(1)
        def _():
            for m in range(2):
                load(i.grads.at[m], o.grads.at[m], s.turn.at[m])
            load(i.kept[1][1].df, r.df, r.held.at[0])
            load(i.kept[1][1].dgu, r.dgu, r.held.at[1])

        loads = {name: load(i.weights[name], s.w[name], s.fetch.at[n]) for n, name in enumerate(s.w)}

        def own_rows(start):
            for n, name in enumerate(GRAD_ROWS):
                for m in range(2):
                    for section in (0, 1):
                        if name in i.kept[section][m]:

                            @on(section)
                            def _():
                                source, target = i.kept[section][m][name], s.x[name].at[0, m]
                                if start:
                                    load(source, target, s.rows.at[2 * n + m])
                                else:
                                    landed(target, s.rows.at[2 * n + m])

        own_rows(True)
        for section in (0, 1):

            @on(section)
            def _():
                load(i.kept[section][0].gain, s.gain_kept, s.rows.at[10])
                if section == 1:
                    load(i.kept[1][1].gain, r.gain, s.rows.at[11])

        def exchange(name, m):
            n = 2 * GRAD_ROWS.index(name) + m
            buf = s.x[name]
            return remote(buf.at[0, m], buf.at[1, m], s.x_send.at[n], s.x_recv.at[n], place.peer(C_BIT))

        loads["ffn"].wait()

        def at(mask):
            return pl.ds(pl.multiple_of(place.ctx(mask) * columns, columns), columns)

        def units_at(mask):
            return pl.ds(pl.multiple_of((place.chip(mask) % 4) * units, units), units)

        def to_sibling(n, mask):
            where = s.w.ffn.at[:, :, at(mask | C_BIT)]
            return remote(where, s.sib_ffn.at[n], s.sib_send.at[n], s.sib_recv.at[n], place.peer(C_BIT))

        def to_owner(mask):
            n = mask // 2
            source, target = s.w.ffn.at[:, :, at(mask)], o.ffn.at[:, units_at(0), :]
            return remote(source, target, s.ffn_send.at[n], s.ffn_recv.at[n], place.peer(mask))

        def from_owner(mask):
            n = mask // 2
            where = o.ffn.at[:, units_at(mask), :]
            remote(where, where, s.ffn_send.at[n], s.ffn_recv.at[n], place.peer(mask)).wait_recv()

        def ffn_grads(e, hid, df_0, dgu_0):
            for section in (0, 1):

                @on(section)
                def _():
                    for m, kept_m in enumerate(i.kept[section]):
                        load(kept_m.e, e.at[m], s.wide.at[m])
                        load(kept_m.hid, hid.at[m], s.wide.at[2 + m])
                    load(i.kept[section][0].df, df_0, s.wide.at[4])
                    load(i.kept[section][0].dgu, dgu_0, s.wide.at[5])

            @on(1)
            def _():
                landed(r.df, r.held.at[0])
                landed(r.dgu, r.held.at[1])

            for m in range(2):
                landed(e.at[m], s.wide.at[m])
                landed(hid.at[m], s.wide.at[2 + m])
            landed(df_0, s.wide.at[4])
            landed(dgu_0, s.wide.at[5])

            def partial(mask):
                where = at(mask)
                up = jnp.zeros((2 * units, columns), F32)
                down = jnp.zeros((units, columns), F32)
                for m, (dgu, df) in enumerate(((dgu_0, df_0), (r.dgu, r.df))):
                    up = up + dot(dgu[...], e[m, :, :, where].reshape(tokens, columns))
                    down = down + dot(hid[m], df[:, :, where].reshape(tokens, columns))
                return up, down

            def store(mask, up, down):
                s.w.ffn[:2, :, at(mask)] = up.astype(BF16).reshape(2, units, columns)
                s.w.ffn[2, :, at(mask)] = down.astype(BF16)

            for n, mask in enumerate(AWAY + (0,)):
                store(mask | C_BIT, *partial(mask | C_BIT))
                to_sibling(n, mask).start()

            @on(0)
            def _():
                layer.scatter.second()

            for n, mask in enumerate(AWAY + (0,)):
                up, down = partial(mask)
                to_sibling(n, mask).wait_recv()
                up = up + s.sib_ffn[n, :2].astype(F32).reshape(2 * units, columns)
                store(mask, up, down + s.sib_ffn[n, 2].astype(F32))
                if n == 2:

                    @on(0)
                    def _():
                        layer.scatter.third()

            to_owner(X_BIT | Y_BIT).start()
            load(s.w.ffn.at[:, :, at(0)], o.ffn.at[:, units_at(0), :], s.fetch.at[4])

            @on(0)
            def _():
                layer.scatter.last()

        def front(part):
            r["part"] = part

            @on(0)
            def _():
                layer.scatter.part = part
                layer.feed_forward()

            pl.run_scoped(
                ffn_grads,
                pltpu.VMEM((2, BLOCKS, rows, width), BF16),
                pltpu.VMEM((2, units, tokens), BF16),
                pltpu.VMEM((BLOCKS, rows, width), BF16),
                pltpu.VMEM((2 * units, tokens), BF16),
            )

            @on(0)
            def _():
                layer.scatter.drain()

        pl.run_scoped(front, pltpu.VMEM((BLOCKS, rows, width), BF16))

        @on(0)
        def _():
            layer.middle()

        own_rows(False)

        def swap(names, ms):
            for name in names:
                for m in ms:
                    exchange(name, m).start()

        swap(("ob", "da", "a"), (0, 1))
        swap(("dq", "dkv"), (0,))

        def both(name, where):
            return s.x[name][:, :, :, where].reshape(4 * rows, where.size)

        def got(names, ms):
            for name in names:
                for m in ms:
                    exchange(name, m).wait_recv()

        def putter(ref):
            def put(index, total):
                ref[index] = total

            return put

        scatters = Refs()
        for name in parts:
            pieces = row_pieces((48, 48, 32), CYCLES) if name == "keyval" else halves(parts[name][0])
            scatters[name] = Scatter(place, s.part[name], s.land[name], pieces, s.sums[name], putter(o.attention[name]))

        def wide_columns(c):
            return pl.ds(pl.multiple_of((2 * c + core) * columns, columns), columns)

        def half(z):
            return pl.ds(z * HALF_COLUMNS, HALF_COLUMNS)

        got(("ob", "da"), (0, 1))
        for z in (0, 1):
            for c in range(4):
                s.part.out[4 * z + c] = dot_tn(both("ob", half(z)), both("da", wide_columns(c))).astype(BF16)
        scatters.out.start(pieces=(0,))

        def rest(w_keyval, w_query, do5, dq5):
            r.update(do5=do5, dq5=dq5)
            r.w.update(keyval=w_keyval, query=w_query)
            load(i.weights.keyval, w_keyval, s.fetch.at[3])
            load(i.weights.query, w_query, s.fetch.at[2])
            loads["out"].wait()

            @on(0)
            def _():
                layer.attention()

            scatters.out.start(pieces=(1,))
            landed(w_query, s.fetch.at[2])
            landed(w_keyval, s.fetch.at[3])

            @on(0)
            def _():
                layer.queries()

            swap(("dq",), (1,))
            got(("a", "dq"), (0, 1))
            for z in (0, 1):
                for c in range(4):
                    s.part.query[4 * z + c] = dot_tn(both("a", wide_columns(c)), both("dq", half(z))).astype(BF16)
            scatters.query.start()

            @on(0)
            def _():
                layer.key_sums()

            to_owner(X_BIT).start()
            to_owner(Y_BIT).start()

            @on(0)
            def _():
                layer.keys()

            swap(("dkv",), (1,))

        pl.run_scoped(
            rest,
            pltpu.VMEM(weights["keyval"].shape, BF16),
            pltpu.VMEM(weights["query"].shape, BF16),
            pltpu.VMEM((QUERY_HEADS * rows, HEAD_SIZE), BF16),
            pltpu.VMEM((QUERY_HEADS * rows, HEAD_SIZE), F32),
        )
        got(("dkv",), (0, 1))
        narrow = width // 16
        for z in (0, 1):
            for c in range(4):
                where = pl.ds(pl.multiple_of((8 * z + 2 * c + core) * narrow, narrow), narrow)
                every = pl.ds(0, 2 * KEY_COLUMNS)
                s.part.keyval[4 * z + c] = dot_tn(both("a", where), both("dkv", every)).astype(BF16)
        scatters.keyval.start()

        landed(s.gain_kept, s.rows.at[10])

        @on(1)
        def _():
            landed(r.gain, s.rows.at[11])

        total = s.gain_kept[...] + r.gain[...]
        lanes = entries // 128
        padding = jnp.zeros((lines - lanes, 128), F32)
        s.gain_all[place.block()] = jnp.concatenate(
            [total[:, n * 128 : (n + 1) * 128] for n in range(lanes)] + [padding], axis=0
        )
        gain_gather = Gather(place, s.gain_all, row_pieces((lines,), TOWARD_Z), s.gain_sems, True)
        gain_gather.start()
        scatters.out.second()
        gain_gather.first()
        gain_gather.second()
        scatters.query.second()
        scatters.out.third()
        scatters.keyval.second()
        scatters.query.third()
        scatters.out.last()
        scatters.keyval.third()
        gain_gather.third()
        scatters.query.last()
        scatters.keyval.last()
        gain_gather.last()
        total = s.gain_all[0]
        for n in range(1, 16):
            total = total + s.gain_all[n]
        o.gains[...] = total
        for mask in AWAY:
            from_owner(mask)
        for mask in AWAY:
            to_owner(mask).wait_send()
        landed(o.ffn.at[:, units_at(0), :], s.fetch.at[4])
        for n, mask in enumerate(AWAY + (0,)):
            to_sibling(n, mask).wait_send()
        for name in GRAD_ROWS:
            for m in range(2):
                exchange(name, m).wait_send()
        for scatter in scatters.values():
            scatter.drain()
        gain_gather.drain()
        landed(o.grads.at[0], s.turn.at[0])

        @on(0)
        def _():
            layer.gather.drain()
            layer.scatter_kv.drain()

        @on(1)
        def _():
            landed(o.grads.at[1], s.turn.at[1])

    outputs = dict(
        grads=Out((2, rows, width), BF16, False),
        attention={name: Out(shape, F32, False) for name, shape in parts.items()},
        ffn=Out((3, 4 * units, columns), BF16, True),
        gains=Out((lines, 128), F32, False),
    )
    b = backward_scratch(rows, width, units)
    row_widths = dict(zip(GRAD_ROWS, (width, width, QUERY_COLUMNS, QUERY_COLUMNS, 2 * KEY_COLUMNS)))
    for name in ("a", "da", "dq", "dkv", "do5", "dq5", "part"):
        del b[name]
    scratch = dict(
        b=b,
        w={name: pltpu.VMEM(weights[name].shape, BF16) for name in ("ffn", "out")},
        gain_kept=pltpu.VMEM((1, entries), F32),
        gain_all=pltpu.VMEM((16, lines, 128), F32),
        sib_ffn=pltpu.VMEM((4, 3, units, columns), BF16),
        x={name: pltpu.VMEM((2, 2, rows, size), BF16) for name, size in row_widths.items()},
        part={name: pltpu.VMEM((BLOCKS,) + shape, BF16) for name, shape in parts.items()},
        land={name: pltpu.VMEM((BLOCKS - 1,) + shape, BF16) for name, shape in parts.items()},
        sums={name: pair(21) for name in parts},
        gain_sems=pair(15),
        ffn_send=pltpu.SemaphoreType.DMA((4,)),
        ffn_recv=pltpu.SemaphoreType.DMA((4,)),
        sib_send=pltpu.SemaphoreType.DMA((4,)),
        sib_recv=pltpu.SemaphoreType.DMA((4,)),
        x_send=pltpu.SemaphoreType.DMA((10,)),
        x_recv=pltpu.SemaphoreType.DMA((10,)),
        fetch=pltpu.SemaphoreType.DMA((5,)),
        rows=pltpu.SemaphoreType.DMA((12,)),
        wide=pltpu.SemaphoreType.DMA((6,)),
        turn=pltpu.SemaphoreType.DMA((2,)),
    )
    operands = near(returned=returned, gains=gains) | far(grads=grads) | dict(tables=near(**tables))
    operands |= dict(weights=far(**weights), past=far(**{name: past[name] for name in BACK_NEEDS}))
    operands["kept"] = [[far(**{n: x for n, x in one.items() if n in GRAD_NEEDS}) for one in side] for side in kept]
    return run(body, 1, operands, outputs, scratch)


BACK_NEEDS = ("u", "h", "qraw", "kraw", "q", "kv", "gu")
GRAD_NEEDS = ("e", "hid", "df", "dgu", "gain") + GRAD_ROWS


def gradients_out(ffn):
    units, columns = ffn.shape[1:]
    steps = 4
    some = units // steps

    def body(source, gateup, down):
        for j in range(2):
            gateup[:, j, :] = jnp.transpose(source[j]).astype(F32)
        down[...] = source[2].astype(F32)

    return pl.pallas_call(
        body,
        grid=(steps,),
        in_specs=[pl.BlockSpec((3, some, columns), lambda i: (0, i, 0))],
        out_specs=(
            pl.BlockSpec((columns, 2, some), lambda i: (0, 0, i)),
            pl.BlockSpec((some, columns), lambda i: (i, 0)),
        ),
        out_shape=(
            jax.ShapeDtypeStruct((columns, 2, units), F32),
            jax.ShapeDtypeStruct((units, columns), F32),
        ),
        compiler_params=pltpu.CompilerParams(vmem_limit_bytes=VMEM_BYTES),
    )(ffn)


def cube_device(
    inputs,
    cotangent,
    slot_order,
    query_weight,
    key_value_matrix,
    out_weight,
    gateup_weight,
    down_weight,
    norm_gains,
):
    tensor_id = lax.axis_index("tensor")
    context_id = lax.axis_index("ctx")
    batches, rows, width = inputs.shape
    tensors, contexts = 2, 8
    span = rows * tensors
    share = norm_gains.shape[1]
    shards = dict(
        query=query_weight[0],
        keyval=key_value_matrix[0],
        out=out_weight[0],
        gateup=jnp.transpose(gateup_weight[0], (1, 2, 0)),
        down=down_weight[0],
        gains=jnp.pad(norm_gains, ((0, 15), (0, -share % 128))),
    )
    own_slot = jnp.sum(jnp.where(jnp.arange(contexts) == context_id, slot_order, 0), axis=1)
    own_pos = own_slot[:, None] * span + tensor_id * rows + jnp.arange(rows)[None, :]
    half_width = HEAD_SIZE // 2
    frequency = ROPE_BASE ** (-(jnp.arange(half_width, dtype=F32) * 2.0) / HEAD_SIZE)
    angles = own_pos.astype(F32)[..., None] * frequency
    cosine, sine = jnp.cos(angles), jnp.sin(angles)
    rowtab = jnp.concatenate(
        [cosine, cosine, -sine, sine, jnp.broadcast_to(own_pos.astype(F32)[..., None], (batches, rows, 128))], axis=-1
    )
    within = jnp.arange(tensors)[:, None, None] * rows + jnp.arange(rows)[None, None, :]
    key_pos = (slot_order[:, None, :, None] * span + within[None]).reshape(batches, 1, -1)
    tables = dict(rowtab=rowtab, postab=key_pos.astype(F32))
    layers = most_layers(inputs, cotangent, shards, tables)
    fwd, back = layers["fwd"], layers["back"]
    kept = [[fwd[0] | back[1], fwd[1]], [fwd[1] | back[0], fwd[2] | back[1]]]
    last = last_layer(layers["passed"], layers["grads"], layers["weights"], layers["gains"], tables, fwd[1], kept)
    start = (tensor_id * contexts + context_id) * share
    attention = last["attention"]
    grad_gateup, grad_down = gradients_out(last["ffn"])
    return (
        layers["section"][None],
        last["grads"][None],
        attention["query"][None],
        attention["keyval"][None],
        attention["out"][None],
        grad_gateup[None],
        grad_down[None],
        lax.dynamic_slice(last["gains"].reshape(-1), (start,), (share,))[None],
    )


def fits_cube(mesh):
    return mesh.shape["section"] == 2 and mesh.shape["tensor"] == 2 and mesh.shape["ctx"] == 8


def solution(mesh):
    return jax.shard_map(
        cube_device if fits_cube(mesh) else per_device,
        mesh=mesh,
        in_specs=(
            P(None, ("tensor", "ctx"), None),
            P(None, ("tensor", "ctx"), None),
            P(),
            P("section", "ctx", "tensor"),
            P("section", ("tensor", "ctx"), None),
            P("section", "tensor", "ctx"),
            P("section", "ctx", None, "tensor"),
            P("section", "tensor", "ctx"),
            P("section", ("tensor", "ctx")),
        ),
        out_specs=(
            P("section", None, ("tensor", "ctx"), None),
            P("section", None, ("tensor", "ctx"), None),
            P("section", "ctx", "tensor"),
            P("section", ("tensor", "ctx"), None),
            P("section", "tensor", "ctx"),
            P("section", "ctx", None, "tensor"),
            P("section", "tensor", "ctx"),
            P("section", ("tensor", "ctx")),
        ),
        check_vma=False,
    )
```
